32 devices in a mesh: ax: 16 (over z, x, core), az: 2 (over y).
Axes of the slice: x: 2, y: 2, z: 4, core: 2. Of those that a mesh axis runs over, the one named last changes fastest.
Arguments:
- initial: float32 [19, 32, 32, 256], P(None, 'ax', 'az'), as said below
- adjoint_seed: float32 [19, 32, 32, 256], P(None, 'ax', 'az'), may hold values from -6 to 6
- porosity: float32 [32, 32, 256], P('ax', 'az'), may hold values from 0.05 to 0.6
- cell_type: int32 [32, 32, 256], P('ax', 'az'), may hold values from 0 to 3
- region: int32 [32, 32, 256], P('ax', 'az'), may hold values from 0 to 8, as said below
Outputs:
- final_state: float32 [19, 32, 32, 256], P(None, 'ax', 'az')
- adjoint_state: float32 [19, 32, 32, 256], P(None, 'ax', 'az')
- sensitivity: float32 [32, 32, 256], P('ax', 'az')
- region_totals: float32 [8], replicated
The draws below stay inside these ranges and needn't reach their ends.
Inputs may be any that keep to these rules, and one draw needn't show every extreme that they name: `cell_type`: the cells of radial index 0 and 255 are walls. All design cells of one aligned block of 2 x 16 x 256 cells share one region; each region holds four such blocks. `initial`: populations are positive.
All inputs are finite; a program needn't handle non-finite values.
Results may differ from the reference program's by a relative error of at most 0.0003.
Values sent between devices are 32-bit elements; how exact they have to be, the bound alone decides.
No kernel may reach another device: no remote copies, remote signals or barrier semaphores. Data moves between devices by JAX's collectives and lax.ppermute only.
A program may use at most 64 MiB of HBM per device.

```python
import jax
import jax.numpy as jnp
from jax import lax

CA = 2
CT = 16
NR = 256
NA = 32
NT = 32
NREG = 8


VELOCITY = [(0, 0, 0), (1, 0, 0), (-1, 0, 0), (0, 1, 0), (0, -1, 0), (0, 0, 1), (0, 0, -1), (1, 1, 0), (-1, -1, 0), (1, -1, 0), (-1, 1, 0), (1, 0, 1), (-1, 0, -1), (1, 0, -1), (-1, 0, 1), (0, 1, 1), (0, -1, -1), (0, 1, -1), (0, -1, 1)]


WEIGHTS = [1.0 / 3.0] + [1.0 / 18.0] * 6 + [1.0 / 36.0] * 12


def draw_initial(key, part):
    keys = jax.random.split(jax.random.fold_in(key, 11), 3)
    cells = (NA, NT, NR)
    density = 1.0 + 0.05 * jnp.clip(jax.random.normal(keys[0], cells, jnp.float32), -3.0, 3.0)
    velocity = jnp.clip(0.04 * jax.random.normal(keys[1], (3,) + cells, jnp.float32), -0.1, 0.1)
    noise = jnp.clip(jax.random.normal(keys[2], (19,) + cells, jnp.float32), -3.0, 3.0)
    speed_sq = velocity[0] * velocity[0] + velocity[1] * velocity[1] + velocity[2] * velocity[2]
    result = []
    for index_q in range(19):
        direc = VELOCITY[index_q]
        projected = direc[0] * velocity[0] + direc[1] * velocity[1] + direc[2] * velocity[2]
        balance = WEIGHTS[index_q] * density * (1.0 + 3.0 * projected + 4.5 * projected * projected - 1.5 * speed_sq)
        result.append(balance + 0.1 * WEIGHTS[index_q] * density * noise[index_q])
    return jnp.stack(result).astype(jnp.float32)


def draw_cell_type(key, part):
    rolls = jax.random.randint(jax.random.fold_in(key, 23), (NA, NT, NR), 0, 100)
    types = jnp.where(rolls < 10, 1, jnp.where(rolls < 13, 2, jnp.where(rolls < 16, 3, 0)))
    radial = jnp.arange(NR)[None, None, :]
    types = jnp.where((radial == 0) | (radial == NR - 1), 1, types)
    return types.astype(jnp.int32)


def draw_region(key, part):
    blocks_a = NA // CA
    blocks_t = NT // CT
    order = jax.random.permutation(jax.random.fold_in(key, 31), blocks_a * blocks_t)
    labels = (1 + order % NREG).reshape(blocks_a, blocks_t)
    labels = jnp.repeat(jnp.repeat(labels, CA, axis=0), CT, axis=1)
    chosen = jax.random.randint(jax.random.fold_in(key, 37), (NA, NT, NR), 0, 2)
    return (labels[:, :, None] * chosen).astype(jnp.int32)


def shard_levels(rng, dims, pieces, least, top_value):
    factor_of, own = 1.0, jax.random.fold_in(rng, 6)
    for position, blocks in pieces:
        steps = jnp.exp(jax.random.uniform(jax.random.fold_in(own, position), (blocks,), jnp.float32, least / len(pieces), top_value / len(pieces)))
        factor_of = factor_of * jnp.repeat(steps, dims[position] // blocks).reshape([-1 if axis == position else 1 for axis in range(len(dims))])
    return factor_of


def gaussian(rng, dims, width, most, cuts=(), dtype=jnp.bfloat16):
    drawn = jax.random.normal(rng, dims, jnp.float32) * width
    if len(cuts) > 0:
        drawn = shard_levels(rng, dims, cuts, -0.22, 0.18) * drawn
    return jnp.clip(drawn, min=-most, max=most).astype(dtype)


def setup_inputs(seed: int = 0) -> dict:
    seeds = jax.random.split(jax.random.key(seed), 6)
    initial = draw_initial(jax.random.fold_in(seeds[5], 71), 0)
    adjoint_seed = gaussian(seeds[1], (19, NA, NT, NR), 1.0, 6.0, ((1, 16), (2, 2)), jnp.float32)
    porosity = jnp.clip(0.05 + 0.55 * jax.random.uniform(seeds[2], (NA, NT, NR), jnp.float32) ** shard_levels(seeds[2], (NA, NT, NR), ((0, 16), (1, 2)), -0.2, 0.2), 0.05, 0.6)
    cell_type = draw_cell_type(jax.random.fold_in(seeds[5], 71), 0)
    region = draw_region(jax.random.fold_in(seeds[5], 71), 0)
    return dict(initial=initial, adjoint_seed=adjoint_seed, porosity=porosity, cell_type=cell_type, region=region)


VELOCITY = [(0, 0, 0), (1, 0, 0), (-1, 0, 0), (0, 1, 0), (0, -1, 0), (0, 0, 1), (0, 0, -1), (1, 1, 0), (-1, -1, 0), (1, -1, 0), (-1, 1, 0), (1, 0, 1), (-1, 0, -1), (1, 0, -1), (-1, 0, 1), (0, 1, 1), (0, -1, -1), (0, 1, -1), (0, -1, 1)]
OPPOSITE = [0, 2, 1, 4, 3, 6, 5, 8, 7, 10, 9, 12, 11, 14, 13, 16, 15, 18, 17]
WEIGHTS = [1.0 / 3.0] + [1.0 / 18.0] * 6 + [1.0 / 36.0] * 12
INLET_SPEED = (0.05, 0.05, 0.0)
HIGH = lax.Precision.HIGHEST

def equilibrium(density, velocity):
    table = jnp.array(VELOCITY, jnp.float32)
    weights = jnp.array(WEIGHTS, jnp.float32).reshape((19,) + (1,) * density.ndim)
    projected = jnp.einsum('qk,k...->q...', table, velocity, precision=HIGH)
    speed_sq = lax.optimization_barrier(jnp.sum(velocity * velocity, axis=0))
    return weights * density * (1.0 + 3.0 * projected + 4.5 * projected * projected - 1.5 * speed_sq)

def collide(pops, porous, types, regions):
    table = jnp.array(VELOCITY, jnp.float32)
    weights = jnp.array(WEIGHTS, jnp.float32).reshape((19,) + (1,) * (pops.ndim - 1))
    density = lax.optimization_barrier(jnp.sum(pops, axis=0))
    momentum = jnp.einsum('qk,q...->k...', table, pops, precision=HIGH)
    velocity = momentum / density
    balance = equilibrium(density, velocity)
    departure = pops - balance
    moments = []
    for first_k, second_k in ((0, 0), (1, 1), (2, 2), (0, 1), (0, 2), (1, 2)):
        factors = table[:, first_k] * table[:, second_k]
        moments.append(jnp.einsum('q,q...->...', factors, departure, precision=HIGH))
    stress_sq = moments[0] ** 2 + moments[1] ** 2 + moments[2] ** 2 + 2.0 * (moments[3] ** 2 + moments[4] ** 2 + moments[5] ** 2)
    shear = 1.5 * jnp.sqrt(stress_sq + 0.0001) / density
    viscous = 0.02 * (shear + 0.01) ** (0.7 - 1.0)
    relax = 0.5 + 3.0 * viscous
    design = (regions > 0).astype(jnp.float32)
    relaxed = pops - departure / relax - porous * design * (balance - weights * density)
    unity = jnp.ones_like(density)
    inlet_vel = jnp.array(INLET_SPEED, jnp.float32).reshape((3,) + (1,) * density.ndim) * unity
    inflow = equilibrium(unity, inlet_vel)
    outflow = equilibrium(unity, velocity)
    return jnp.where(types == 2, inflow, jnp.where(types == 3, outflow, relaxed))

def displaced(field, shift_a, shift_t, shift_r):
    rolled = jnp.roll(field, -shift_t, axis=1)
    padded = jnp.pad(rolled, ((1, 1), (0, 0), (1, 1)))
    rows_a, rows_r = (field.shape[0], field.shape[2])
    return padded[1 + shift_a:1 + shift_a + rows_a, :, 1 + shift_r:1 + shift_r + rows_r]

def stream(post, flags):
    result = []
    for index_q in range(19):
        direc = VELOCITY[index_q]
        source_ok = displaced(flags, -direc[0], -direc[1], -direc[2]) > 0
        moved = displaced(post[index_q], -direc[0], -direc[1], -direc[2])
        result.append(jnp.where(source_ok, moved, post[OPPOSITE[index_q]]))
    return jnp.stack(result)

def stream_adjoint(adjoint, flags):
    result = []
    for index_q in range(19):
        direc = VELOCITY[index_q]
        ahead = displaced(adjoint[index_q], direc[0], direc[1], direc[2])
        blocked = 1.0 - displaced(flags, direc[0], direc[1], direc[2])
        result.append(flags * ahead + blocked * adjoint[OPPOSITE[index_q]])
    return jnp.stack(result)

def collide_all(pops, porous, types, regions):

    def one_row(entries):
        return collide(entries[0], entries[1], entries[2], entries[3])
    mapped = lax.map(one_row, (jnp.moveaxis(pops, 1, 0), porous, types, regions))
    return jnp.moveaxis(mapped, 0, 1)

def adjoint_all(upstream, pops, porous, types, regions):

    def one_row(entries):
        row_types, row_regions = (entries[3], entries[4])
        primal, pullback = jax.vjp(lambda current, coefficient: collide(current, coefficient, row_types, row_regions), entries[1], entries[2])
        return pullback(entries[0])
    back_pops, back_porous = lax.map(one_row, (jnp.moveaxis(upstream, 1, 0), jnp.moveaxis(pops, 1, 0), porous, types, regions))
    return (jnp.moveaxis(back_pops, 0, 1), back_porous)

def reference(initial, adjoint_seed, porosity, cell_type, region):
    flags = (cell_type != 1).astype(jnp.float32)
    state_one = stream(collide_all(initial, porosity, cell_type, region), flags)
    final_state = stream(collide_all(state_one, porosity, cell_type, region), flags)
    adjoint = adjoint_seed
    sensitivity = jnp.zeros(porosity.shape, jnp.float32)
    for recorded in (state_one, initial):
        upstream = stream_adjoint(adjoint, flags)
        adjoint, partial_sens = adjoint_all(upstream, recorded, porosity, cell_type, region)
        sensitivity = sensitivity + partial_sens
    totals = jax.ops.segment_sum(sensitivity.reshape(-1), region.reshape(-1), num_segments=NREG + 1)[1:]
    return (final_state, adjoint, sensitivity, totals)
```

```python
import functools

import jax
import jax.numpy as jnp
import numpy as np
from jax import lax
from jax.experimental import pallas as pl
from jax.experimental.pallas import tpu as pltpu
from jax.sharding import PartitionSpec as P

VELOCITY = [
    (0, 0, 0),
    (1, 0, 0),
    (-1, 0, 0),
    (0, 1, 0),
    (0, -1, 0),
    (0, 0, 1),
    (0, 0, -1),
    (1, 1, 0),
    (-1, -1, 0),
    (1, -1, 0),
    (-1, 1, 0),
    (1, 0, 1),
    (-1, 0, -1),
    (1, 0, -1),
    (-1, 0, 1),
    (0, 1, 1),
    (0, -1, -1),
    (0, 1, -1),
    (0, -1, 1),
]
OPPOSITE = [0, 2, 1, 4, 3, 6, 5, 8, 7, 10, 9, 12, 11, 14, 13, 16, 15, 18, 17]
INLET_SPEED = (0.05, 0.05, 0.0)
W_AXIS = 1.0 / 18.0
W_EDGE = 1.0 / 36.0


def moving(axis, sign):
    return [q for q in range(19) if VELOCITY[q][axis] == sign]


LO, HI = 0, 1
POST, ADJ, FLAG = 0, 1, 2


def face_fields(axis, side):
    sign = -1 if side == LO else 1
    fields = [(POST, q) for q in moving(axis, sign)] + [(ADJ, q) for q in moving(axis, -sign)]
    return fields + [(FLAG, 0)]


AX_SLOT = [{key: i for i, key in enumerate(face_fields(0, side))} for side in (LO, HI)]


def azimuthal_rows():
    place, corner, rest = {}, [[], []], []
    for a, sign, block in ((1, 1, 0), (0, -1, 1)):
        for side in (LO, HI):
            for kind, q in face_fields(1, side):
                leaves = VELOCITY[q][0] == (sign if kind == POST else -sign)
                if kind == FLAG or leaves:
                    corner[block].append((side, kind, q, a))
                else:
                    rest.append((side, kind, q, a))
    for block in (0, 1):
        for i, key in enumerate(corner[block]):
            place[key] = (block, i)
    for i, key in enumerate(rest):
        place[key] = (2 + i // 8, i % 8)
    return place, 2 + (len(rest) + 7) // 8


AZ_PLACE, AZ_BLOCKS = azimuthal_rows()


def pairs_of(values):
    sums = [values[q] + values[q + 1] for q in range(1, 19, 2)]
    diffs = [values[q] - values[q + 1] for q in range(1, 19, 2)]
    return sums, diffs


def projections(vec):
    va, vt, vr = vec
    return [va, vt, vr, va + vt, va - vt, va + vr, va - vr, vt + vr, vt - vr]


def linearise(pops, porous, types, regions):
    sums, diffs = pairs_of(pops)
    s0, s1, s2, s3, s4, s5, s6, s7, s8 = sums
    d0, d1, d2, d3, d4, d5, d6, d7, d8 = diffs
    at, ar, tr = s3 + s4, s5 + s6, s7 + s8
    rho = pops[0] + ((s0 + s1) + (s2 + at)) + (ar + tr)
    ma = (d0 + (d3 + d4)) + (d5 + d6)
    mt = (d1 + (d3 - d4)) + (d7 + d8)
    mr = (d2 + (d5 - d6)) + (d7 - d8)
    inv = 1.0 / rho
    ua, ut, ur = ma * inv, mt * inv, mr * inv
    third = rho * (1.0 / 3.0)
    paa = (s0 + at + ar - third) - ma * ua
    ptt = (s1 + at + tr - third) - mt * ut
    prr = (s2 + ar + tr - third) - mr * ur
    pat = (s3 - s4) - ma * ut
    par = (s5 - s6) - ma * ur
    ptr = (s7 - s8) - mt * ur
    square = (paa * paa + ptt * ptt + prr * prr) + 2.0 * (pat * pat + par * par + ptr * ptr) + 0.0001
    inv_root = lax.rsqrt(square)
    shear = 1.5 * (square * inv_root) * inv
    shifted = shear + 0.01
    viscous = 0.02 * jnp.exp((0.7 - 1.0) * jnp.log(shifted))
    omega = 1.0 / (0.5 + 3.0 * viscous)
    relaxed = (types != 2) & (types != 3)
    kappa = jnp.where(regions > 0, porous, 0.0)
    return dict(
        rho=rho,
        inv=inv,
        u=(ua, ut, ur),
        p=(paa, ptt, prr, pat, par, ptr),
        inv_root=inv_root,
        shear=shear,
        shifted=shifted,
        viscous=viscous,
        omega=omega,
        relaxed=relaxed,
        kappa=kappa,
        keep=jnp.where(relaxed, 1.0 - omega, 0.0),
        design=jnp.where(relaxed & (regions > 0), 1.0, 0.0),
        inlet=types == 2,
        outlet=types == 3,
    )


def collide(pops, lin):
    rho, relaxed, inlet = lin["rho"], lin["relaxed"], lin["inlet"]
    ua, ut, ur = (jnp.where(inlet, speed, x) for x, speed in zip(lin["u"], INLET_SPEED))
    scale = jnp.where(relaxed, (lin["omega"] - lin["kappa"]) * rho, 1.0)
    rest = jnp.where(relaxed, lin["kappa"] * rho, 0.0)
    keep = lin["keep"]
    still = 1.0 - 1.5 * (ua * ua + ut * ut + ur * ur)
    post = [keep * pops[0] + (1.0 / 3.0) * (scale * still + rest)]
    for i, cu in enumerate(projections((ua, ut, ur))):
        weight = W_AXIS if i < 3 else W_EDGE
        even = weight * (scale * (still + 4.5 * cu * cu) + rest)
        odd = (3.0 * weight) * (scale * cu)
        post.append(keep * pops[1 + 2 * i] + (even + odd))
        post.append(keep * pops[2 + 2 * i] + (even - odd))
    return post


def pull_back(back, pops, lin):
    sums, diffs = pairs_of(back)
    s0, s1, s2, s3, s4, s5, s6, s7, s8 = sums
    d0, d1, d2, d3, d4, d5, d6, d7, d8 = diffs
    at, ar, tr = s3 + s4, s5 + s6, s7 + s8
    b0 = (1.0 / 3.0) * back[0] + W_AXIS * (s0 + s1 + s2) + W_EDGE * (at + ar + tr)
    ba = W_AXIS * d0 + W_EDGE * ((d3 + d4) + (d5 + d6))
    bt = W_AXIS * d1 + W_EDGE * ((d3 - d4) + (d7 + d8))
    br = W_AXIS * d2 + W_EDGE * ((d5 - d6) + (d7 - d8))
    baa = W_AXIS * s0 + W_EDGE * (at + ar)
    btt = W_AXIS * s1 + W_EDGE * (at + tr)
    brr = W_AXIS * s2 + W_EDGE * (ar + tr)
    bat, bar, btr = W_EDGE * (s3 - s4), W_EDGE * (s5 - s6), W_EDGE * (s7 - s8)
    along = back[0] * pops[0]
    for q in range(1, 19):
        along = along + back[q] * pops[q]
    rho, inv = lin["rho"], lin["inv"]
    ua, ut, ur = lin["u"]
    qa = baa * ua + bat * ut + bar * ur
    qt = bat * ua + btt * ut + btr * ur
    qr = bar * ua + btr * ut + brr * ur
    uu = ua * ua + ut * ut + ur * ur
    slope = 3.0 * (ua * ba + ut * bt + ur * br) + 4.5 * (ua * qa + ut * qt + ur * qr) - 1.5 * (uu * b0)
    full = b0 + slope
    sens = -(lin["design"] * (rho * slope))
    relaxed, omega = lin["relaxed"], lin["omega"]
    shear_bar = (rho * full - along) * (omega * omega) * (0.9 * lin["viscous"]) / lin["shifted"]
    shear_bar = jnp.where(relaxed, shear_bar, 0.0)
    z = shear_bar * (1.5 * inv) * lin["inv_root"]
    maa, mtt, mrr, mat, mar, mtr = (z * x for x in lin["p"])
    scale = jnp.where(relaxed, omega - lin["kappa"], jnp.where(lin["outlet"], inv, 0.0))
    la = maa * ua + mat * ut + mar * ur
    lt = mat * ua + mtt * ut + mtr * ur
    lr = mar * ua + mtr * ut + mrr * ur
    va = scale * (3.0 * (ba - b0 * ua) + 9.0 * qa) - 2.0 * la
    vt = scale * (3.0 * (bt - b0 * ut) + 9.0 * qt) - 2.0 * lt
    vr = scale * (3.0 * (br - b0 * ur) + 9.0 * qr) - 2.0 * lr
    total = jnp.where(relaxed, lin["kappa"] * b0 + scale * full, 0.0)
    total = total - shear_bar * lin["shear"] * inv - (1.0 / 3.0) * (maa + mtt + mrr)
    total = total - ((la + va) * ua + (lt + vt) * ut + (lr + vr) * ur)
    keep = lin["keep"]
    taa, ttt, trr = total + maa, total + mtt, total + mrr
    sat, sar, str_ = taa + mtt, taa + mrr, ttt + mrr
    mat2, mar2, mtr2 = 2.0 * mat, 2.0 * mar, 2.0 * mtr
    evens = [taa, ttt, trr, sat + mat2, sat - mat2, sar + mar2, sar - mar2, str_ + mtr2, str_ - mtr2]
    result = [keep * back[0] + total]
    for i, odd in enumerate(projections((va, vt, vr))):
        result.append(keep * back[1 + 2 * i] + (evens[i] + odd))
        result.append(keep * back[2 + 2 * i] + (evens[i] - odd))
    return result, sens


class Fields:
    def __init__(self, own, halo):
        self.own = own
        self.halo = halo
        up_e = halo["parity"] == 0
        self.up_e = up_e

    def row(self, kind, q, a):
        rows_a = self.own[POST].shape[1]
        if 0 <= a < rows_a:
            return self.own[FLAG][a] if kind == FLAG else self.own[kind][q, a]
        e, o = self.halo["e"], self.halo["o"]
        if a < 0:
            slot = AX_SLOT[HI][(kind, q)]
            return jnp.where(self.up_e, o[slot], e[slot])
        slot = AX_SLOT[LO][(kind, q)]
        return jnp.where(self.up_e, e[slot], o[slot])

    def edge(self, side, kind, q, a):
        rows_a = self.own[POST].shape[1]
        if 0 <= a < rows_a:
            block, i = AZ_PLACE[(side, kind, q, a)]
            return self.halo["t"][block, i : i + 1, :]
        ec, oc = self.halo["ec"], self.halo["oc"]
        if a < 0:
            block, i = AZ_PLACE[(side, kind, q, 1)]
            return jnp.where(self.up_e, oc[block, i : i + 1, :], ec[block, i : i + 1, :])
        block, i = AZ_PLACE[(side, kind, q, 0)]
        return jnp.where(self.up_e, ec[block, i : i + 1, :], oc[block, i : i + 1, :])

    def moved(self, kind, q, a, shift):
        sa, st, sr = shift
        value = self.row(kind, q, a + sa)
        rows_t, rows_r = value.shape
        if st:
            value = pltpu.roll(value, (-st) % rows_t, 0)
            beyond = self.edge(LO if st > 0 else HI, kind, q, a + sa)
            at_edge = lax.broadcasted_iota(jnp.int32, value.shape, 0) == (rows_t - 1 if st > 0 else 0)
            value = jnp.where(at_edge, beyond, value)
        if sr:
            value = pltpu.roll(value, (-sr) % rows_r, 1)
        return value


def pack(own, parity, e_ref, o_ref, t_ref):
    rows_a, rows_t = own[POST].shape[1], own[POST].shape[2]
    with_flags = FLAG in own
    even = parity == 0

    def cells(kind, q, a):
        return own[FLAG][a] if kind == FLAG else own[kind][q, a]

    for slot in range(len(AX_SLOT[LO])):
        low = [key for key, i in AX_SLOT[LO].items() if i == slot][0]
        high = [key for key, i in AX_SLOT[HI].items() if i == slot][0]
        if low[0] == FLAG and not with_flags:
            continue
        low, high = cells(*low, 0), cells(*high, rows_a - 1)
        e_ref[slot] = jnp.where(even, high, low)
        o_ref[slot] = jnp.where(even, low, high)
    for (side, kind, q, a), (block, i) in AZ_PLACE.items():
        if kind == FLAG and not with_flags:
            continue
        t = 0 if side == LO else rows_t - 1
        source = own[FLAG].at[a] if kind == FLAG else own[kind].at[q, a]
        t_ref[block, i : i + 1, :] = source[t : t + 1, :]


def chunks(shape, body):
    rows_a, rows_t, rows_r = shape
    counts = (rows_a, rows_t // 8, rows_r // 128)

    def step(i, carry):
        a = i // (counts[1] * counts[2])
        t = pl.multiple_of((i // counts[2]) % counts[1] * 8, 8)
        r = pl.multiple_of(i % counts[2] * 128, 128)
        body((a, pl.ds(t, 8), pl.ds(r, 128)))
        return carry

    lax.fori_loop(0, counts[0] * counts[1] * counts[2], step, 0)


def load(ref, where):
    return [ref[(q,) + where] for q in range(19)]


def store(ref, where, values):
    for q in range(19):
        ref[(q,) + where] = values[q]


def first_kernel(parity_ref, pops, seed, porous, types, regions, post, e_out, o_out, t_out, flags):
    def body(where):
        values = load(pops, where)
        lin = linearise(values, porous[where], types[where], regions[where])
        store(post, where, collide(values, lin))

    chunks(porous.shape, body)
    flags[...] = jnp.where(types[...] != 1, 1.0, 0.0)
    pack({POST: post, ADJ: seed, FLAG: flags}, parity_ref[0], e_out, o_out, t_out)


def second_kernel(
    parity_ref, post, seed, flags, porous, types, regions, e, o, t, ec, oc,
    post_next, adj, sens, around, e_out, o_out, t_out, state, back,
):
    halo = dict(parity=parity_ref[0], e=e, o=o, t=t, ec=ec, oc=oc)
    fields = Fields({POST: post, ADJ: seed, FLAG: flags}, halo)
    rows_a = porous.shape[0]
    for a in range(rows_a):
        centre = flags[a]
        state[0, a] = post[0, a]
        back[0, a] = seed[0, a]
        for q in range(1, 19):
            direc = VELOCITY[q]
            behind = tuple(-c for c in direc)
            open_ = fields.moved(FLAG, 0, a, behind)
            around[q - 1, a] = open_
            opp = OPPOSITE[q]
            state[q, a] = jnp.where(open_ > 0, fields.moved(POST, q, a, behind), post[opp, a])
            back[opp, a] = centre * fields.moved(ADJ, opp, a, behind) + (1.0 - open_) * seed[q, a]

    def body(where):
        values = load(state, where)
        lin = linearise(values, porous[where], types[where], regions[where])
        store(post_next, where, collide(values, lin))
        result, partial_sens = pull_back(load(back, where), values, lin)
        store(adj, where, result)
        sens[where] = partial_sens

    chunks(porous.shape, body)
    pack({POST: post_next, ADJ: adj}, parity_ref[0], e_out, o_out, t_out)


def third_kernel(
    parity_ref, post, adj, flags, around, pops, porous, types, regions, sens_one, e, o, t, ec, oc,
    final, result, sens, totals, back, acc,
):
    halo = dict(parity=parity_ref[0], e=e, o=o, t=t, ec=ec, oc=oc)
    fields = Fields({POST: post, ADJ: adj, FLAG: flags}, halo)
    rows_a = porous.shape[0]
    for a in range(rows_a):
        centre = flags[a]
        final[0, a] = post[0, a]
        back[0, a] = adj[0, a]
        for q in range(1, 19):
            behind = tuple(-c for c in VELOCITY[q])
            open_ = around[q - 1, a]
            opp = OPPOSITE[q]
            final[q, a] = jnp.where(open_ > 0, fields.moved(POST, q, a, behind), post[opp, a])
            back[opp, a] = centre * fields.moved(ADJ, opp, a, behind) + (1.0 - open_) * adj[q, a]
    acc[...] = jnp.zeros_like(acc)

    def body(where):
        values = load(pops, where)
        lin = linearise(values, porous[where], types[where], regions[where])
        adjoint, partial_sens = pull_back(load(back, where), values, lin)
        store(result, where, adjoint)
        both = partial_sens + sens_one[where]
        sens[where] = both
        acc[...] += jnp.where(regions[where] > 0, both, 0.0)

    chunks(porous.shape, body)
    label = jnp.max(regions[...], axis=(0, 1, 2), keepdims=True)[0]
    total = jnp.sum(acc[...], axis=(0, 1), keepdims=True)
    lanes = lax.broadcasted_iota(jnp.int32, totals.shape, 1) + 1
    totals[...] = jnp.where(lanes == label, total, 0.0)


def call(body, out_shapes, scratch, parity, *arrays):
    return pl.pallas_call(
        body,
        out_shape=[jax.ShapeDtypeStruct(s, jnp.float32) for s in out_shapes],
        in_specs=[pl.BlockSpec(memory_space=pltpu.SMEM)]
        + [pl.BlockSpec(memory_space=pltpu.VMEM)] * len(arrays),
        out_specs=[pl.BlockSpec(memory_space=pltpu.VMEM)] * len(out_shapes),
        scratch_shapes=[pltpu.VMEM(s, jnp.float32) for s in scratch],
        compiler_params=pltpu.CompilerParams(vmem_limit_bytes=40 * 1024 * 1024),
    )(parity, *arrays)


def even_pairs(size):
    return [(i, i ^ 1) for i in range(size) if i ^ 1 < size]


def odd_pairs(size):
    return [(i, ((i + 1) ^ 1) - 1) for i in range(size) if 0 <= ((i + 1) ^ 1) - 1 < size]


def exchange(e_msg, o_msg, t_msg):
    size_a, size_t = lax.axis_size("ax"), lax.axis_size("az")
    ring = [(i, (i + 1) % size_t) for i in range(size_t)]
    t = lax.ppermute(t_msg, "az", ring)
    if size_t > 2:
        from_high = np.zeros((AZ_BLOCKS, 8, 1), bool)
        for (side, _, _, _), (block, i) in AZ_PLACE.items():
            from_high[block, i] = side == HI
        t_down = lax.ppermute(t_msg, "az", [(j, i) for i, j in ring])
        t = jnp.where(jnp.asarray(from_high), t, t_down)
    e = lax.ppermute(e_msg, "ax", even_pairs(size_a))
    o = lax.ppermute(o_msg, "ax", odd_pairs(size_a))
    corners = t[:2]
    ec = lax.ppermute(corners, "ax", even_pairs(size_a))
    oc = lax.ppermute(corners, "ax", odd_pairs(size_a))
    return e, o, t, ec, oc


def sum_all(x):
    for axis in ("az", "ax"):
        size = lax.axis_size(axis)
        if size & (size - 1):
            x = lax.psum(x, axis)
            continue
        step = 1
        while step < size:
            x = x + lax.ppermute(x, axis, [(i, i ^ step) for i in range(size)])
            step *= 2
    return x


def shards(initial, adjoint_seed, porosity, cell_type, region):
    cells = porosity.shape
    pops = (19,) + cells
    fields = len(AX_SLOT[LO])
    face, rows = cells[1:], (AZ_BLOCKS, 8, cells[2])
    parity = (lax.axis_index("ax") % 2).astype(jnp.int32).reshape(1)
    post, e, o, t, flags = call(
        first_kernel,
        [pops, (fields,) + face, (fields,) + face, rows, cells],
        [],
        parity, initial, adjoint_seed, porosity, cell_type, region,
    )
    near = exchange(e, o, t)
    post, adj, sens_one, around, e, o, t = call(
        second_kernel,
        [pops, pops, cells, (18,) + cells, (fields - 1,) + face, (fields - 1,) + face, rows],
        [pops, pops],
        parity, post, adjoint_seed, flags, porosity, cell_type, region, *near,
    )
    near = exchange(e, o, t)
    regions = lax.axis_size("ax") * lax.axis_size("az") // 4
    lanes = -(-regions // 128) * 128
    final, adjoint, sensitivity, partial = call(
        third_kernel,
        [pops, pops, cells, (1, lanes)],
        [pops, (8, 128)],
        parity, post, adj, flags, around, initial, porosity, cell_type, region, sens_one, *near,
    )
    totals = sum_all(partial)[0, :regions]
    return final, adjoint, sensitivity, totals


def solution(mesh):
    return jax.shard_map(
        shards,
        mesh=mesh,
        in_specs=(
            P(None, "ax", "az", None),
            P(None, "ax", "az", None),
            P("ax", "az", None),
            P("ax", "az", None),
            P("ax", "az", None),
        ),
        out_specs=(P(None, "ax", "az", None), P(None, "ax", "az", None), P("ax", "az", None), P()),
        check_vma=False,
    )
```

```python
import functools

import jax
import jax.numpy as jnp
import numpy as np
from jax import lax
from jax.experimental import pallas as pl
from jax.experimental.pallas import tpu as pltpu
from jax.sharding import PartitionSpec as P

VELOCITY = [
    (0, 0, 0),
    (1, 0, 0),
    (-1, 0, 0),
    (0, 1, 0),
    (0, -1, 0),
    (0, 0, 1),
    (0, 0, -1),
    (1, 1, 0),
    (-1, -1, 0),
    (1, -1, 0),
    (-1, 1, 0),
    (1, 0, 1),
    (-1, 0, -1),
    (1, 0, -1),
    (-1, 0, 1),
    (0, 1, 1),
    (0, -1, -1),
    (0, 1, -1),
    (0, -1, 1),
]
OPPOSITE = [0, 2, 1, 4, 3, 6, 5, 8, 7, 10, 9, 12, 11, 14, 13, 16, 15, 18, 17]
INLET_SPEED = (0.05, 0.05, 0.0)
W_AXIS = 1.0 / 18.0
W_EDGE = 1.0 / 36.0


def moving(axis, sign):
    return [q for q in range(19) if VELOCITY[q][axis] == sign]


LO, HI = 0, 1
POST, ADJ, FACTOR, FLAG = 0, 1, 2, 3


def face_fields(kinds, axis, side):
    sign = -1 if side == LO else 1
    fields = []
    for kind in kinds:
        if kind == FLAG:
            fields.append((FLAG, 0))
        else:
            fields += [(kind, q) for q in moving(axis, -sign if kind == ADJ else sign)]
    return fields


class Layout:
    def __init__(self, kinds, extra):
        self.ax = [face_fields(kinds, 0, side) for side in (LO, HI)]
        self.slot = [{key: i for i, key in enumerate(fields)} for fields in self.ax]
        self.fields = len(self.ax[LO])
        corner, rest = [], []
        for a, sign in ((1, 1), (0, -1)):
            for side in (LO, HI):
                for kind, q in face_fields(kinds, 1, side):
                    leaves = VELOCITY[q][0] == (-sign if kind == ADJ else sign)
                    key = (side, kind, q, a)
                    (corner if kind == FLAG or leaves else rest).append(key)
        corner += extra
        self.corner_blocks = -(-len(corner) // 8)
        self.blocks = self.corner_blocks + -(-len(rest) // 8)
        self.place = {key: (i // 8, i % 8) for i, key in enumerate(corner)}
        self.place.update({key: (self.corner_blocks + i // 8, i % 8) for i, key in enumerate(rest)})


FIRST = Layout((POST, ADJ, FACTOR, FLAG), [(LO, "label"), (HI, "label")])
SECOND = Layout((POST, ADJ), [(LO, "sum")])


def pairs_of(values):
    sums = [values[q] + values[q + 1] for q in range(1, 19, 2)]
    diffs = [values[q] - values[q + 1] for q in range(1, 19, 2)]
    return sums, diffs


def projections(vec):
    va, vt, vr = vec
    return [va, vt, vr, va + vt, va - vt, va + vr, va - vr, vt + vr, vt - vr]


def linearise(pops, porous, types, regions):
    sums, diffs = pairs_of(pops)
    s0, s1, s2, s3, s4, s5, s6, s7, s8 = sums
    d0, d1, d2, d3, d4, d5, d6, d7, d8 = diffs
    at, ar, tr = s3 + s4, s5 + s6, s7 + s8
    rho = pops[0] + ((s0 + s1) + (s2 + at)) + (ar + tr)
    ma = (d0 + (d3 + d4)) + (d5 + d6)
    mt = (d1 + (d3 - d4)) + (d7 + d8)
    mr = (d2 + (d5 - d6)) + (d7 - d8)
    inv = 1.0 / rho
    ua, ut, ur = ma * inv, mt * inv, mr * inv
    third = rho * (1.0 / 3.0)
    paa = (s0 + at + ar - third) - ma * ua
    ptt = (s1 + at + tr - third) - mt * ut
    prr = (s2 + ar + tr - third) - mr * ur
    pat = (s3 - s4) - ma * ut
    par = (s5 - s6) - ma * ur
    ptr = (s7 - s8) - mt * ur
    square = (paa * paa + ptt * ptt + prr * prr) + 2.0 * (pat * pat + par * par + ptr * ptr) + 0.0001
    inv_root = lax.rsqrt(square)
    shear = 1.5 * (square * inv_root) * inv
    shifted = shear + 0.01
    viscous = 0.02 * jnp.exp((0.7 - 1.0) * jnp.log(shifted))
    omega = 1.0 / (0.5 + 3.0 * viscous)
    relaxed = (types != 2) & (types != 3)
    kappa = jnp.where(regions > 0, porous, 0.0)
    return dict(
        rho=rho,
        inv=inv,
        u=(ua, ut, ur),
        p=(paa, ptt, prr, pat, par, ptr),
        inv_root=inv_root,
        shear=shear,
        shifted=shifted,
        viscous=viscous,
        omega=omega,
        relaxed=relaxed,
        kappa=kappa,
        keep=jnp.where(relaxed, 1.0 - omega, 0.0),
        design=jnp.where(relaxed & (regions > 0), 1.0, 0.0),
        inlet=types == 2,
        outlet=types == 3,
    )


def collide(pops, lin):
    rho, relaxed, inlet = lin["rho"], lin["relaxed"], lin["inlet"]
    ua, ut, ur = (jnp.where(inlet, speed, x) for x, speed in zip(lin["u"], INLET_SPEED))
    scale = jnp.where(relaxed, (lin["omega"] - lin["kappa"]) * rho, 1.0)
    rest = jnp.where(relaxed, lin["kappa"] * rho, 0.0)
    keep = lin["keep"]
    still = 1.0 - 1.5 * (ua * ua + ut * ut + ur * ur)
    post = [keep * pops[0] + (1.0 / 3.0) * (scale * still + rest)]
    for i, cu in enumerate(projections((ua, ut, ur))):
        weight = W_AXIS if i < 3 else W_EDGE
        even = weight * (scale * (still + 4.5 * cu * cu) + rest)
        odd = (3.0 * weight) * (scale * cu)
        post.append(keep * pops[1 + 2 * i] + (even + odd))
        post.append(keep * pops[2 + 2 * i] + (even - odd))
    return post


def pull_back(back, pops, lin):
    sums, diffs = pairs_of(back)
    s0, s1, s2, s3, s4, s5, s6, s7, s8 = sums
    d0, d1, d2, d3, d4, d5, d6, d7, d8 = diffs
    at, ar, tr = s3 + s4, s5 + s6, s7 + s8
    b0 = (1.0 / 3.0) * back[0] + W_AXIS * (s0 + s1 + s2) + W_EDGE * (at + ar + tr)
    ba = W_AXIS * d0 + W_EDGE * ((d3 + d4) + (d5 + d6))
    bt = W_AXIS * d1 + W_EDGE * ((d3 - d4) + (d7 + d8))
    br = W_AXIS * d2 + W_EDGE * ((d5 - d6) + (d7 - d8))
    baa = W_AXIS * s0 + W_EDGE * (at + ar)
    btt = W_AXIS * s1 + W_EDGE * (at + tr)
    brr = W_AXIS * s2 + W_EDGE * (ar + tr)
    bat, bar, btr = W_EDGE * (s3 - s4), W_EDGE * (s5 - s6), W_EDGE * (s7 - s8)
    along = back[0] * pops[0]
    for q in range(1, 19):
        along = along + back[q] * pops[q]
    rho, inv = lin["rho"], lin["inv"]
    ua, ut, ur = lin["u"]
    qa = baa * ua + bat * ut + bar * ur
    qt = bat * ua + btt * ut + btr * ur
    qr = bar * ua + btr * ut + brr * ur
    uu = ua * ua + ut * ut + ur * ur
    slope = 3.0 * (ua * ba + ut * bt + ur * br) + 4.5 * (ua * qa + ut * qt + ur * qr) - 1.5 * (uu * b0)
    full = b0 + slope
    sens = -(lin["design"] * (rho * slope))
    relaxed, omega = lin["relaxed"], lin["omega"]
    shear_bar = (rho * full - along) * (omega * omega) * (0.9 * lin["viscous"]) / lin["shifted"]
    shear_bar = jnp.where(relaxed, shear_bar, 0.0)
    z = shear_bar * (1.5 * inv) * lin["inv_root"]
    maa, mtt, mrr, mat, mar, mtr = (z * x for x in lin["p"])
    scale = jnp.where(relaxed, omega - lin["kappa"], jnp.where(lin["outlet"], inv, 0.0))
    la = maa * ua + mat * ut + mar * ur
    lt = mat * ua + mtt * ut + mtr * ur
    lr = mar * ua + mtr * ut + mrr * ur
    va = scale * (3.0 * (ba - b0 * ua) + 9.0 * qa) - 2.0 * la
    vt = scale * (3.0 * (bt - b0 * ut) + 9.0 * qt) - 2.0 * lt
    vr = scale * (3.0 * (br - b0 * ur) + 9.0 * qr) - 2.0 * lr
    total = jnp.where(relaxed, lin["kappa"] * b0 + scale * full, 0.0)
    total = total - shear_bar * lin["shear"] * inv - (1.0 / 3.0) * (maa + mtt + mrr)
    total = total - ((la + va) * ua + (lt + vt) * ut + (lr + vr) * ur)
    keep = lin["keep"]
    taa, ttt, trr = total + maa, total + mtt, total + mrr
    sat, sar, str_ = taa + mtt, taa + mrr, ttt + mrr
    mat2, mar2, mtr2 = 2.0 * mat, 2.0 * mar, 2.0 * mtr
    evens = [taa, ttt, trr, sat + mat2, sat - mat2, sar + mar2, sar - mar2, str_ + mtr2, str_ - mtr2]
    result = [keep * back[0] + total]
    for i, odd in enumerate(projections((va, vt, vr))):
        result.append(keep * back[1 + 2 * i] + (evens[i] + odd))
        result.append(keep * back[2 + 2 * i] + (evens[i] - odd))
    return result, sens


class Fields:
    def __init__(self, layout, own, parity, e, o, t, ec, oc):
        self.layout, self.own = layout, own
        self.e, self.o, self.t, self.ec, self.oc = e, o, t, ec, oc
        self.up_e = parity == 0
        self.rows_a = own[POST].shape[1]

    def row(self, kind, q, a):
        if 0 <= a < self.rows_a:
            return self.own[FLAG][a] if kind == FLAG else self.own[kind][q, a]
        if a < 0:
            slot = self.layout.slot[HI][(kind, q)]
            return jnp.where(self.up_e, self.o[slot], self.e[slot])
        slot = self.layout.slot[LO][(kind, q)]
        return jnp.where(self.up_e, self.e[slot], self.o[slot])

    def row_label(self, a):
        slot = self.layout.fields
        e, o = self.e[slot, 0:1, :], self.o[slot, 0:1, :]
        return jnp.where(self.up_e, o, e) if a < 0 else jnp.where(self.up_e, e, o)

    def message(self, key, a):
        block, i = self.layout.place[key]
        rows = (block, slice(i, i + 1))
        if 0 <= a < self.rows_a:
            return self.t[rows]
        if a < 0:
            return jnp.where(self.up_e, self.oc[rows], self.ec[rows])
        return jnp.where(self.up_e, self.ec[rows], self.oc[rows])

    def edge(self, side, kind, q, a):
        row = self.rows_a - 1 if a < 0 else 0 if a >= self.rows_a else a
        return self.message((side, kind, q, row), a)

    def moved(self, kind, q, a, shift):
        sa, st, sr = shift
        value = self.row(kind, q, a + sa)
        rows_t, rows_r = value.shape
        if st:
            value = pltpu.roll(value, (-st) % rows_t, 0)
            beyond = self.edge(LO if st > 0 else HI, kind, q, a + sa)
            at_edge = lax.broadcasted_iota(jnp.int32, value.shape, 0) == (rows_t - 1 if st > 0 else 0)
            value = jnp.where(at_edge, beyond, value)
        if sr:
            value = pltpu.roll(value, (-sr) % rows_r, 1)
        return value


def pack(layout, own, parity, e_ref, o_ref, t_ref):
    rows_a, rows_t = own[POST].shape[1], own[POST].shape[2]
    even = parity == 0

    def cells(kind, q, a):
        return own[FLAG].at[a] if kind == FLAG else own[kind].at[q, a]

    for key, (block, i) in layout.place.items():
        if len(key) == 4:
            side, kind, q, a = key
            t = 0 if side == LO else rows_t - 1
            t_ref[block, i : i + 1, :] = cells(kind, q, a)[t : t + 1, :]
    for slot in range(layout.fields):
        low = cells(*layout.ax[LO][slot], 0)[...]
        high = cells(*layout.ax[HI][slot], rows_a - 1)[...]
        e_ref[slot] = jnp.where(even, high, low)
        o_ref[slot] = jnp.where(even, low, high)


def chunks(rows_a, shape, body):
    counts = (len(rows_a), shape[1] // 8, shape[2] // 128)

    def step(i, carry):
        a = rows_a[0] + i // (counts[1] * counts[2])
        t = pl.multiple_of((i // counts[2]) % counts[1] * 8, 8)
        r = pl.multiple_of(i % counts[2] * 128, 128)
        body((a, pl.ds(t, 8), pl.ds(r, 128)))
        return carry

    lax.fori_loop(0, counts[0] * counts[1] * counts[2], step, 0)


def load(ref, where):
    return [ref[(q,) + where] for q in range(19)]


def store(ref, where, values):
    for q in range(19):
        ref[(q,) + where] = values[q]


def label_of(regions, wide):
    label = jnp.max(jnp.max(regions[...], axis=0), axis=(0, 1), keepdims=True)
    return jnp.broadcast_to(label.astype(jnp.float32), (1, wide))


def porosity_factors(lin):
    ua, ut, ur = lin["u"]
    weight = -(lin["design"] * lin["rho"])
    still = -1.5 * (ua * ua + ut * ut + ur * ur)
    result = [(1.0 / 3.0) * weight * still]
    for i, cu in enumerate(projections((ua, ut, ur))):
        scaled = (W_AXIS if i < 3 else W_EDGE) * weight
        even, odd = scaled * (still + 4.5 * cu * cu), 3.0 * scaled * cu
        result += [even + odd, even - odd]
    return result


def first_kernel(
    parity_ref, pops_hbm, seed_hbm, porous_hbm, types_hbm, regions_hbm,
    post, factors, e_out, o_out, t_out, flags, pops, seed, porous, types, regions, sems,
):
    rows_a = porous.shape[0]
    loads = [
        pltpu.make_async_copy(source, target, sems.at[i])
        for i, (source, target) in enumerate(
            [(types_hbm, types), (regions_hbm, regions), (porous_hbm, porous)]
            + [(pops_hbm.at[:, a], pops.at[:, a]) for a in range(rows_a)]
            + [(seed_hbm, seed)]
        )
    ]
    for copy in loads:
        copy.start()
    for copy in loads[:3]:
        copy.wait()
    flags[...] = jnp.where(types[...] != 1, 1.0, 0.0)
    label = label_of(regions, porous.shape[2])
    for side in (LO, HI):
        block, i = FIRST.place[(side, "label")]
        t_out[block, i : i + 1, :] = label
    for out in (e_out, o_out):
        out[FIRST.fields] = jnp.broadcast_to(label, out.shape[1:])

    def body(where):
        values = load(pops, where)
        lin = linearise(values, porous[where], types[where], regions[where])
        store(post, where, collide(values, lin))
        store(factors, where, porosity_factors(lin))

    for a in range(rows_a):
        loads[3 + a].wait()
        chunks([a], porous.shape, body)
    loads[-1].wait()
    own = {POST: post, ADJ: seed, FACTOR: factors, FLAG: flags}
    pack(FIRST, own, parity_ref[0], e_out, o_out, t_out)


def second_kernel(
    parity_ref, post, seed, factors, flags, porous, types, regions, e, o, t, ec, oc,
    post_next, adj, sens, around, e_out, o_out, t_out, state, back, parts,
):
    own = {POST: post, ADJ: seed, FACTOR: factors, FLAG: flags}
    fields = Fields(FIRST, own, parity_ref[0], e, o, t, ec, oc)
    rows_a, rows_t, rows_r = porous.shape
    for a in range(rows_a):
        centre = flags[a]
        state[0, a] = post[0, a]
        back[0, a] = seed[0, a]
        for q in range(1, 19):
            behind = tuple(-c for c in VELOCITY[q])
            open_ = fields.moved(FLAG, 0, a, behind)
            around[q - 1, a] = open_
            opp = OPPOSITE[q]
            state[q, a] = jnp.where(open_ > 0, fields.moved(POST, q, a, behind), post[opp, a])
            back[opp, a] = centre * fields.moved(ADJ, opp, a, behind) + (1.0 - open_) * seed[q, a]

    def body(where):
        values = load(state, where)
        lin = linearise(values, porous[where], types[where], regions[where])
        store(post_next, where, collide(values, lin))
        result, partial_sens = pull_back(load(back, where), values, lin)
        store(adj, where, result)
        sens[where] = partial_sens

    chunks(range(rows_a), porous.shape, body)
    pack(SECOND, {POST: post_next, ADJ: adj}, parity_ref[0], e_out, o_out, t_out)
    sums = {(i, st): [] for i in (-1, 0, 1) for st in (-1, 0, 1)}
    for a in range(rows_a):
        sums[(0, 0)] += [sens[a], factors[0, a] * adj[0, a]]
        for q in range(1, 19):
            behind = tuple(-c for c in VELOCITY[q])
            open_, value = around[q - 1, a], adj[q, a]
            sums[(0, 0)].append(jnp.where(open_ > 0, 0.0, factors[OPPOSITE[q], a]) * value)
            term = jnp.where(open_ > 0, fields.moved(FACTOR, q, a, behind), 0.0) * value
            from_a = a + behind[0]
            beyond = -1 if from_a < 0 else 1 if from_a >= rows_a else 0
            sums[(beyond, behind[1])].append(term)
    at_t = lax.broadcasted_iota(jnp.int32, (rows_t, rows_r), 0)
    rows = []
    for beyond in (-1, 0, 1):
        low, centre, high = (functools.reduce(jnp.add, sums[(beyond, st)]) for st in (-1, 0, 1))
        inner = centre + jnp.where(at_t == 0, 0.0, low) + jnp.where(at_t == rows_t - 1, 0.0, high)
        label = label_of(regions, rows_r) if beyond == 0 else fields.row_label(beyond)
        a = {-1: -1, 0: 0, 1: rows_a}[beyond]
        rows.append((jnp.sum(inner, axis=0, keepdims=True), label))
        rows.append((high[rows_t - 1 : rows_t], fields.message((LO, "label"), a)))
        rows.append((low[0:1], fields.message((HI, "label"), a)))
    parts[...] = jnp.zeros_like(parts)
    for i, (value, label) in enumerate(rows):
        parts[0, i : i + 1, :] = value
        parts[1, i : i + 1, :] = label
    lanes = lax.broadcasted_iota(jnp.int32, parts.shape[1:], 1) + 1
    total = jnp.sum(parts[0], axis=1, keepdims=True)
    chosen = jnp.where(lanes == parts[1].astype(jnp.int32), total, 0.0)
    block, i = SECOND.place[(LO, "sum")]
    t_out[block, i : i + 1, :] = jnp.sum(chosen, axis=0, keepdims=True)


def third_kernel(
    parity_ref, post, adj, flags, around, pops, porous, types, regions, sens_one, e, o, t, ec, oc,
    final_hbm, result_hbm, sens, final, result, back, sems,
):
    fields = Fields(SECOND, {POST: post, ADJ: adj}, parity_ref[0], e, o, t, ec, oc)
    rows_a = porous.shape[0]
    stores = []
    for a in range(rows_a):
        final[0, a] = post[0, a]
        for q in range(1, 19):
            behind = tuple(-c for c in VELOCITY[q])
            moved = fields.moved(POST, q, a, behind)
            final[q, a] = jnp.where(around[q - 1, a] > 0, moved, post[OPPOSITE[q], a])
        stores.append(pltpu.make_async_copy(final.at[:, a], final_hbm.at[:, a], sems.at[a]))
        stores[-1].start()

    def body(where):
        values = load(pops, where)
        lin = linearise(values, porous[where], types[where], regions[where])
        adjoint, partial_sens = pull_back(load(back, where), values, lin)
        store(result, where, adjoint)
        sens[where] = partial_sens + sens_one[where]

    for a in range(rows_a):
        centre = flags[a]
        back[0, a] = adj[0, a]
        for q in range(1, 19):
            behind = tuple(-c for c in VELOCITY[q])
            opp = OPPOSITE[q]
            ahead = centre * fields.moved(ADJ, opp, a, behind)
            back[opp, a] = ahead + (1.0 - around[q - 1, a]) * adj[q, a]
        chunks([a], porous.shape, body)
        stores.append(pltpu.make_async_copy(result.at[:, a], result_hbm.at[:, a], sems.at[rows_a + a]))
        stores[-1].start()
    for copy in stores:
        copy.wait()


VMEM, HBM = pltpu.VMEM, pltpu.HBM


def call(body, in_spaces, outs, scratch, parity, *arrays):
    spaces = in_spaces + [VMEM] * (len(arrays) - len(in_spaces))
    return pl.pallas_call(
        body,
        out_shape=[jax.ShapeDtypeStruct(shape, jnp.float32) for shape, _ in outs],
        in_specs=[pl.BlockSpec(memory_space=pltpu.SMEM)]
        + [pl.BlockSpec(memory_space=space) for space in spaces],
        out_specs=[pl.BlockSpec(memory_space=space) for _, space in outs],
        scratch_shapes=scratch,
        compiler_params=pltpu.CompilerParams(vmem_limit_bytes=40 * 1024 * 1024),
    )(parity, *arrays)


def even_pairs(size):
    return [(i, i ^ 1) for i in range(size) if i ^ 1 < size]


def odd_pairs(size):
    return [(i, ((i + 1) ^ 1) - 1) for i in range(size) if 0 <= ((i + 1) ^ 1) - 1 < size]


def exchange(layout, e_msg, o_msg, t_msg, totals_row=None):
    size_a, size_t = lax.axis_size("ax"), lax.axis_size("az")
    ring = [(i, (i + 1) % size_t) for i in range(size_t)]
    t = lax.ppermute(t_msg, "az", ring)
    if size_t > 2:
        from_high = np.zeros((layout.blocks, 8, 1), bool)
        for key, (block, i) in layout.place.items():
            from_high[block, i] = key[0] == HI
        t_down = lax.ppermute(t_msg, "az", [(j, i) for i, j in ring])
        t = jnp.where(jnp.asarray(from_high), t, t_down)
    e = lax.ppermute(e_msg, "ax", even_pairs(size_a))
    o = lax.ppermute(o_msg, "ax", odd_pairs(size_a))
    corners = t[: layout.corner_blocks]
    total = None
    if totals_row is not None:
        block, i = totals_row
        total = t_msg[block, i : i + 1]
        total = total + t[block, i : i + 1] if size_t == 2 else sum_over(total, "az", 1)
        corners = lax.dynamic_update_slice(corners, total[None], (block, i, 0))
    ec = lax.ppermute(corners, "ax", even_pairs(size_a))
    oc = lax.ppermute(corners, "ax", odd_pairs(size_a))
    if totals_row is not None:
        if size_a & (size_a - 1):
            total = lax.psum(total, "ax")
        elif size_a > 1:
            total = sum_over(total + ec[block, i : i + 1], "ax", 2)
    return (e, o, t, ec, oc), total


def sum_over(x, axis, step):
    size = lax.axis_size(axis)
    if size & (size - 1):
        return lax.psum(x, axis)
    while step < size:
        x = x + lax.ppermute(x, axis, [(i, i ^ step) for i in range(size)])
        step *= 2
    return x


def shards(initial, adjoint_seed, porosity, cell_type, region):
    cells = porosity.shape
    pops = (19,) + cells
    face, wide = cells[1:], cells[2]
    parity = (lax.axis_index("ax") % 2).astype(jnp.int32).reshape(1)
    scratch = functools.partial(pltpu.VMEM, dtype=jnp.float32)
    ints = functools.partial(pltpu.VMEM, dtype=jnp.int32)

    def messages(layout, more):
        axial = (layout.fields + more,) + face
        return [(axial, VMEM), (axial, VMEM), ((layout.blocks, 8, wide), VMEM)]

    post, factors, e, o, t, flags = call(
        first_kernel,
        [HBM] * 5,
        [(pops, VMEM), (pops, VMEM)] + messages(FIRST, 1) + [(cells, VMEM)],
        [scratch(pops), scratch(pops), scratch(cells), ints(cells), ints(cells)]
        + [pltpu.SemaphoreType.DMA((4 + cells[0],))],
        parity, initial, adjoint_seed, porosity, cell_type, region,
    )
    near, _ = exchange(FIRST, e, o, t)
    post, adj, sens_one, around, e, o, t = call(
        second_kernel,
        [],
        [(pops, VMEM), (pops, VMEM), (cells, VMEM), ((18,) + cells, VMEM)] + messages(SECOND, 0),
        [scratch(pops), scratch(pops), scratch((2, 16, wide))],
        parity, post, adjoint_seed, factors, flags, porosity, cell_type, region, *near,
    )
    near, totals = exchange(SECOND, e, o, t, SECOND.place[(LO, "sum")])
    final, adjoint, sensitivity = call(
        third_kernel,
        [],
        [(pops, HBM), (pops, HBM), (cells, VMEM)],
        [scratch(pops), scratch(pops), scratch(pops), pltpu.SemaphoreType.DMA((2 * cells[0],))],
        parity, post, adj, flags, around, initial, porosity, cell_type, region, sens_one, *near,
    )
    regions = lax.axis_size("ax") * lax.axis_size("az") // 4
    return final, adjoint, sensitivity, totals[0, :regions]


def solution(mesh):
    return jax.shard_map(
        shards,
        mesh=mesh,
        in_specs=(
            P(None, "ax", "az", None),
            P(None, "ax", "az", None),
            P("ax", "az", None),
            P("ax", "az", None),
            P("ax", "az", None),
        ),
        out_specs=(P(None, "ax", "az", None), P(None, "ax", "az", None), P("ax", "az", None), P()),
        check_vma=False,
    )
```

```python
import functools

import jax
import jax.numpy as jnp
import numpy as np
from jax import lax
from jax.experimental import pallas as pl
from jax.experimental.pallas import tpu as pltpu
from jax.sharding import PartitionSpec as P

VELOCITY = [
    (0, 0, 0),
    (1, 0, 0),
    (-1, 0, 0),
    (0, 1, 0),
    (0, -1, 0),
    (0, 0, 1),
    (0, 0, -1),
    (1, 1, 0),
    (-1, -1, 0),
    (1, -1, 0),
    (-1, 1, 0),
    (1, 0, 1),
    (-1, 0, -1),
    (1, 0, -1),
    (-1, 0, 1),
    (0, 1, 1),
    (0, -1, -1),
    (0, 1, -1),
    (0, -1, 1),
]
OPPOSITE = [0, 2, 1, 4, 3, 6, 5, 8, 7, 10, 9, 12, 11, 14, 13, 16, 15, 18, 17]
INLET_SPEED = (0.05, 0.05, 0.0)
W_AXIS = 1.0 / 18.0
W_EDGE = 1.0 / 36.0


def moving(axis, sign):
    return [q for q in range(19) if VELOCITY[q][axis] == sign]


LO, HI = 0, 1
POST, ADJ, FACTOR, FLAG = 0, 1, 2, 3


def face_fields(kinds, axis, side):
    sign = -1 if side == LO else 1
    fields = []
    for kind in kinds:
        if kind == FLAG:
            fields.append((FLAG, 0))
        else:
            fields += [(kind, q) for q in moving(axis, -sign if kind == ADJ else sign)]
    return fields


class Layout:
    def __init__(self, kinds, extra):
        self.ax = [face_fields(kinds, 0, side) for side in (LO, HI)]
        self.slot = [{key: i for i, key in enumerate(fields)} for fields in self.ax]
        self.fields = len(self.ax[LO])
        corner, rest = [], []
        for a, sign in ((1, 1), (0, -1)):
            for side in (LO, HI):
                for kind, q in face_fields(kinds, 1, side):
                    leaves = VELOCITY[q][0] == (-sign if kind == ADJ else sign)
                    key = (side, kind, q, a)
                    (corner if kind == FLAG or leaves else rest).append(key)
        corner += extra
        self.corner_blocks = -(-len(corner) // 8)
        self.blocks = self.corner_blocks + -(-len(rest) // 8)
        self.place = {key: (i // 8, i % 8) for i, key in enumerate(corner)}
        self.place.update({key: (self.corner_blocks + i // 8, i % 8) for i, key in enumerate(rest)})


FIRST = Layout((POST, ADJ, FACTOR, FLAG), [(LO, "label"), (HI, "label"), (LO, "own")])
SECOND = Layout((POST, ADJ), [(LO, "sum")])


def pairs_of(values):
    sums = [values[q] + values[q + 1] for q in range(1, 19, 2)]
    diffs = [values[q] - values[q + 1] for q in range(1, 19, 2)]
    return sums, diffs


def projections(vec):
    va, vt, vr = vec
    return [va, vt, vr, va + vt, va - vt, va + vr, va - vr, vt + vr, vt - vr]


def linearise(pops, porous, types, regions):
    sums, diffs = pairs_of(pops)
    s0, s1, s2, s3, s4, s5, s6, s7, s8 = sums
    d0, d1, d2, d3, d4, d5, d6, d7, d8 = diffs
    at, ar, tr = s3 + s4, s5 + s6, s7 + s8
    rho = pops[0] + ((s0 + s1) + (s2 + at)) + (ar + tr)
    ma = (d0 + (d3 + d4)) + (d5 + d6)
    mt = (d1 + (d3 - d4)) + (d7 + d8)
    mr = (d2 + (d5 - d6)) + (d7 - d8)
    inv = 1.0 / rho
    ua, ut, ur = ma * inv, mt * inv, mr * inv
    third = rho * (1.0 / 3.0)
    paa = (s0 + at + ar - third) - ma * ua
    ptt = (s1 + at + tr - third) - mt * ut
    prr = (s2 + ar + tr - third) - mr * ur
    pat = (s3 - s4) - ma * ut
    par = (s5 - s6) - ma * ur
    ptr = (s7 - s8) - mt * ur
    square = (paa * paa + ptt * ptt + prr * prr) + 2.0 * (pat * pat + par * par + ptr * ptr) + 0.0001
    inv_root = lax.rsqrt(square)
    shear = 1.5 * (square * inv_root) * inv
    shifted = shear + 0.01
    viscous = 0.02 * jnp.exp((0.7 - 1.0) * jnp.log(shifted))
    omega = 1.0 / (0.5 + 3.0 * viscous)
    relaxed = (types != 2) & (types != 3)
    kappa = jnp.where(regions > 0, porous, 0.0)
    return dict(
        rho=rho,
        inv=inv,
        u=(ua, ut, ur),
        p=(paa, ptt, prr, pat, par, ptr),
        inv_root=inv_root,
        shear=shear,
        shifted=shifted,
        viscous=viscous,
        omega=omega,
        relaxed=relaxed,
        kappa=kappa,
        keep=jnp.where(relaxed, 1.0 - omega, 0.0),
        design=jnp.where(relaxed & (regions > 0), 1.0, 0.0),
        inlet=types == 2,
        outlet=types == 3,
    )


def collide(pops, lin):
    rho, relaxed, inlet = lin["rho"], lin["relaxed"], lin["inlet"]
    ua, ut, ur = (jnp.where(inlet, speed, x) for x, speed in zip(lin["u"], INLET_SPEED))
    scale = jnp.where(relaxed, (lin["omega"] - lin["kappa"]) * rho, 1.0)
    rest = jnp.where(relaxed, lin["kappa"] * rho, 0.0)
    keep = lin["keep"]
    still = 1.0 - 1.5 * (ua * ua + ut * ut + ur * ur)
    post = [keep * pops[0] + (1.0 / 3.0) * (scale * still + rest)]
    for i, cu in enumerate(projections((ua, ut, ur))):
        weight = W_AXIS if i < 3 else W_EDGE
        even = weight * (scale * (still + 4.5 * cu * cu) + rest)
        odd = (3.0 * weight) * (scale * cu)
        post.append(keep * pops[1 + 2 * i] + (even + odd))
        post.append(keep * pops[2 + 2 * i] + (even - odd))
    return post


def pull_back(back, pops, lin):
    sums, diffs = pairs_of(back)
    s0, s1, s2, s3, s4, s5, s6, s7, s8 = sums
    d0, d1, d2, d3, d4, d5, d6, d7, d8 = diffs
    at, ar, tr = s3 + s4, s5 + s6, s7 + s8
    b0 = (1.0 / 3.0) * back[0] + W_AXIS * (s0 + s1 + s2) + W_EDGE * (at + ar + tr)
    ba = W_AXIS * d0 + W_EDGE * ((d3 + d4) + (d5 + d6))
    bt = W_AXIS * d1 + W_EDGE * ((d3 - d4) + (d7 + d8))
    br = W_AXIS * d2 + W_EDGE * ((d5 - d6) + (d7 - d8))
    baa = W_AXIS * s0 + W_EDGE * (at + ar)
    btt = W_AXIS * s1 + W_EDGE * (at + tr)
    brr = W_AXIS * s2 + W_EDGE * (ar + tr)
    bat, bar, btr = W_EDGE * (s3 - s4), W_EDGE * (s5 - s6), W_EDGE * (s7 - s8)
    along = back[0] * pops[0]
    for q in range(1, 19):
        along = along + back[q] * pops[q]
    rho, inv = lin["rho"], lin["inv"]
    ua, ut, ur = lin["u"]
    qa = baa * ua + bat * ut + bar * ur
    qt = bat * ua + btt * ut + btr * ur
    qr = bar * ua + btr * ut + brr * ur
    uu = ua * ua + ut * ut + ur * ur
    slope = 3.0 * (ua * ba + ut * bt + ur * br) + 4.5 * (ua * qa + ut * qt + ur * qr) - 1.5 * (uu * b0)
    full = b0 + slope
    sens = -(lin["design"] * (rho * slope))
    relaxed, omega = lin["relaxed"], lin["omega"]
    shear_bar = (rho * full - along) * (omega * omega) * (0.9 * lin["viscous"]) / lin["shifted"]
    shear_bar = jnp.where(relaxed, shear_bar, 0.0)
    z = shear_bar * (1.5 * inv) * lin["inv_root"]
    maa, mtt, mrr, mat, mar, mtr = (z * x for x in lin["p"])
    scale = jnp.where(relaxed, omega - lin["kappa"], jnp.where(lin["outlet"], inv, 0.0))
    la = maa * ua + mat * ut + mar * ur
    lt = mat * ua + mtt * ut + mtr * ur
    lr = mar * ua + mtr * ut + mrr * ur
    va = scale * (3.0 * (ba - b0 * ua) + 9.0 * qa) - 2.0 * la
    vt = scale * (3.0 * (bt - b0 * ut) + 9.0 * qt) - 2.0 * lt
    vr = scale * (3.0 * (br - b0 * ur) + 9.0 * qr) - 2.0 * lr
    total = jnp.where(relaxed, lin["kappa"] * b0 + scale * full, 0.0)
    total = total - shear_bar * lin["shear"] * inv - (1.0 / 3.0) * (maa + mtt + mrr)
    total = total - ((la + va) * ua + (lt + vt) * ut + (lr + vr) * ur)
    keep = lin["keep"]
    taa, ttt, trr = total + maa, total + mtt, total + mrr
    sat, sar, str_ = taa + mtt, taa + mrr, ttt + mrr
    mat2, mar2, mtr2 = 2.0 * mat, 2.0 * mar, 2.0 * mtr
    evens = [taa, ttt, trr, sat + mat2, sat - mat2, sar + mar2, sar - mar2, str_ + mtr2, str_ - mtr2]
    result = [keep * back[0] + total]
    for i, odd in enumerate(projections((va, vt, vr))):
        result.append(keep * back[1 + 2 * i] + (evens[i] + odd))
        result.append(keep * back[2 + 2 * i] + (evens[i] - odd))
    return result, sens


class Fields:
    def __init__(self, layout, own, parity, e, o, t, ec=None, oc=None):
        self.layout, self.own = layout, own
        self.e, self.o, self.t, self.ec, self.oc = e, o, t, ec, oc
        self.up_e = parity == 0
        self.rows_a = own[POST].shape[1]

    def row(self, kind, q, a):
        if 0 <= a < self.rows_a:
            return self.own[FLAG][a] if kind == FLAG else self.own[kind][q, a]
        if a < 0:
            slot = self.layout.slot[HI][(kind, q)]
            return jnp.where(self.up_e, self.o[slot], self.e[slot])
        slot = self.layout.slot[LO][(kind, q)]
        return jnp.where(self.up_e, self.e[slot], self.o[slot])

    def message(self, key, a):
        block, i = self.layout.place[key]
        rows = (block, slice(i, i + 1))
        if 0 <= a < self.rows_a:
            return self.t[rows]
        if self.ec is None:
            rows = (self.layout.fields, slice(8 * block + i, 8 * block + i + 1))
            e, o = self.e[rows], self.o[rows]
        else:
            e, o = self.ec[rows], self.oc[rows]
        return jnp.where(self.up_e, o, e) if a < 0 else jnp.where(self.up_e, e, o)

    def edge(self, side, kind, q, a):
        row = self.rows_a - 1 if a < 0 else 0 if a >= self.rows_a else a
        return self.message((side, kind, q, row), a)

    def moved(self, kind, q, a, shift):
        sa, st, sr = shift
        value = self.row(kind, q, a + sa)
        rows_t, rows_r = value.shape
        if st:
            value = pltpu.roll(value, (-st) % rows_t, 0)
            beyond = self.edge(LO if st > 0 else HI, kind, q, a + sa)
            at_edge = lax.broadcasted_iota(jnp.int32, value.shape, 0) == (rows_t - 1 if st > 0 else 0)
            value = jnp.where(at_edge, beyond, value)
        if sr:
            value = pltpu.roll(value, (-sr) % rows_r, 1)
        return value


def cells(own, kind, q, a):
    return own[FLAG].at[a] if kind == FLAG else own[kind].at[q, a]


def pack_azimuthal(layout, own, t_ref):
    rows_t = own[POST].shape[2]
    for key, (block, i) in layout.place.items():
        if len(key) == 4:
            side, kind, q, a = key
            t = 0 if side == LO else rows_t - 1
            t_ref[block, i : i + 1, :] = cells(own, kind, q, a)[t : t + 1, :]


def pack_axial(layout, own, parity, e_ref, o_ref):
    rows_a = own[POST].shape[1]
    even = parity == 0
    for slot in range(layout.fields):
        low = cells(own, *layout.ax[LO][slot], 0)[...]
        high = cells(own, *layout.ax[HI][slot], rows_a - 1)[...]
        e_ref[slot] = jnp.where(even, high, low)
        o_ref[slot] = jnp.where(even, low, high)


def chunks(rows_a, shape, body):
    counts = (len(rows_a), shape[1] // 8, shape[2] // 128)

    def step(i, carry):
        a = rows_a[0] + i // (counts[1] * counts[2])
        t = pl.multiple_of((i // counts[2]) % counts[1] * 8, 8)
        r = pl.multiple_of(i % counts[2] * 128, 128)
        body((a, pl.ds(t, 8), pl.ds(r, 128)))
        return carry

    lax.fori_loop(0, counts[0] * counts[1] * counts[2], step, 0)


def load(ref, where):
    return [ref[(q,) + where] for q in range(19)]


def store(ref, where, values):
    for q in range(19):
        ref[(q,) + where] = values[q]


def label_of(regions, wide):
    label = jnp.max(jnp.max(regions[...], axis=0), axis=(0, 1), keepdims=True)
    return jnp.broadcast_to(label.astype(jnp.float32), (1, wide))


def porosity_factors(lin):
    ua, ut, ur = lin["u"]
    weight = -(lin["design"] * lin["rho"])
    still = -1.5 * (ua * ua + ut * ut + ur * ur)
    result = [(1.0 / 3.0) * weight * still]
    for i, cu in enumerate(projections((ua, ut, ur))):
        scaled = (W_AXIS if i < 3 else W_EDGE) * weight
        even, odd = scaled * (still + 4.5 * cu * cu), 3.0 * scaled * cu
        result += [even + odd, even - odd]
    return result


def edge_kernel(
    pops_hbm, seed_hbm, porous_hbm, types_hbm, regions_hbm,
    pops, seed, porous, types, regions, t_out, edge, edge_post, edge_factors, sems,
):
    rows_a, rows_t, rows_r = porous.shape
    pairs = [(types_hbm, types), (regions_hbm, regions), (porous_hbm, porous)]
    pairs += [(pops_hbm, pops), (seed_hbm, seed)]
    loads = [pltpu.make_async_copy(*pair, sems.at[i]) for i, pair in enumerate(pairs)]
    for copy in loads:
        copy.start()
    for copy in loads[:3]:
        copy.wait()
    label = label_of(regions, rows_r)
    for key in ((LO, "label"), (HI, "label"), (LO, "own")):
        block, i = FIRST.place[key]
        t_out[block, i : i + 1, :] = label
    columns = [(a, t) for a in range(rows_a) for t in (0, rows_t - 1)]

    def gather(source, target):
        for i, (a, t) in enumerate(columns):
            target[i : i + 1, :] = source[a, t : t + 1, :]

    gather(porous, edge.at[19])
    gather_types = jnp.concatenate([types[a, t : t + 1, :] for a, t in columns] * 2)
    gather_regions = jnp.concatenate([regions[a, t : t + 1, :] for a, t in columns] * 2)
    for i in range(len(columns), edge.shape[1]):
        edge[:, i, :] = jnp.ones((edge.shape[0], rows_r), jnp.float32)
    loads[3].wait()
    for q in range(19):
        gather(pops.at[q], edge.at[q])
    values = [edge[q] for q in range(19)]
    lin = linearise(values, edge[19], gather_types, gather_regions)
    post = collide(values, lin)
    factors = porosity_factors(lin)
    for q in range(19):
        edge_post[q] = post[q]
        edge_factors[q] = factors[q]
    edge[0] = jnp.where(gather_types != 1, 1.0, 0.0)
    loads[4].wait()
    for key, (block, i) in FIRST.place.items():
        if len(key) == 4:
            side, kind, q, a = key
            t = 0 if side == LO else rows_t - 1
            k = columns.index((a, t))
            if kind == ADJ:
                row = seed[q, a, t : t + 1, :]
            elif kind == FLAG:
                row = edge[0, k : k + 1, :]
            else:
                row = (edge_post if kind == POST else edge_factors)[q, k : k + 1, :]
            t_out[block, i : i + 1, :] = row


def first_kernel(
    parity_ref, pops, seed, porous, types, regions, post, factors, e_out, o_out, flags
):
    def body(where):
        values = load(pops, where)
        lin = linearise(values, porous[where], types[where], regions[where])
        store(post, where, collide(values, lin))
        store(factors, where, porosity_factors(lin))

    chunks(range(porous.shape[0]), porous.shape, body)
    flags[...] = jnp.where(types[...] != 1, 1.0, 0.0)
    own = {POST: post, ADJ: seed, FACTOR: factors, FLAG: flags}
    pack_axial(FIRST, own, parity_ref[0], e_out, o_out)


def forward_kernel(t_near, t, corners):
    for block in range(FIRST.corner_blocks):
        corners[block] = t_near[block]
    block, i = FIRST.place[(LO, "own")]
    corners[block, i : i + 1, :] = t[block, i : i + 1, :]


def second_kernel(
    parity_ref, post, seed, factors, flags, porous, types, regions, e, o, t, ec, oc,
    post_next, adj, sens, around, e_out, o_out, t_out, partial, state, back, parts,
):
    own = {POST: post, ADJ: seed, FACTOR: factors, FLAG: flags}
    fields = Fields(FIRST, own, parity_ref[0], e, o, t, ec, oc)
    rows_a, rows_t, rows_r = porous.shape
    for a in range(rows_a):
        centre = flags[a]
        state[0, a] = post[0, a]
        back[0, a] = seed[0, a]
        for q in range(1, 19):
            behind = tuple(-c for c in VELOCITY[q])
            open_ = fields.moved(FLAG, 0, a, behind)
            around[q - 1, a] = open_
            opp = OPPOSITE[q]
            state[q, a] = jnp.where(open_ > 0, fields.moved(POST, q, a, behind), post[opp, a])
            back[opp, a] = centre * fields.moved(ADJ, opp, a, behind) + (1.0 - open_) * seed[q, a]

    def body(where):
        values = load(state, where)
        lin = linearise(values, porous[where], types[where], regions[where])
        store(post_next, where, collide(values, lin))
        result, partial_sens = pull_back(load(back, where), values, lin)
        store(adj, where, result)
        sens[where] = partial_sens

    chunks(range(rows_a), porous.shape, body)
    pack_axial(SECOND, {POST: post_next, ADJ: adj}, parity_ref[0], e_out, o_out)
    pack_azimuthal(SECOND, {POST: post_next, ADJ: adj}, t_out)
    sums = {(i, st): [] for i in (-1, 0, 1) for st in (-1, 0, 1)}
    for a in range(rows_a):
        sums[(0, 0)] += [sens[a], factors[0, a] * adj[0, a]]
        for q in range(1, 19):
            behind = tuple(-c for c in VELOCITY[q])
            open_, value = around[q - 1, a], adj[q, a]
            sums[(0, 0)].append(jnp.where(open_ > 0, 0.0, factors[OPPOSITE[q], a]) * value)
            term = jnp.where(open_ > 0, fields.moved(FACTOR, q, a, behind), 0.0) * value
            from_a = a + behind[0]
            beyond = -1 if from_a < 0 else 1 if from_a >= rows_a else 0
            sums[(beyond, behind[1])].append(term)
    at_t = lax.broadcasted_iota(jnp.int32, (rows_t, rows_r), 0)
    rows = []
    for beyond in (-1, 0, 1):
        low, centre, high = (functools.reduce(jnp.add, sums[(beyond, st)]) for st in (-1, 0, 1))
        inner = centre + jnp.where(at_t == 0, 0.0, low) + jnp.where(at_t == rows_t - 1, 0.0, high)
        a = {-1: -1, 0: 0, 1: rows_a}[beyond]
        label = fields.message((LO, "own"), a) if beyond else label_of(regions, rows_r)
        rows.append((jnp.sum(inner, axis=0, keepdims=True), label))
        rows.append((high[rows_t - 1 : rows_t], fields.message((LO, "label"), a)))
        rows.append((low[0:1], fields.message((HI, "label"), a)))
    parts[...] = jnp.zeros_like(parts)
    for i, (value, label) in enumerate(rows):
        parts[0, i : i + 1, :] = value
        parts[1, i : i + 1, :] = label
    lanes = lax.broadcasted_iota(jnp.int32, parts.shape[1:], 1) + 1
    total = jnp.sum(parts[0], axis=1, keepdims=True)
    chosen = jnp.where(lanes == parts[1].astype(jnp.int32), total, 0.0)
    partial[...] = jnp.sum(chosen, axis=0, keepdims=True)


def corner_kernel(e, o, t, total, e_out, o_out):
    slot, (row, i) = SECOND.fields, SECOND.place[(LO, "sum")]
    for out in (e_out, o_out):
        for block in range(SECOND.corner_blocks):
            out[slot, 8 * block : 8 * block + 8, :] = t[block]
        out[slot, 8 * row + i : 8 * row + i + 1, :] = total[...]


def third_kernel(
    parity_ref, post, adj, flags, around, pops, porous, types, regions, sens_one, e, o, t,
    final_hbm, result_hbm, sens, final, result, back, sems,
):
    fields = Fields(SECOND, {POST: post, ADJ: adj}, parity_ref[0], e, o, t)
    rows_a = porous.shape[0]
    stores = []
    for a in range(rows_a):
        final[0, a] = post[0, a]
        for q in range(1, 19):
            behind = tuple(-c for c in VELOCITY[q])
            moved = fields.moved(POST, q, a, behind)
            final[q, a] = jnp.where(around[q - 1, a] > 0, moved, post[OPPOSITE[q], a])
        stores.append(pltpu.make_async_copy(final.at[:, a], final_hbm.at[:, a], sems.at[a]))
        stores[-1].start()

    def body(where):
        values = load(pops, where)
        lin = linearise(values, porous[where], types[where], regions[where])
        adjoint, partial_sens = pull_back(load(back, where), values, lin)
        store(result, where, adjoint)
        sens[where] = partial_sens + sens_one[where]

    for a in range(rows_a):
        centre = flags[a]
        back[0, a] = adj[0, a]
        for q in range(1, 19):
            behind = tuple(-c for c in VELOCITY[q])
            opp = OPPOSITE[q]
            ahead = centre * fields.moved(ADJ, opp, a, behind)
            back[opp, a] = ahead + (1.0 - around[q - 1, a]) * adj[q, a]
        chunks([a], porous.shape, body)
        stores.append(pltpu.make_async_copy(result.at[:, a], result_hbm.at[:, a], sems.at[rows_a + a]))
        stores[-1].start()
    for copy in stores:
        copy.wait()


VMEM, HBM = pltpu.VMEM, pltpu.HBM


def call(body, in_spaces, outs, scratch, *arrays, aliases=None, cost=None):
    return pl.pallas_call(
        body,
        out_shape=[jax.ShapeDtypeStruct(shape, dtype) for shape, dtype, _ in outs],
        in_specs=[pl.BlockSpec(memory_space=space) for space in in_spaces],
        out_specs=[pl.BlockSpec(memory_space=space) for _, _, space in outs],
        scratch_shapes=scratch,
        input_output_aliases=aliases or {},
        cost_estimate=cost,
        compiler_params=pltpu.CompilerParams(vmem_limit_bytes=16 * 1024 * 1024),
    )(*arrays)


def even_pairs(size):
    return [(i, i ^ 1) for i in range(size) if i ^ 1 < size]


def odd_pairs(size):
    return [(i, ((i + 1) ^ 1) - 1) for i in range(size) if 0 <= ((i + 1) ^ 1) - 1 < size]


def send_azimuthal(layout, message):
    size = lax.axis_size("az")
    ring = [(i, (i + 1) % size) for i in range(size)]
    t = lax.ppermute(message, "az", ring)
    if size > 2:
        from_high = np.zeros((layout.blocks, 8, 1), bool)
        for key, (block, i) in layout.place.items():
            from_high[block, i] = key[0] == HI
        t_down = lax.ppermute(message, "az", [(j, i) for i, j in ring])
        t = jnp.where(jnp.asarray(from_high), t, t_down)
    return t


def send_axial(e_message, o_message):
    size = lax.axis_size("ax")
    e = lax.ppermute(e_message, "ax", even_pairs(size))
    return e, lax.ppermute(o_message, "ax", odd_pairs(size))


def sum_over(x, axis, step, last_after=None):
    size = lax.axis_size(axis)
    if size & (size - 1):
        return lax.psum(x, axis)
    while step < size:
        if last_after is not None and 2 * step == size:
            x, _ = lax.optimization_barrier((x, last_after))
        x = x + lax.ppermute(x, axis, [(i, i ^ step) for i in range(size)])
        step *= 2
    return x


def shards(initial, adjoint_seed, porosity, cell_type, region):
    cells_ = porosity.shape
    pops = (19,) + cells_
    wide = cells_[2]
    f32, i32 = jnp.float32, jnp.int32
    size_a, size_t = lax.axis_size("ax"), lax.axis_size("az")
    parity = (lax.axis_index("ax") % 2).astype(i32).reshape(1)

    def axial(fields):
        return [((fields,) + cells_[1:], f32, VMEM)] * 2

    inputs = (initial, adjoint_seed, porosity, cell_type, region)
    *near_inputs, t = call(
        edge_kernel,
        [HBM] * 5,
        [(x.shape, x.dtype, VMEM) for x in inputs] + [((FIRST.blocks, 8, wide), f32, VMEM)],
        [VMEM((20, 8, wide), f32), VMEM((19, 8, wide), f32), VMEM((19, 8, wide), f32)]
        + [pltpu.SemaphoreType.DMA((5,))],
        *(pltpu.with_memory_space_constraint(x, HBM) for x in inputs),
    )
    post, factors, e, o, flags = call(
        first_kernel,
        [pltpu.SMEM] + [VMEM] * 5,
        [(pops, f32, VMEM), (pops, f32, VMEM)] + axial(FIRST.fields) + [(cells_, f32, VMEM)],
        [],
        parity, *near_inputs,
    )
    t_near = send_azimuthal(FIRST, t)
    e, o = send_axial(e, o)
    corners = call(
        forward_kernel,
        [VMEM] * 2,
        [((FIRST.corner_blocks, 8, wide), f32, VMEM)],
        [],
        t_near, t,
        cost=pl.CostEstimate(flops=1 << 30, bytes_accessed=40 << 20, transcendentals=0),
    )[0]
    ec, oc = send_axial(corners, corners)
    post, adj, sens_one, around, e, o, t, total = call(
        second_kernel,
        [pltpu.SMEM] + [VMEM] * 12,
        [(pops, f32, VMEM), (pops, f32, VMEM), (cells_, f32, VMEM), ((18,) + cells_, f32, VMEM)]
        + axial(SECOND.fields + 1)
        + [((SECOND.blocks, 8, wide), f32, VMEM), ((1, wide), f32, VMEM)],
        [VMEM(pops, f32), VMEM(pops, f32), VMEM((2, 16, wide), f32)],
        parity, post, adjoint_seed, factors, flags, porosity, cell_type, region, e, o, t_near, ec, oc,
    )
    t_near = send_azimuthal(SECOND, t)
    halving = size_a % 4 == 0 and size_a & (size_a - 1) == 0
    if halving:
        total = total + lax.ppermute(total, "ax", [(i, i ^ 2) for i in range(size_a)])
    e, o = call(
        corner_kernel,
        [VMEM] * 4,
        axial(SECOND.fields + 1),
        [],
        e, o, t_near, total,
        aliases={0: 0, 1: 1},
    )
    e, o = send_axial(e, o)
    if halving:
        block, i = SECOND.place[(LO, "sum")]
        total = total + e[SECOND.fields, 8 * block + i : 8 * block + i + 1]
        total = sum_over(total, "az", 1)
        totals = sum_over(total, "ax", 4, o)
    else:
        totals = lax.psum(total, ("ax", "az"))
    final, adjoint, sensitivity = call(
        third_kernel,
        [pltpu.SMEM] + [VMEM] * 12,
        [(pops, f32, HBM), (pops, f32, HBM), (cells_, f32, VMEM)],
        [VMEM(pops, f32), VMEM(pops, f32), VMEM(pops, f32)]
        + [pltpu.SemaphoreType.DMA((2 * cells_[0],))],
        parity, post, adj, flags, around, initial, porosity, cell_type, region, sens_one, e, o, t_near,
    )
    return final, adjoint, sensitivity, totals[0, : size_a * size_t // 4]


def solution(mesh):
    return jax.shard_map(
        shards,
        mesh=mesh,
        in_specs=(
            P(None, "ax", "az", None),
            P(None, "ax", "az", None),
            P("ax", "az", None),
            P("ax", "az", None),
            P("ax", "az", None),
        ),
        out_specs=(P(None, "ax", "az", None), P(None, "ax", "az", None), P("ax", "az", None), P()),
        check_vma=False,
    )
```

```python
import functools

import jax
import jax.numpy as jnp
import numpy as np
from jax import lax
from jax.experimental import pallas as pl
from jax.experimental.pallas import tpu as pltpu
from jax.sharding import PartitionSpec as P

VELOCITY = [
    (0, 0, 0),
    (1, 0, 0),
    (-1, 0, 0),
    (0, 1, 0),
    (0, -1, 0),
    (0, 0, 1),
    (0, 0, -1),
    (1, 1, 0),
    (-1, -1, 0),
    (1, -1, 0),
    (-1, 1, 0),
    (1, 0, 1),
    (-1, 0, -1),
    (1, 0, -1),
    (-1, 0, 1),
    (0, 1, 1),
    (0, -1, -1),
    (0, 1, -1),
    (0, -1, 1),
]
OPPOSITE = [0, 2, 1, 4, 3, 6, 5, 8, 7, 10, 9, 12, 11, 14, 13, 16, 15, 18, 17]
INLET_SPEED = (0.05, 0.05, 0.0)
W_AXIS = 1.0 / 18.0
W_EDGE = 1.0 / 36.0


def moving(axis, sign):
    return [q for q in range(19) if VELOCITY[q][axis] == sign]


LO, HI = 0, 1
POST, ADJ, FACTOR, FLAG, MOTION = 0, 1, 2, 3, 4


def face_fields(kinds, axis, side):
    sign = -1 if side == LO else 1
    fields = []
    for kind in kinds:
        if kind == FLAG:
            fields.append((FLAG, 0))
        elif kind == FACTOR and axis == 0:
            fields += [(MOTION, k) for k in range(4)]
        else:
            fields += [(kind, q) for q in moving(axis, -sign if kind == ADJ else sign)]
    return fields


class Layout:
    def __init__(self, kinds, extra, least_blocks=0):
        self.ax = [face_fields(kinds, 0, side) for side in (LO, HI)]
        self.slot = [{key: i for i, key in enumerate(fields)} for fields in self.ax]
        self.fields = len(self.ax[LO])
        corner, rest = [], []
        for a, sign in ((1, 1), (0, -1)):
            for side in (LO, HI):
                for kind, q in face_fields(kinds, 1, side):
                    leaves = VELOCITY[q][0] == (-sign if kind == ADJ else sign)
                    key = (side, kind, q, a)
                    (corner if kind == FLAG or leaves else rest).append(key)
        corner += extra
        self.corner_blocks = -(-len(corner) // 8)
        self.blocks = max(self.corner_blocks + -(-len(rest) // 8), least_blocks)
        self.place = {key: (i // 8, i % 8) for i, key in enumerate(corner)}
        self.place.update({key: (self.corner_blocks + i // 8, i % 8) for i, key in enumerate(rest)})


FIRST = Layout((POST, ADJ, FACTOR, FLAG), [(LO, "label"), (HI, "label"), (LO, "own")], 18)
SECOND = Layout((POST, ADJ), [(LO, "sum")])


def pairs_of(values):
    sums = [values[q] + values[q + 1] for q in range(1, 19, 2)]
    diffs = [values[q] - values[q + 1] for q in range(1, 19, 2)]
    return sums, diffs


def projections(vec):
    va, vt, vr = vec
    return [va, vt, vr, va + vt, va - vt, va + vr, va - vr, vt + vr, vt - vr]


def linearise(pops, porous, types, regions):
    sums, diffs = pairs_of(pops)
    s0, s1, s2, s3, s4, s5, s6, s7, s8 = sums
    d0, d1, d2, d3, d4, d5, d6, d7, d8 = diffs
    at, ar, tr = s3 + s4, s5 + s6, s7 + s8
    rho = pops[0] + ((s0 + s1) + (s2 + at)) + (ar + tr)
    ma = (d0 + (d3 + d4)) + (d5 + d6)
    mt = (d1 + (d3 - d4)) + (d7 + d8)
    mr = (d2 + (d5 - d6)) + (d7 - d8)
    inv = 1.0 / rho
    ua, ut, ur = ma * inv, mt * inv, mr * inv
    third = rho * (1.0 / 3.0)
    paa = (s0 + at + ar - third) - ma * ua
    ptt = (s1 + at + tr - third) - mt * ut
    prr = (s2 + ar + tr - third) - mr * ur
    pat = (s3 - s4) - ma * ut
    par = (s5 - s6) - ma * ur
    ptr = (s7 - s8) - mt * ur
    square = (paa * paa + ptt * ptt + prr * prr) + 2.0 * (pat * pat + par * par + ptr * ptr) + 0.0001
    inv_root = lax.rsqrt(square)
    shear = 1.5 * (square * inv_root) * inv
    shifted = shear + 0.01
    viscous = 0.02 * jnp.exp((0.7 - 1.0) * jnp.log(shifted))
    omega = 1.0 / (0.5 + 3.0 * viscous)
    relaxed = (types != 2) & (types != 3)
    kappa = jnp.where(regions > 0, porous, 0.0)
    return dict(
        rho=rho,
        inv=inv,
        u=(ua, ut, ur),
        p=(paa, ptt, prr, pat, par, ptr),
        inv_root=inv_root,
        shear=shear,
        shifted=shifted,
        viscous=viscous,
        omega=omega,
        relaxed=relaxed,
        kappa=kappa,
        keep=jnp.where(relaxed, 1.0 - omega, 0.0),
        design=jnp.where(relaxed & (regions > 0), 1.0, 0.0),
        inlet=types == 2,
        outlet=types == 3,
    )


def collide(pops, lin):
    rho, relaxed, inlet = lin["rho"], lin["relaxed"], lin["inlet"]
    ua, ut, ur = (jnp.where(inlet, speed, x) for x, speed in zip(lin["u"], INLET_SPEED))
    scale = jnp.where(relaxed, (lin["omega"] - lin["kappa"]) * rho, 1.0)
    rest = jnp.where(relaxed, lin["kappa"] * rho, 0.0)
    keep = lin["keep"]
    still = 1.0 - 1.5 * (ua * ua + ut * ut + ur * ur)
    post = [keep * pops[0] + (1.0 / 3.0) * (scale * still + rest)]
    for i, cu in enumerate(projections((ua, ut, ur))):
        weight = W_AXIS if i < 3 else W_EDGE
        even = weight * (scale * (still + 4.5 * cu * cu) + rest)
        odd = (3.0 * weight) * (scale * cu)
        post.append(keep * pops[1 + 2 * i] + (even + odd))
        post.append(keep * pops[2 + 2 * i] + (even - odd))
    return post


def pull_back(back, pops, lin):
    sums, diffs = pairs_of(back)
    s0, s1, s2, s3, s4, s5, s6, s7, s8 = sums
    d0, d1, d2, d3, d4, d5, d6, d7, d8 = diffs
    at, ar, tr = s3 + s4, s5 + s6, s7 + s8
    b0 = (1.0 / 3.0) * back[0] + W_AXIS * (s0 + s1 + s2) + W_EDGE * (at + ar + tr)
    ba = W_AXIS * d0 + W_EDGE * ((d3 + d4) + (d5 + d6))
    bt = W_AXIS * d1 + W_EDGE * ((d3 - d4) + (d7 + d8))
    br = W_AXIS * d2 + W_EDGE * ((d5 - d6) + (d7 - d8))
    baa = W_AXIS * s0 + W_EDGE * (at + ar)
    btt = W_AXIS * s1 + W_EDGE * (at + tr)
    brr = W_AXIS * s2 + W_EDGE * (ar + tr)
    bat, bar, btr = W_EDGE * (s3 - s4), W_EDGE * (s5 - s6), W_EDGE * (s7 - s8)
    along = back[0] * pops[0]
    for q in range(1, 19):
        along = along + back[q] * pops[q]
    rho, inv = lin["rho"], lin["inv"]
    ua, ut, ur = lin["u"]
    qa = baa * ua + bat * ut + bar * ur
    qt = bat * ua + btt * ut + btr * ur
    qr = bar * ua + btr * ut + brr * ur
    uu = ua * ua + ut * ut + ur * ur
    slope = 3.0 * (ua * ba + ut * bt + ur * br) + 4.5 * (ua * qa + ut * qt + ur * qr) - 1.5 * (uu * b0)
    full = b0 + slope
    sens = -(lin["design"] * (rho * slope))
    relaxed, omega = lin["relaxed"], lin["omega"]
    shear_bar = (rho * full - along) * (omega * omega) * (0.9 * lin["viscous"]) / lin["shifted"]
    shear_bar = jnp.where(relaxed, shear_bar, 0.0)
    z = shear_bar * (1.5 * inv) * lin["inv_root"]
    maa, mtt, mrr, mat, mar, mtr = (z * x for x in lin["p"])
    scale = jnp.where(relaxed, omega - lin["kappa"], jnp.where(lin["outlet"], inv, 0.0))
    la = maa * ua + mat * ut + mar * ur
    lt = mat * ua + mtt * ut + mtr * ur
    lr = mar * ua + mtr * ut + mrr * ur
    va = scale * (3.0 * (ba - b0 * ua) + 9.0 * qa) - 2.0 * la
    vt = scale * (3.0 * (bt - b0 * ut) + 9.0 * qt) - 2.0 * lt
    vr = scale * (3.0 * (br - b0 * ur) + 9.0 * qr) - 2.0 * lr
    total = jnp.where(relaxed, lin["kappa"] * b0 + scale * full, 0.0)
    total = total - shear_bar * lin["shear"] * inv - (1.0 / 3.0) * (maa + mtt + mrr)
    total = total - ((la + va) * ua + (lt + vt) * ut + (lr + vr) * ur)
    keep = lin["keep"]
    taa, ttt, trr = total + maa, total + mtt, total + mrr
    sat, sar, str_ = taa + mtt, taa + mrr, ttt + mrr
    mat2, mar2, mtr2 = 2.0 * mat, 2.0 * mar, 2.0 * mtr
    evens = [taa, ttt, trr, sat + mat2, sat - mat2, sar + mar2, sar - mar2, str_ + mtr2, str_ - mtr2]
    result = [keep * back[0] + total]
    for i, odd in enumerate(projections((va, vt, vr))):
        result.append(keep * back[1 + 2 * i] + (evens[i] + odd))
        result.append(keep * back[2 + 2 * i] + (evens[i] - odd))
    return result, sens


class Fields:
    def __init__(self, layout, own, parity, real, e, o, t, ec=None, oc=None):
        self.layout, self.own = layout, own
        self.e, self.o, self.t, self.ec, self.oc = e, o, t, ec, oc
        self.up_e = parity == 0
        self.o_real = real == 1
        self.rows_a = own[POST].shape[1]

    def row(self, kind, q, a):
        if 0 <= a < self.rows_a:
            return self.own[FLAG][a] if kind == FLAG else self.own[kind][q, a]
        if kind == FACTOR:
            weight, *velocity = (self.row(MOTION, k, a) for k in range(4))
            return porosity_factor(q, weight, velocity)
        slot = self.layout.slot[HI if a < 0 else LO][(kind, q)]
        return self.beyond(kind, a, self.e[slot], self.o[slot])

    def beyond(self, kind, a, e, o):
        if kind in (ADJ, FLAG):
            o = jnp.where(self.o_real, o, 0.0)
        return jnp.where(self.up_e, o, e) if a < 0 else jnp.where(self.up_e, e, o)

    def message(self, key, a):
        block, i = self.layout.place[key]
        rows = (block, slice(i, i + 1))
        if 0 <= a < self.rows_a:
            return self.t[rows]
        if self.ec is None:
            rows = (self.layout.fields, slice(8 * block + i, 8 * block + i + 1))
            e, o = self.e[rows], self.o[rows]
        else:
            e, o = self.ec[rows], self.oc[rows]
        return self.beyond(key[1], a, e, o)

    def edge(self, side, kind, q, a):
        row = self.rows_a - 1 if a < 0 else 0 if a >= self.rows_a else a
        return self.message((side, kind, q, row), a)

    def moved(self, kind, q, a, shift):
        sa, st, sr = shift
        value = self.row(kind, q, a + sa)
        rows_t, rows_r = value.shape
        if st:
            value = pltpu.roll(value, (-st) % rows_t, 0)
            beyond = self.edge(LO if st > 0 else HI, kind, q, a + sa)
            at_edge = lax.broadcasted_iota(jnp.int32, value.shape, 0) == (rows_t - 1 if st > 0 else 0)
            value = jnp.where(at_edge, beyond, value)
        if sr:
            value = pltpu.roll(value, (-sr) % rows_r, 1)
        return value


def cells(own, kind, q, a):
    return own[FLAG].at[a] if kind == FLAG else own[kind].at[q, a]


def pack_azimuthal(layout, own, t_ref):
    rows_t = own[POST].shape[2]
    for key, (block, i) in layout.place.items():
        if len(key) == 4:
            side, kind, q, a = key
            t = 0 if side == LO else rows_t - 1
            t_ref[block, i : i + 1, :] = cells(own, kind, q, a)[t : t + 1, :]


def pack_axial(layout, own, parity, e_ref, o_ref):
    rows_a = own[POST].shape[1]
    even = parity == 0
    for slot in range(layout.fields):
        low = cells(own, *layout.ax[LO][slot], 0)[...]
        high = cells(own, *layout.ax[HI][slot], rows_a - 1)[...]
        e_ref[slot] = jnp.where(even, high, low)
        o_ref[slot] = jnp.where(even, low, high)


def chunks(rows_a, shape, body):
    counts = (len(rows_a), shape[1] // 8, shape[2] // 128)

    def step(i, carry):
        a = rows_a[0] + i // (counts[1] * counts[2])
        t = pl.multiple_of((i // counts[2]) % counts[1] * 8, 8)
        r = pl.multiple_of(i % counts[2] * 128, 128)
        body((a, pl.ds(t, 8), pl.ds(r, 128)))
        return carry

    lax.fori_loop(0, counts[0] * counts[1] * counts[2], step, 0)


def load(ref, where):
    return [ref[(q,) + where] for q in range(19)]


def store(ref, where, values):
    for q in range(19):
        ref[(q,) + where] = values[q]


def label_of(regions, wide):
    label = jnp.max(jnp.max(regions[...], axis=0), axis=(0, 1), keepdims=True)
    return jnp.broadcast_to(label.astype(jnp.float32), (1, wide))


def porosity_factor(q, weight, velocity):
    ua, ut, ur = velocity
    pair = (q - 1) // 2
    cu = projections(velocity)[pair]
    scaled = (W_AXIS if pair < 3 else W_EDGE) * weight
    still = -1.5 * (ua * ua + ut * ut + ur * ur)
    return scaled * (still + 4.5 * cu * cu + (3.0 * cu if q % 2 else -3.0 * cu))


def factor_weight(lin):
    return -(lin["design"] * lin["rho"])


def porosity_factors(lin):
    ua, ut, ur = lin["u"]
    weight = factor_weight(lin)
    still = -1.5 * (ua * ua + ut * ut + ur * ur)
    result = [(1.0 / 3.0) * weight * still]
    for i, cu in enumerate(projections((ua, ut, ur))):
        scaled = (W_AXIS if i < 3 else W_EDGE) * weight
        even, odd = scaled * (still + 4.5 * cu * cu), 3.0 * scaled * cu
        result += [even + odd, even - odd]
    return result


def edge_kernel(
    pops_hbm, seed_hbm, porous_hbm, types_hbm, regions_hbm,
    pops, seed, porous, types, regions, t_out, edge, edge_post, edge_factors, sems,
):
    rows_a, rows_t, rows_r = porous.shape
    pairs = [(types_hbm, types), (regions_hbm, regions), (porous_hbm, porous)]
    pairs += [(pops_hbm, pops), (seed_hbm, seed)]
    loads = [pltpu.make_async_copy(*pair, sems.at[i]) for i, pair in enumerate(pairs)]
    for copy in loads:
        copy.start()
    for copy in loads[:3]:
        copy.wait()
    label = label_of(regions, rows_r)
    for key in ((LO, "label"), (HI, "label"), (LO, "own")):
        block, i = FIRST.place[key]
        t_out[block, i : i + 1, :] = label
    columns = [(a, t) for a in range(rows_a) for t in (0, rows_t - 1)]

    def gather(source, target):
        for i, (a, t) in enumerate(columns):
            target[i : i + 1, :] = source[a, t : t + 1, :]

    gather(porous, edge.at[19])
    gather_types = jnp.concatenate([types[a, t : t + 1, :] for a, t in columns] * 2)
    gather_regions = jnp.concatenate([regions[a, t : t + 1, :] for a, t in columns] * 2)
    for i in range(len(columns), edge.shape[1]):
        edge[:, i, :] = jnp.ones((edge.shape[0], rows_r), jnp.float32)
    loads[3].wait()
    for q in range(19):
        gather(pops.at[q], edge.at[q])
    values = [edge[q] for q in range(19)]
    lin = linearise(values, edge[19], gather_types, gather_regions)
    post = collide(values, lin)
    factors = porosity_factors(lin)
    for q in range(19):
        edge_post[q] = post[q]
        edge_factors[q] = factors[q]
    edge[0] = jnp.where(gather_types != 1, 1.0, 0.0)
    loads[4].wait()
    for key, (block, i) in FIRST.place.items():
        if len(key) == 4:
            side, kind, q, a = key
            t = 0 if side == LO else rows_t - 1
            k = columns.index((a, t))
            if kind == ADJ:
                row = seed[q, a, t : t + 1, :]
            elif kind == FLAG:
                row = edge[0, k : k + 1, :]
            else:
                row = (edge_post if kind == POST else edge_factors)[q, k : k + 1, :]
            t_out[block, i : i + 1, :] = row


def first_kernel(
    parity_ref, real_ref, pops, seed, porous, types, regions, post, factors, e_out, o_out, flags, motion
):
    def body(where):
        values = load(pops, where)
        lin = linearise(values, porous[where], types[where], regions[where])
        store(post, where, collide(values, lin))
        store(factors, where, porosity_factors(lin))
        for k, value in enumerate([factor_weight(lin), *lin["u"]]):
            motion[(k,) + where] = value

    chunks(range(porous.shape[0]), porous.shape, body)
    flags[...] = jnp.where(types[...] != 1, 1.0, 0.0)
    own = {POST: post, ADJ: seed, MOTION: motion, FLAG: flags}
    pack_axial(FIRST, own, parity_ref[0], e_out, o_out)


def forward_kernel(t_near, t, corners):
    for block in range(FIRST.corner_blocks):
        corners[block] = t_near[block]
    block, i = FIRST.place[(LO, "own")]
    corners[block, i : i + 1, :] = t[block, i : i + 1, :]


def second_kernel(
    parity_ref, real_ref, post, seed, factors, flags, porous, types, regions, e, o, t, ec, oc,
    post_next, adj, sens, around, e_out, o_out, t_out, partial, state, back, parts,
):
    own = {POST: post, ADJ: seed, FACTOR: factors, FLAG: flags}
    fields = Fields(FIRST, own, parity_ref[0], real_ref[0], e, o, t, ec, oc)
    rows_a, rows_t, rows_r = porous.shape
    for a in range(rows_a):
        centre = flags[a]
        state[0, a] = post[0, a]
        back[0, a] = seed[0, a]
        for q in range(1, 19):
            behind = tuple(-c for c in VELOCITY[q])
            open_ = fields.moved(FLAG, 0, a, behind)
            around[q - 1, a] = open_
            opp = OPPOSITE[q]
            state[q, a] = jnp.where(open_ > 0, fields.moved(POST, q, a, behind), post[opp, a])
            back[opp, a] = centre * fields.moved(ADJ, opp, a, behind) + (1.0 - open_) * seed[q, a]

    def body(where):
        values = load(state, where)
        lin = linearise(values, porous[where], types[where], regions[where])
        store(post_next, where, collide(values, lin))
        result, partial_sens = pull_back(load(back, where), values, lin)
        store(adj, where, result)
        sens[where] = partial_sens

    chunks(range(rows_a), porous.shape, body)
    pack_axial(SECOND, {POST: post_next, ADJ: adj}, parity_ref[0], e_out, o_out)
    pack_azimuthal(SECOND, {POST: post_next, ADJ: adj}, t_out)
    sums = {(i, st): [] for i in (-1, 0, 1) for st in (-1, 0, 1)}
    for a in range(rows_a):
        sums[(0, 0)] += [sens[a], factors[0, a] * adj[0, a]]
        for q in range(1, 19):
            behind = tuple(-c for c in VELOCITY[q])
            open_, value = around[q - 1, a], adj[q, a]
            sums[(0, 0)].append(jnp.where(open_ > 0, 0.0, factors[OPPOSITE[q], a]) * value)
            term = jnp.where(open_ > 0, fields.moved(FACTOR, q, a, behind), 0.0) * value
            from_a = a + behind[0]
            beyond = -1 if from_a < 0 else 1 if from_a >= rows_a else 0
            sums[(beyond, behind[1])].append(term)
    at_t = lax.broadcasted_iota(jnp.int32, (rows_t, rows_r), 0)
    rows = []
    for beyond in (-1, 0, 1):
        low, centre, high = (functools.reduce(jnp.add, sums[(beyond, st)]) for st in (-1, 0, 1))
        inner = centre + jnp.where(at_t == 0, 0.0, low) + jnp.where(at_t == rows_t - 1, 0.0, high)
        a = {-1: -1, 0: 0, 1: rows_a}[beyond]
        label = fields.message((LO, "own"), a) if beyond else label_of(regions, rows_r)
        rows.append((jnp.sum(inner, axis=0, keepdims=True), label))
        rows.append((high[rows_t - 1 : rows_t], fields.message((LO, "label"), a)))
        rows.append((low[0:1], fields.message((HI, "label"), a)))
    parts[...] = jnp.zeros_like(parts)
    for i, (value, label) in enumerate(rows):
        parts[0, i : i + 1, :] = value
        parts[1, i : i + 1, :] = label
    lanes = lax.broadcasted_iota(jnp.int32, parts.shape[1:], 1) + 1
    total = jnp.sum(parts[0], axis=1, keepdims=True)
    chosen = jnp.where(lanes == parts[1].astype(jnp.int32), total, 0.0)
    partial[...] = jnp.sum(chosen, axis=0, keepdims=True)


def corner_kernel(e, o, t, total, e_out, o_out):
    slot, (row, i) = SECOND.fields, SECOND.place[(LO, "sum")]
    for out in (e_out, o_out):
        for block in range(SECOND.corner_blocks):
            out[slot, 8 * block : 8 * block + 8, :] = t[block]
        out[slot, 8 * row + i : 8 * row + i + 1, :] = total[...]


def third_kernel(
    parity_ref, real_ref, post, adj, flags, around, pops, porous, types, regions, sens_one, e, o, t,
    final_hbm, result_hbm, sens, final, result, back, sems,
):
    fields = Fields(SECOND, {POST: post, ADJ: adj}, parity_ref[0], real_ref[0], e, o, t)
    rows_a = porous.shape[0]
    stores = []
    for a in range(rows_a):
        final[0, a] = post[0, a]
        for q in range(1, 19):
            behind = tuple(-c for c in VELOCITY[q])
            moved = fields.moved(POST, q, a, behind)
            final[q, a] = jnp.where(around[q - 1, a] > 0, moved, post[OPPOSITE[q], a])
        stores.append(pltpu.make_async_copy(final.at[:, a], final_hbm.at[:, a], sems.at[a]))
        stores[-1].start()

    def body(where):
        values = load(pops, where)
        lin = linearise(values, porous[where], types[where], regions[where])
        adjoint, partial_sens = pull_back(load(back, where), values, lin)
        store(result, where, adjoint)
        sens[where] = partial_sens + sens_one[where]

    for a in range(rows_a):
        centre = flags[a]
        back[0, a] = adj[0, a]
        for q in range(1, 19):
            behind = tuple(-c for c in VELOCITY[q])
            opp = OPPOSITE[q]
            ahead = centre * fields.moved(ADJ, opp, a, behind)
            back[opp, a] = ahead + (1.0 - around[q - 1, a]) * adj[q, a]
        chunks([a], porous.shape, body)
        stores.append(pltpu.make_async_copy(result.at[:, a], result_hbm.at[:, a], sems.at[rows_a + a]))
        stores[-1].start()
    for copy in stores:
        copy.wait()


VMEM, HBM = pltpu.VMEM, pltpu.HBM


def call(body, in_spaces, outs, scratch, *arrays, aliases=None, cost=None):
    return pl.pallas_call(
        body,
        out_shape=[jax.ShapeDtypeStruct(shape, dtype) for shape, dtype, _ in outs],
        in_specs=[pl.BlockSpec(memory_space=space) for space in in_spaces],
        out_specs=[pl.BlockSpec(memory_space=space) for _, _, space in outs],
        scratch_shapes=scratch,
        input_output_aliases=aliases or {},
        cost_estimate=cost,
        compiler_params=pltpu.CompilerParams(vmem_limit_bytes=16 * 1024 * 1024),
    )(*arrays)


def axial_pairs(flip):
    size_a, size_t = lax.axis_size("ax"), lax.axis_size("az")
    pairs = []
    for a in range(size_a):
        partner = ((a + flip) ^ 1) - flip
        for t in range(size_t):
            if 0 <= partner < size_a:
                pairs.append((a * size_t + t, partner * size_t + t))
            elif size_t % 2 == 0:
                pairs.append((a * size_t + t, a * size_t + (t ^ 1)))
    return pairs


def send_azimuthal(layout, message):
    size = lax.axis_size("az")
    ring = [(i, (i + 1) % size) for i in range(size)]
    t = lax.ppermute(message, "az", ring)
    if size > 2:
        from_high = np.zeros((layout.blocks, 8, 1), bool)
        for key, (block, i) in layout.place.items():
            from_high[block, i] = key[0] == HI
        t_down = lax.ppermute(message, "az", [(j, i) for i, j in ring])
        t = jnp.where(jnp.asarray(from_high), t, t_down)
    return t


def send_axial(e_message, o_message):
    e = lax.ppermute(e_message, ("ax", "az"), axial_pairs(0))
    return e, lax.ppermute(o_message, ("ax", "az"), axial_pairs(1))


def add_partner(x, flip_a, flip_t=0):
    size_a, size_t = lax.axis_size("ax"), lax.axis_size("az")
    pairs = [
        (a * size_t + t, (a ^ flip_a) * size_t + (t ^ flip_t))
        for a in range(size_a)
        for t in range(size_t)
    ]
    return x + lax.ppermute(x, ("ax", "az"), pairs)


def shards(initial, adjoint_seed, porosity, cell_type, region):
    cells_ = porosity.shape
    pops = (19,) + cells_
    wide = cells_[2]
    f32, i32 = jnp.float32, jnp.int32
    size_a, size_t = lax.axis_size("ax"), lax.axis_size("az")
    index = lax.axis_index("ax")
    real = (index != 0) & (index != size_a - 1)
    place = ((index % 2).astype(i32).reshape(1), real.astype(i32).reshape(1))

    def axial(fields):
        return [((fields,) + cells_[1:], f32, VMEM)] * 2

    inputs = (initial, adjoint_seed, porosity, cell_type, region)
    *near_inputs, t = call(
        edge_kernel,
        [HBM] * 5,
        [(x.shape, x.dtype, VMEM) for x in inputs] + [((FIRST.blocks, 8, wide), f32, VMEM)],
        [VMEM((20, 8, wide), f32), VMEM((19, 8, wide), f32), VMEM((19, 8, wide), f32)]
        + [pltpu.SemaphoreType.DMA((5,))],
        *(pltpu.with_memory_space_constraint(x, HBM) for x in inputs),
    )
    post, factors, e, o, flags = call(
        first_kernel,
        [pltpu.SMEM] * 2 + [VMEM] * 5,
        [(pops, f32, VMEM), (pops, f32, VMEM)] + axial(FIRST.fields) + [(cells_, f32, VMEM)],
        [VMEM((4,) + cells_, f32)],
        *place, *near_inputs,
    )
    t_near = send_azimuthal(FIRST, t)
    e, o = send_axial(e, o)
    corners = call(
        forward_kernel,
        [VMEM] * 2,
        [((FIRST.corner_blocks, 8, wide), f32, VMEM)],
        [],
        t_near, t,
        cost=pl.CostEstimate(flops=1 << 30, bytes_accessed=40 << 20, transcendentals=0),
    )[0]
    ec, oc = send_axial(corners, corners)
    post, adj, sens_one, around, e, o, t, total = call(
        second_kernel,
        [pltpu.SMEM] * 2 + [VMEM] * 12,
        [(pops, f32, VMEM), (pops, f32, VMEM), (cells_, f32, VMEM), ((18,) + cells_, f32, VMEM)]
        + axial(SECOND.fields + 1)
        + [((SECOND.blocks, 8, wide), f32, VMEM), ((1, wide), f32, VMEM)],
        [VMEM(pops, f32), VMEM(pops, f32), VMEM((2, 16, wide), f32)],
        *place, post, adjoint_seed, factors, flags, porosity, cell_type, region, e, o, t_near, ec, oc,
    )
    t_near = send_azimuthal(SECOND, t)
    halving = size_a >= 4 and not (size_a & (size_a - 1) or size_t & (size_t - 1))
    if halving:
        total = add_partner(total, 3)
    e, o = call(
        corner_kernel,
        [VMEM] * 4,
        axial(SECOND.fields + 1),
        [],
        e, o, t_near, total,
        aliases={0: 0, 1: 1},
    )
    e, o = send_axial(e, o)
    if halving:
        block, i = SECOND.place[(LO, "sum")]
        totals = total + e[SECOND.fields, 8 * block + i : 8 * block + i + 1]
        flips = [(1, 1 << k) for k in range(size_t.bit_length() - 1)]
        flips += [((1 << k) | 1, 0) for k in range(2, size_a.bit_length() - 1)]
        for flip in flips:
            if flip == flips[-1]:
                totals, _ = lax.optimization_barrier((totals, o))
            totals = add_partner(totals, *flip)
    else:
        totals = lax.psum(total, ("ax", "az"))
    final, adjoint, sensitivity = call(
        third_kernel,
        [pltpu.SMEM] * 2 + [VMEM] * 12,
        [(pops, f32, HBM), (pops, f32, HBM), (cells_, f32, VMEM)],
        [VMEM(pops, f32), VMEM(pops, f32), VMEM(pops, f32)]
        + [pltpu.SemaphoreType.DMA((2 * cells_[0],))],
        *place, post, adj, flags, around, initial, porosity, cell_type, region, sens_one, e, o, t_near,
    )
    return final, adjoint, sensitivity, totals[0, : size_a * size_t // 4]


def solution(mesh):
    return jax.shard_map(
        shards,
        mesh=mesh,
        in_specs=(
            P(None, "ax", "az", None),
            P(None, "ax", "az", None),
            P("ax", "az", None),
            P("ax", "az", None),
            P("ax", "az", None),
        ),
        out_specs=(P(None, "ax", "az", None), P(None, "ax", "az", None), P("ax", "az", None), P()),
        check_vma=False,
    )
```

```python
import functools

import jax
import jax.numpy as jnp
import numpy as np
from jax import lax
from jax.experimental import pallas as pl
from jax.experimental.pallas import tpu as pltpu
from jax.sharding import PartitionSpec as P

VELOCITY = [
    (0, 0, 0),
    (1, 0, 0),
    (-1, 0, 0),
    (0, 1, 0),
    (0, -1, 0),
    (0, 0, 1),
    (0, 0, -1),
    (1, 1, 0),
    (-1, -1, 0),
    (1, -1, 0),
    (-1, 1, 0),
    (1, 0, 1),
    (-1, 0, -1),
    (1, 0, -1),
    (-1, 0, 1),
    (0, 1, 1),
    (0, -1, -1),
    (0, 1, -1),
    (0, -1, 1),
]
OPPOSITE = [0, 2, 1, 4, 3, 6, 5, 8, 7, 10, 9, 12, 11, 14, 13, 16, 15, 18, 17]
INLET_SPEED = (0.05, 0.05, 0.0)
W_AXIS = 1.0 / 18.0
W_EDGE = 1.0 / 36.0


def moving(axis, sign):
    return [q for q in range(19) if VELOCITY[q][axis] == sign]


LO, HI = 0, 1
POST, ADJ, FACTOR, FLAG, MOTION = 0, 1, 2, 3, 4


def face_fields(kinds, axis, side):
    sign = -1 if side == LO else 1
    fields = []
    for kind in kinds:
        if kind == FLAG:
            fields.append((FLAG, 0))
        elif kind == FACTOR and axis == 0:
            fields += [(MOTION, k) for k in range(4)]
        else:
            fields += [(kind, q) for q in moving(axis, -sign if kind == ADJ else sign)]
    return fields


class Layout:
    def __init__(self, kinds, extra):
        self.ax = [face_fields(kinds, 0, side) for side in (LO, HI)]
        self.slot = [{key: i for i, key in enumerate(fields)} for fields in self.ax]
        self.fields = len(self.ax[LO])
        corner, rest = [], []
        for a, sign in ((1, 1), (0, -1)):
            for side in (LO, HI):
                for kind, q in face_fields(kinds, 1, side):
                    leaves = VELOCITY[q][0] == (-sign if kind == ADJ else sign)
                    key = (side, kind, q, a)
                    (corner if kind == FLAG or leaves else rest).append(key)
        corner += extra
        self.corner_blocks = -(-len(corner) // 8)
        self.blocks = self.corner_blocks + -(-len(rest) // 8)
        self.place = {key: (i // 8, i % 8) for i, key in enumerate(corner)}
        self.place.update({key: (self.corner_blocks + i // 8, i % 8) for i, key in enumerate(rest)})


FIRST = Layout((POST, ADJ, FACTOR, FLAG), [(LO, "label"), (HI, "label")])
SECOND = Layout((POST, ADJ), [(LO, "sum")])


def pairs_of(values):
    sums = [values[q] + values[q + 1] for q in range(1, 19, 2)]
    diffs = [values[q] - values[q + 1] for q in range(1, 19, 2)]
    return sums, diffs


def projections(vec):
    va, vt, vr = vec
    return [va, vt, vr, va + vt, va - vt, va + vr, va - vr, vt + vr, vt - vr]


def linearise(pops, porous, types, regions):
    sums, diffs = pairs_of(pops)
    s0, s1, s2, s3, s4, s5, s6, s7, s8 = sums
    d0, d1, d2, d3, d4, d5, d6, d7, d8 = diffs
    at, ar, tr = s3 + s4, s5 + s6, s7 + s8
    rho = pops[0] + ((s0 + s1) + (s2 + at)) + (ar + tr)
    ma = (d0 + (d3 + d4)) + (d5 + d6)
    mt = (d1 + (d3 - d4)) + (d7 + d8)
    mr = (d2 + (d5 - d6)) + (d7 - d8)
    inv = 1.0 / rho
    ua, ut, ur = ma * inv, mt * inv, mr * inv
    third = rho * (1.0 / 3.0)
    paa = (s0 + at + ar - third) - ma * ua
    ptt = (s1 + at + tr - third) - mt * ut
    prr = (s2 + ar + tr - third) - mr * ur
    pat = (s3 - s4) - ma * ut
    par = (s5 - s6) - ma * ur
    ptr = (s7 - s8) - mt * ur
    square = (paa * paa + ptt * ptt + prr * prr) + 2.0 * (pat * pat + par * par + ptr * ptr) + 0.0001
    inv_root = lax.rsqrt(square)
    shear = 1.5 * (square * inv_root) * inv
    shifted = shear + 0.01
    viscous = 0.02 * jnp.exp((0.7 - 1.0) * jnp.log(shifted))
    omega = 1.0 / (0.5 + 3.0 * viscous)
    relaxed = (types != 2) & (types != 3)
    kappa = jnp.where(regions > 0, porous, 0.0)
    return dict(
        rho=rho,
        inv=inv,
        u=(ua, ut, ur),
        p=(paa, ptt, prr, pat, par, ptr),
        inv_root=inv_root,
        shear=shear,
        shifted=shifted,
        viscous=viscous,
        omega=omega,
        relaxed=relaxed,
        kappa=kappa,
        keep=jnp.where(relaxed, 1.0 - omega, 0.0),
        design=jnp.where(relaxed & (regions > 0), 1.0, 0.0),
        inlet=types == 2,
        outlet=types == 3,
    )


def collide(pops, lin):
    rho, relaxed, inlet = lin["rho"], lin["relaxed"], lin["inlet"]
    ua, ut, ur = (jnp.where(inlet, speed, x) for x, speed in zip(lin["u"], INLET_SPEED))
    scale = jnp.where(relaxed, (lin["omega"] - lin["kappa"]) * rho, 1.0)
    rest = jnp.where(relaxed, lin["kappa"] * rho, 0.0)
    keep = lin["keep"]
    still = 1.0 - 1.5 * (ua * ua + ut * ut + ur * ur)
    post = [keep * pops[0] + (1.0 / 3.0) * (scale * still + rest)]
    for i, cu in enumerate(projections((ua, ut, ur))):
        weight = W_AXIS if i < 3 else W_EDGE
        even = weight * (scale * (still + 4.5 * cu * cu) + rest)
        odd = (3.0 * weight) * (scale * cu)
        post.append(keep * pops[1 + 2 * i] + (even + odd))
        post.append(keep * pops[2 + 2 * i] + (even - odd))
    return post


def pull_back(back, pops, lin):
    sums, diffs = pairs_of(back)
    s0, s1, s2, s3, s4, s5, s6, s7, s8 = sums
    d0, d1, d2, d3, d4, d5, d6, d7, d8 = diffs
    at, ar, tr = s3 + s4, s5 + s6, s7 + s8
    b0 = (1.0 / 3.0) * back[0] + W_AXIS * (s0 + s1 + s2) + W_EDGE * (at + ar + tr)
    ba = W_AXIS * d0 + W_EDGE * ((d3 + d4) + (d5 + d6))
    bt = W_AXIS * d1 + W_EDGE * ((d3 - d4) + (d7 + d8))
    br = W_AXIS * d2 + W_EDGE * ((d5 - d6) + (d7 - d8))
    baa = W_AXIS * s0 + W_EDGE * (at + ar)
    btt = W_AXIS * s1 + W_EDGE * (at + tr)
    brr = W_AXIS * s2 + W_EDGE * (ar + tr)
    bat, bar, btr = W_EDGE * (s3 - s4), W_EDGE * (s5 - s6), W_EDGE * (s7 - s8)
    along = back[0] * pops[0]
    for q in range(1, 19):
        along = along + back[q] * pops[q]
    rho, inv = lin["rho"], lin["inv"]
    ua, ut, ur = lin["u"]
    qa = baa * ua + bat * ut + bar * ur
    qt = bat * ua + btt * ut + btr * ur
    qr = bar * ua + btr * ut + brr * ur
    uu = ua * ua + ut * ut + ur * ur
    slope = 3.0 * (ua * ba + ut * bt + ur * br) + 4.5 * (ua * qa + ut * qt + ur * qr) - 1.5 * (uu * b0)
    full = b0 + slope
    sens = -(lin["design"] * (rho * slope))
    relaxed, omega = lin["relaxed"], lin["omega"]
    shear_bar = (rho * full - along) * (omega * omega) * (0.9 * lin["viscous"]) / lin["shifted"]
    shear_bar = jnp.where(relaxed, shear_bar, 0.0)
    z = shear_bar * (1.5 * inv) * lin["inv_root"]
    maa, mtt, mrr, mat, mar, mtr = (z * x for x in lin["p"])
    scale = jnp.where(relaxed, omega - lin["kappa"], jnp.where(lin["outlet"], inv, 0.0))
    la = maa * ua + mat * ut + mar * ur
    lt = mat * ua + mtt * ut + mtr * ur
    lr = mar * ua + mtr * ut + mrr * ur
    va = scale * (3.0 * (ba - b0 * ua) + 9.0 * qa) - 2.0 * la
    vt = scale * (3.0 * (bt - b0 * ut) + 9.0 * qt) - 2.0 * lt
    vr = scale * (3.0 * (br - b0 * ur) + 9.0 * qr) - 2.0 * lr
    total = jnp.where(relaxed, lin["kappa"] * b0 + scale * full, 0.0)
    total = total - shear_bar * lin["shear"] * inv - (1.0 / 3.0) * (maa + mtt + mrr)
    total = total - ((la + va) * ua + (lt + vt) * ut + (lr + vr) * ur)
    keep = lin["keep"]
    taa, ttt, trr = total + maa, total + mtt, total + mrr
    sat, sar, str_ = taa + mtt, taa + mrr, ttt + mrr
    mat2, mar2, mtr2 = 2.0 * mat, 2.0 * mar, 2.0 * mtr
    evens = [taa, ttt, trr, sat + mat2, sat - mat2, sar + mar2, sar - mar2, str_ + mtr2, str_ - mtr2]
    result = [keep * back[0] + total]
    for i, odd in enumerate(projections((va, vt, vr))):
        result.append(keep * back[1 + 2 * i] + (evens[i] + odd))
        result.append(keep * back[2 + 2 * i] + (evens[i] - odd))
    return result, sens


def face_rows(slot):
    return slice(16 * slot, 16 * slot + 16)


class Fields:
    def __init__(self, layout, own, parity, real, e, o, t, ed=None, od=None):
        self.layout, self.own = layout, own
        self.e, self.o, self.t, self.ed, self.od = e, o, t, ed, od
        self.up_e = parity == 0
        self.o_real = real == 1
        self.rows_a = own[POST].shape[1]

    def row(self, kind, q, a):
        if 0 <= a < self.rows_a:
            return self.own[FLAG][a] if kind == FLAG else self.own[kind][q, a]
        if kind == FACTOR:
            weight, *velocity = (self.row(MOTION, k, a) for k in range(4))
            return porosity_factor(q, weight, velocity)
        rows = face_rows(self.layout.slot[HI if a < 0 else LO][(kind, q)])
        return self.beyond(kind, a, self.e[rows, :], self.o[rows, :])

    def row_label(self, a):
        row = slice(16 * self.layout.fields, 16 * self.layout.fields + 1)
        return self.beyond(None, a, self.e[row, :], self.o[row, :])

    def beyond(self, kind, a, e, o):
        if kind in (ADJ, FLAG):
            o = jnp.where(self.o_real, o, 0.0)
        return jnp.where(self.up_e, o, e) if a < 0 else jnp.where(self.up_e, e, o)

    def message(self, key, a):
        block, i = self.layout.place[key]
        if 0 <= a < self.rows_a:
            return self.t[block, i : i + 1, :]
        if self.ed is None:
            row = 16 * self.layout.fields + 8 * block + i
            e, o = self.e[row : row + 1, :], self.o[row : row + 1, :]
        else:
            block = max(block - 1, 0)
            e, o = self.ed[block, i : i + 1, :], self.od[block, i : i + 1, :]
        return self.beyond(key[1], a, e, o)

    def edge(self, side, kind, q, a):
        row = self.rows_a - 1 if a < 0 else 0 if a >= self.rows_a else a
        return self.message((side, kind, q, row), a)

    def moved(self, kind, q, a, shift):
        sa, st, sr = shift
        value = self.row(kind, q, a + sa)
        rows_t, rows_r = value.shape
        if st:
            value = pltpu.roll(value, (-st) % rows_t, 0)
            beyond = self.edge(LO if st > 0 else HI, kind, q, a + sa)
            at_edge = lax.broadcasted_iota(jnp.int32, value.shape, 0) == (rows_t - 1 if st > 0 else 0)
            value = jnp.where(at_edge, beyond, value)
        if sr:
            value = pltpu.roll(value, (-sr) % rows_r, 1)
        return value


def cells(own, kind, q, a):
    return own[FLAG].at[a] if kind == FLAG else own[kind].at[q, a]


def pack_azimuthal(layout, own, t_ref):
    rows_t = own[POST].shape[2]
    for key, (block, i) in layout.place.items():
        if len(key) == 4:
            side, kind, q, a = key
            t = 0 if side == LO else rows_t - 1
            t_ref[block, i : i + 1, :] = cells(own, kind, q, a)[t : t + 1, :]


def pack_axial(layout, own, parity, e_ref, o_ref):
    rows_a = own[POST].shape[1]
    even = parity == 0
    for slot in range(layout.fields):
        low = cells(own, *layout.ax[LO][slot], 0)[...]
        high = cells(own, *layout.ax[HI][slot], rows_a - 1)[...]
        e_ref[face_rows(slot), :] = jnp.where(even, high, low)
        o_ref[face_rows(slot), :] = jnp.where(even, low, high)


def chunks(rows_a, shape, body):
    counts = (len(rows_a), shape[1] // 8, shape[2] // 128)

    def step(i, carry):
        a = rows_a[0] + i // (counts[1] * counts[2])
        t = pl.multiple_of((i // counts[2]) % counts[1] * 8, 8)
        r = pl.multiple_of(i % counts[2] * 128, 128)
        body((a, pl.ds(t, 8), pl.ds(r, 128)))
        return carry

    lax.fori_loop(0, counts[0] * counts[1] * counts[2], step, 0)


def load(ref, where):
    return [ref[(q,) + where] for q in range(19)]


def store(ref, where, values):
    for q in range(19):
        ref[(q,) + where] = values[q]


def label_of(regions, wide):
    label = jnp.max(jnp.max(regions[...], axis=0), axis=(0, 1), keepdims=True)
    return jnp.broadcast_to(label.astype(jnp.float32), (1, wide))


def porosity_factor(q, weight, velocity):
    ua, ut, ur = velocity
    pair = (q - 1) // 2
    cu = projections(velocity)[pair]
    scaled = (W_AXIS if pair < 3 else W_EDGE) * weight
    still = -1.5 * (ua * ua + ut * ut + ur * ur)
    return scaled * (still + 4.5 * cu * cu + (3.0 * cu if q % 2 else -3.0 * cu))


def factor_weight(lin):
    return -(lin["design"] * lin["rho"])


def porosity_factors(lin):
    ua, ut, ur = lin["u"]
    weight = factor_weight(lin)
    still = -1.5 * (ua * ua + ut * ut + ur * ur)
    result = [(1.0 / 3.0) * weight * still]
    for i, cu in enumerate(projections((ua, ut, ur))):
        scaled = (W_AXIS if i < 3 else W_EDGE) * weight
        even, odd = scaled * (still + 4.5 * cu * cu), 3.0 * scaled * cu
        result += [even + odd, even - odd]
    return result


def first_kernel(
    parity_ref, pops_hbm, seed_hbm, porous_hbm, types_hbm, regions_hbm,
    post, factors, e_out, o_out, t_out, ed_out, od_out, flags,
    pops, seed, porous, types, regions, motion, sems,
):
    rows_a, _, rows_r = porous.shape
    pairs = [(types_hbm, types), (regions_hbm, regions), (porous_hbm, porous)]
    pairs += [(pops_hbm.at[:, a], pops.at[:, a]) for a in range(rows_a)] + [(seed_hbm, seed)]
    loads = [pltpu.make_async_copy(*pair, sems.at[i]) for i, pair in enumerate(pairs)]
    for copy in loads:
        copy.start()
    for copy in loads[:3]:
        copy.wait()
    flags[...] = jnp.where(types[...] != 1, 1.0, 0.0)
    label = label_of(regions, rows_r)
    for side in (LO, HI):
        block, i = FIRST.place[(side, "label")]
        t_out[block, i : i + 1, :] = label
    for out in (e_out, o_out):
        out[16 * FIRST.fields : 16 * FIRST.fields + 8, :] = jnp.broadcast_to(label, (8, rows_r))

    def body(where):
        values = load(pops, where)
        lin = linearise(values, porous[where], types[where], regions[where])
        store(post, where, collide(values, lin))
        store(factors, where, porosity_factors(lin))
        for k, value in enumerate([factor_weight(lin), *lin["u"]]):
            motion[(k,) + where] = value

    for a in range(rows_a):
        loads[3 + a].wait()
        chunks([a], porous.shape, body)
    loads[-1].wait()
    own = {POST: post, ADJ: seed, FACTOR: factors, MOTION: motion, FLAG: flags}
    even = parity_ref[0] == 0
    pack_axial(FIRST, own, parity_ref[0], e_out, o_out)
    pack_azimuthal(FIRST, own, t_out)
    ed_out[0] = jnp.where(even, t_out[0], t_out[1])
    od_out[0] = jnp.where(even, t_out[1], t_out[0])
    for out in (ed_out, od_out):
        out[1] = t_out[2]


def second_kernel(
    parity_ref, real_ref, post, seed, factors, flags, porous, types, regions, e, o, t, ed, od,
    post_next, adj, sens, around, e_out, o_out, t_out, partial, state, back, parts,
):
    own = {POST: post, ADJ: seed, FACTOR: factors, FLAG: flags}
    fields = Fields(FIRST, own, parity_ref[0], real_ref[0], e, o, t, ed, od)
    rows_a, rows_t, rows_r = porous.shape
    for a in range(rows_a):
        centre = flags[a]
        state[0, a] = post[0, a]
        back[0, a] = seed[0, a]
        for q in range(1, 19):
            behind = tuple(-c for c in VELOCITY[q])
            open_ = fields.moved(FLAG, 0, a, behind)
            around[q - 1, a] = open_
            opp = OPPOSITE[q]
            state[q, a] = jnp.where(open_ > 0, fields.moved(POST, q, a, behind), post[opp, a])
            back[opp, a] = centre * fields.moved(ADJ, opp, a, behind) + (1.0 - open_) * seed[q, a]

    def body(where):
        values = load(state, where)
        lin = linearise(values, porous[where], types[where], regions[where])
        store(post_next, where, collide(values, lin))
        result, partial_sens = pull_back(load(back, where), values, lin)
        store(adj, where, result)
        sens[where] = partial_sens

    chunks(range(rows_a), porous.shape, body)
    pack_axial(SECOND, {POST: post_next, ADJ: adj}, parity_ref[0], e_out, o_out)
    pack_azimuthal(SECOND, {POST: post_next, ADJ: adj}, t_out)
    sums = {(i, st): [] for i in (-1, 0, 1) for st in (-1, 0, 1)}
    for a in range(rows_a):
        sums[(0, 0)] += [sens[a], factors[0, a] * adj[0, a]]
        for q in range(1, 19):
            behind = tuple(-c for c in VELOCITY[q])
            open_, value = around[q - 1, a], adj[q, a]
            sums[(0, 0)].append(jnp.where(open_ > 0, 0.0, factors[OPPOSITE[q], a]) * value)
            term = jnp.where(open_ > 0, fields.moved(FACTOR, q, a, behind), 0.0) * value
            from_a = a + behind[0]
            beyond = -1 if from_a < 0 else 1 if from_a >= rows_a else 0
            sums[(beyond, behind[1])].append(term)
    at_t = lax.broadcasted_iota(jnp.int32, (rows_t, rows_r), 0)
    rows = []
    for beyond in (-1, 0, 1):
        low, centre, high = (functools.reduce(jnp.add, sums[(beyond, st)]) for st in (-1, 0, 1))
        inner = centre + jnp.where(at_t == 0, 0.0, low) + jnp.where(at_t == rows_t - 1, 0.0, high)
        a = {-1: -1, 0: 0, 1: rows_a}[beyond]
        label = fields.row_label(a) if beyond else label_of(regions, rows_r)
        rows.append((jnp.sum(inner, axis=0, keepdims=True), label))
        rows.append((high[rows_t - 1 : rows_t], fields.message((LO, "label"), a)))
        rows.append((low[0:1], fields.message((HI, "label"), a)))
    parts[...] = jnp.zeros_like(parts)
    for i, (value, label) in enumerate(rows):
        parts[0, i : i + 1, :] = value
        parts[1, i : i + 1, :] = label
    lanes = lax.broadcasted_iota(jnp.int32, parts.shape[1:], 1) + 1
    total = jnp.sum(parts[0], axis=1, keepdims=True)
    chosen = jnp.where(lanes == parts[1].astype(jnp.int32), total, 0.0)
    partial[...] = jnp.sum(chosen, axis=0, keepdims=True)


def corner_kernel(e, o, t, total, e_out, o_out):
    block, i = SECOND.place[(LO, "sum")]
    for out in (e_out, o_out):
        corners = out.at[16 * SECOND.fields : 16 * SECOND.fields + 16]
        for k in range(SECOND.corner_blocks):
            corners[8 * k : 8 * k + 8, :] = t[k]
        corners[8 * block + i : 8 * block + i + 1, :] = total[...]


def third_kernel(
    parity_ref, real_ref, post, adj, flags, around, pops, porous, types, regions, sens_one, e, o, t,
    final_hbm, result_hbm, sens, final, result, back, sems,
):
    fields = Fields(SECOND, {POST: post, ADJ: adj}, parity_ref[0], real_ref[0], e, o, t)
    rows_a = porous.shape[0]
    stores = []
    for a in range(rows_a):
        final[0, a] = post[0, a]
        for q in range(1, 19):
            behind = tuple(-c for c in VELOCITY[q])
            moved = fields.moved(POST, q, a, behind)
            final[q, a] = jnp.where(around[q - 1, a] > 0, moved, post[OPPOSITE[q], a])
        stores.append(pltpu.make_async_copy(final.at[:, a], final_hbm.at[:, a], sems.at[a]))
        stores[-1].start()

    def body(where):
        values = load(pops, where)
        lin = linearise(values, porous[where], types[where], regions[where])
        adjoint, partial_sens = pull_back(load(back, where), values, lin)
        store(result, where, adjoint)
        sens[where] = partial_sens + sens_one[where]

    for a in range(rows_a):
        centre = flags[a]
        back[0, a] = adj[0, a]
        for q in range(1, 19):
            behind = tuple(-c for c in VELOCITY[q])
            opp = OPPOSITE[q]
            ahead = centre * fields.moved(ADJ, opp, a, behind)
            back[opp, a] = ahead + (1.0 - around[q - 1, a]) * adj[q, a]
        chunks([a], porous.shape, body)
        stores.append(pltpu.make_async_copy(result.at[:, a], result_hbm.at[:, a], sems.at[rows_a + a]))
        stores[-1].start()
    for copy in stores:
        copy.wait()


VMEM, HBM = pltpu.VMEM, pltpu.HBM


def call(body, in_spaces, outs, scratch, *arrays, aliases=None, cost=None):
    return pl.pallas_call(
        body,
        out_shape=[jax.ShapeDtypeStruct(shape, dtype) for shape, dtype, _ in outs],
        in_specs=[pl.BlockSpec(memory_space=space) for space in in_spaces],
        out_specs=[pl.BlockSpec(memory_space=space) for _, _, space in outs],
        scratch_shapes=scratch,
        input_output_aliases=aliases or {},
        cost_estimate=cost,
        compiler_params=pltpu.CompilerParams(vmem_limit_bytes=16 * 1024 * 1024),
    )(*arrays)


def axial_pairs(flip, shift_t=0):
    size_a, size_t = lax.axis_size("ax"), lax.axis_size("az")
    pairs = []
    for a in range(size_a):
        partner = ((a + flip) ^ 1) - flip
        for t in range(size_t):
            if 0 <= partner < size_a:
                pairs.append((a * size_t + t, partner * size_t + (t + shift_t) % size_t))
            elif shift_t:
                pairs.append((a * size_t + t, a * size_t + (t + shift_t) % size_t))
            elif size_t % 2 == 0:
                pairs.append((a * size_t + t, a * size_t + (t ^ 1)))
    return pairs


def from_both_sectors(message, high_rows, send):
    if lax.axis_size("az") == 2:
        return send(message, 1)
    return jnp.where(jnp.asarray(high_rows), send(message, 1), send(message, -1))


def high_rows(layout):
    rows = np.zeros((layout.blocks, 8, 1), bool)
    for key, (block, i) in layout.place.items():
        rows[block, i] = key[0] == HI
    return rows


def send_azimuthal(layout, message):
    size = lax.axis_size("az")

    def send(x, shift):
        return lax.ppermute(x, "az", [(i, (i + shift) % size) for i in range(size)])

    return from_both_sectors(message, high_rows(layout), send)


def send_axial(message, flip):
    return lax.ppermute(message, ("ax", "az"), axial_pairs(flip))


def send_diagonal(message, flip):
    def send(x, shift):
        return lax.ppermute(x, ("ax", "az"), axial_pairs(flip, shift))

    rows = high_rows(FIRST)
    return from_both_sectors(message, np.stack([rows[0], rows[2]]), send)


def from_partner(x, flip_a, flip_t):
    size_a, size_t = lax.axis_size("ax"), lax.axis_size("az")
    pairs = [
        (a * size_t + t, (a ^ flip_a) * size_t + (t ^ flip_t))
        for a in range(size_a)
        for t in range(size_t)
    ]
    return lax.ppermute(x, ("ax", "az"), pairs)


def shards(initial, adjoint_seed, porosity, cell_type, region):
    cells_ = porosity.shape
    pops = (19,) + cells_
    wide = cells_[2]
    f32, i32 = jnp.float32, jnp.int32
    size_a, size_t = lax.axis_size("ax"), lax.axis_size("az")
    index = lax.axis_index("ax")
    real = (index != 0) & (index != size_a - 1)
    place = ((index % 2).astype(i32).reshape(1), real.astype(i32).reshape(1))

    def axial(layout, more):
        return [((16 * layout.fields + more, wide), f32, VMEM)] * 2

    def azimuthal(layout):
        return [((layout.blocks, 8, wide), f32, VMEM)]

    inputs = (initial, adjoint_seed, porosity, cell_type, region)
    post, factors, e, o, t, ed, od, flags = call(
        first_kernel,
        [pltpu.SMEM] + [HBM] * 5,
        [(pops, f32, VMEM), (pops, f32, VMEM)] + axial(FIRST, 8) + azimuthal(FIRST)
        + [((2, 8, wide), f32, VMEM)] * 2 + [(cells_, f32, VMEM)],
        [VMEM(x.shape, x.dtype) for x in inputs]
        + [VMEM((4,) + cells_, f32), pltpu.SemaphoreType.DMA((4 + cells_[0],))],
        place[0],
        *(pltpu.with_memory_space_constraint(x, HBM) for x in inputs),
    )
    e, o = send_axial(e, 0), send_axial(o, 1)
    t_near = send_azimuthal(FIRST, t)
    ed, od = send_diagonal(ed, 0), send_diagonal(od, 1)
    post, adj, sens_one, around, e, o, t, total = call(
        second_kernel,
        [pltpu.SMEM] * 2 + [VMEM] * 12,
        [(pops, f32, VMEM), (pops, f32, VMEM), (cells_, f32, VMEM), ((18,) + cells_, f32, VMEM)]
        + axial(SECOND, 16) + azimuthal(SECOND) + [((1, wide), f32, VMEM)],
        [VMEM(pops, f32), VMEM(pops, f32), VMEM((2, 16, wide), f32)],
        *place, post, adjoint_seed, factors, flags, porosity, cell_type, region, e, o, t_near, ed, od,
    )
    t_near = send_azimuthal(SECOND, t)
    block, i = SECOND.place[(LO, "sum")]
    halving = size_a >= 4 and not (size_a & (size_a - 1) or size_t & (size_t - 1))
    flips = [((1 << k) | 1, 0) for k in range(2, size_a.bit_length() - 1)]
    if halving:
        total = total + from_partner(total, 3, 0)
        flips = [(1, 1 << k) for k in range(size_t.bit_length() - 1)] + flips
    e, o = call(
        corner_kernel,
        [VMEM] * 4,
        axial(SECOND, 16),
        [],
        e, o, t_near, total,
        aliases={0: 0, 1: 1},
    )
    e, o = send_axial(e, 0), send_axial(o, 1)
    if halving:
        row = 16 * SECOND.fields + 8 * block + i
        totals = total + e[row : row + 1]
        for flip in flips:
            if flip == flips[-1]:
                totals, _ = lax.optimization_barrier((totals, o))
            totals = totals + from_partner(totals, *flip)
    else:
        totals = lax.psum(total, ("ax", "az"))
    final, adjoint, sensitivity = call(
        third_kernel,
        [pltpu.SMEM] * 2 + [VMEM] * 12,
        [(pops, f32, HBM), (pops, f32, HBM), (cells_, f32, VMEM)],
        [VMEM(pops, f32), VMEM(pops, f32), VMEM(pops, f32)]
        + [pltpu.SemaphoreType.DMA((2 * cells_[0],))],
        *place, post, adj, flags, around, initial, porosity, cell_type, region, sens_one, e, o, t_near,
    )
    return final, adjoint, sensitivity, totals[0, : size_a * size_t // 4]


def solution(mesh):
    return jax.shard_map(
        shards,
        mesh=mesh,
        in_specs=(
            P(None, "ax", "az", None),
            P(None, "ax", "az", None),
            P("ax", "az", None),
            P("ax", "az", None),
            P("ax", "az", None),
        ),
        out_specs=(P(None, "ax", "az", None), P(None, "ax", "az", None), P("ax", "az", None), P()),
        check_vma=False,
    )
```

```python
import functools

import jax
import jax.numpy as jnp
import numpy as np
from jax import lax
from jax.experimental import pallas as pl
from jax.experimental.pallas import tpu as pltpu
from jax.sharding import PartitionSpec as P

VELOCITY = [
    (0, 0, 0),
    (1, 0, 0),
    (-1, 0, 0),
    (0, 1, 0),
    (0, -1, 0),
    (0, 0, 1),
    (0, 0, -1),
    (1, 1, 0),
    (-1, -1, 0),
    (1, -1, 0),
    (-1, 1, 0),
    (1, 0, 1),
    (-1, 0, -1),
    (1, 0, -1),
    (-1, 0, 1),
    (0, 1, 1),
    (0, -1, -1),
    (0, 1, -1),
    (0, -1, 1),
]
OPPOSITE = [0, 2, 1, 4, 3, 6, 5, 8, 7, 10, 9, 12, 11, 14, 13, 16, 15, 18, 17]
INLET_SPEED = (0.05, 0.05, 0.0)
W_AXIS = 1.0 / 18.0
W_EDGE = 1.0 / 36.0


def moving(axis, sign):
    return [q for q in range(19) if VELOCITY[q][axis] == sign]


LO, HI = 0, 1
POST, ADJ, FACTOR, FLAG, MOTION = 0, 1, 2, 3, 4


def face_fields(kinds, axis, side):
    sign = -1 if side == LO else 1
    fields = []
    for kind in kinds:
        if kind == FLAG:
            fields.append((FLAG, 0))
        elif kind == FACTOR and axis == 0:
            fields += [(MOTION, k) for k in range(4)]
        else:
            fields += [(kind, q) for q in moving(axis, -sign if kind == ADJ else sign)]
    return fields


class Layout:
    def __init__(self, kinds, extra):
        self.ax = [face_fields(kinds, 0, side) for side in (LO, HI)]
        self.slot = [{key: i for i, key in enumerate(fields)} for fields in self.ax]
        self.fields = len(self.ax[LO])
        corner, rest = [], []
        for a, sign in ((1, 1), (0, -1)):
            for side in (LO, HI):
                for kind, q in face_fields(kinds, 1, side):
                    leaves = VELOCITY[q][0] == (-sign if kind == ADJ else sign)
                    key = (side, kind, q, a)
                    (corner if kind == FLAG or leaves else rest).append(key)
        corner += extra
        self.corner_blocks = -(-len(corner) // 8)
        self.blocks = self.corner_blocks + -(-len(rest) // 8)
        self.place = {key: (i // 8, i % 8) for i, key in enumerate(corner)}
        self.place.update({key: (self.corner_blocks + i // 8, i % 8) for i, key in enumerate(rest)})


FIRST = Layout((POST, ADJ, FACTOR, FLAG), [(LO, "label"), (HI, "label")])
SECOND = Layout((POST, ADJ), [(LO, "sum")])


def pairs_of(values):
    sums = [values[q] + values[q + 1] for q in range(1, 19, 2)]
    diffs = [values[q] - values[q + 1] for q in range(1, 19, 2)]
    return sums, diffs


def projections(vec):
    va, vt, vr = vec
    return [va, vt, vr, va + vt, va - vt, va + vr, va - vr, vt + vr, vt - vr]


def linearise(pops, porous, types, regions):
    sums, diffs = pairs_of(pops)
    s0, s1, s2, s3, s4, s5, s6, s7, s8 = sums
    d0, d1, d2, d3, d4, d5, d6, d7, d8 = diffs
    at, ar, tr = s3 + s4, s5 + s6, s7 + s8
    rho = pops[0] + ((s0 + s1) + (s2 + at)) + (ar + tr)
    ma = (d0 + (d3 + d4)) + (d5 + d6)
    mt = (d1 + (d3 - d4)) + (d7 + d8)
    mr = (d2 + (d5 - d6)) + (d7 - d8)
    inv = 1.0 / rho
    ua, ut, ur = ma * inv, mt * inv, mr * inv
    third = rho * (1.0 / 3.0)
    paa = (s0 + at + ar - third) - ma * ua
    ptt = (s1 + at + tr - third) - mt * ut
    prr = (s2 + ar + tr - third) - mr * ur
    pat = (s3 - s4) - ma * ut
    par = (s5 - s6) - ma * ur
    ptr = (s7 - s8) - mt * ur
    square = (paa * paa + ptt * ptt + prr * prr) + 2.0 * (pat * pat + par * par + ptr * ptr) + 0.0001
    inv_root = lax.rsqrt(square)
    shear = 1.5 * (square * inv_root) * inv
    shifted = shear + 0.01
    viscous = 0.02 * jnp.exp((0.7 - 1.0) * jnp.log(shifted))
    omega = 1.0 / (0.5 + 3.0 * viscous)
    relaxed = (types != 2) & (types != 3)
    kappa = jnp.where(regions > 0, porous, 0.0)
    return dict(
        rho=rho,
        inv=inv,
        u=(ua, ut, ur),
        p=(paa, ptt, prr, pat, par, ptr),
        inv_root=inv_root,
        shear=shear,
        shifted=shifted,
        viscous=viscous,
        omega=omega,
        relaxed=relaxed,
        kappa=kappa,
        keep=jnp.where(relaxed, 1.0 - omega, 0.0),
        design=jnp.where(relaxed & (regions > 0), 1.0, 0.0),
        inlet=types == 2,
        outlet=types == 3,
    )


def collide(pops, lin):
    rho, relaxed, inlet = lin["rho"], lin["relaxed"], lin["inlet"]
    ua, ut, ur = (jnp.where(inlet, speed, x) for x, speed in zip(lin["u"], INLET_SPEED))
    scale = jnp.where(relaxed, (lin["omega"] - lin["kappa"]) * rho, 1.0)
    rest = jnp.where(relaxed, lin["kappa"] * rho, 0.0)
    keep = lin["keep"]
    still = 1.0 - 1.5 * (ua * ua + ut * ut + ur * ur)
    post = [keep * pops[0] + (1.0 / 3.0) * (scale * still + rest)]
    for i, cu in enumerate(projections((ua, ut, ur))):
        weight = W_AXIS if i < 3 else W_EDGE
        even = weight * (scale * (still + 4.5 * cu * cu) + rest)
        odd = (3.0 * weight) * (scale * cu)
        post.append(keep * pops[1 + 2 * i] + (even + odd))
        post.append(keep * pops[2 + 2 * i] + (even - odd))
    return post


def pull_back(back, pops, lin):
    sums, diffs = pairs_of(back)
    s0, s1, s2, s3, s4, s5, s6, s7, s8 = sums
    d0, d1, d2, d3, d4, d5, d6, d7, d8 = diffs
    at, ar, tr = s3 + s4, s5 + s6, s7 + s8
    b0 = (1.0 / 3.0) * back[0] + W_AXIS * (s0 + s1 + s2) + W_EDGE * (at + ar + tr)
    ba = W_AXIS * d0 + W_EDGE * ((d3 + d4) + (d5 + d6))
    bt = W_AXIS * d1 + W_EDGE * ((d3 - d4) + (d7 + d8))
    br = W_AXIS * d2 + W_EDGE * ((d5 - d6) + (d7 - d8))
    baa = W_AXIS * s0 + W_EDGE * (at + ar)
    btt = W_AXIS * s1 + W_EDGE * (at + tr)
    brr = W_AXIS * s2 + W_EDGE * (ar + tr)
    bat, bar, btr = W_EDGE * (s3 - s4), W_EDGE * (s5 - s6), W_EDGE * (s7 - s8)
    along = back[0] * pops[0]
    for q in range(1, 19):
        along = along + back[q] * pops[q]
    rho, inv = lin["rho"], lin["inv"]
    ua, ut, ur = lin["u"]
    qa = baa * ua + bat * ut + bar * ur
    qt = bat * ua + btt * ut + btr * ur
    qr = bar * ua + btr * ut + brr * ur
    uu = ua * ua + ut * ut + ur * ur
    slope = 3.0 * (ua * ba + ut * bt + ur * br) + 4.5 * (ua * qa + ut * qt + ur * qr) - 1.5 * (uu * b0)
    full = b0 + slope
    sens = -(lin["design"] * (rho * slope))
    relaxed, omega = lin["relaxed"], lin["omega"]
    shear_bar = (rho * full - along) * (omega * omega) * (0.9 * lin["viscous"]) / lin["shifted"]
    shear_bar = jnp.where(relaxed, shear_bar, 0.0)
    z = shear_bar * (1.5 * inv) * lin["inv_root"]
    maa, mtt, mrr, mat, mar, mtr = (z * x for x in lin["p"])
    scale = jnp.where(relaxed, omega - lin["kappa"], jnp.where(lin["outlet"], inv, 0.0))
    la = maa * ua + mat * ut + mar * ur
    lt = mat * ua + mtt * ut + mtr * ur
    lr = mar * ua + mtr * ut + mrr * ur
    va = scale * (3.0 * (ba - b0 * ua) + 9.0 * qa) - 2.0 * la
    vt = scale * (3.0 * (bt - b0 * ut) + 9.0 * qt) - 2.0 * lt
    vr = scale * (3.0 * (br - b0 * ur) + 9.0 * qr) - 2.0 * lr
    total = jnp.where(relaxed, lin["kappa"] * b0 + scale * full, 0.0)
    total = total - shear_bar * lin["shear"] * inv - (1.0 / 3.0) * (maa + mtt + mrr)
    total = total - ((la + va) * ua + (lt + vt) * ut + (lr + vr) * ur)
    keep = lin["keep"]
    taa, ttt, trr = total + maa, total + mtt, total + mrr
    sat, sar, str_ = taa + mtt, taa + mrr, ttt + mrr
    mat2, mar2, mtr2 = 2.0 * mat, 2.0 * mar, 2.0 * mtr
    evens = [taa, ttt, trr, sat + mat2, sat - mat2, sar + mar2, sar - mar2, str_ + mtr2, str_ - mtr2]
    result = [keep * back[0] + total]
    for i, odd in enumerate(projections((va, vt, vr))):
        result.append(keep * back[1 + 2 * i] + (evens[i] + odd))
        result.append(keep * back[2 + 2 * i] + (evens[i] - odd))
    return result, sens


def face_rows(slot):
    return slice(16 * slot, 16 * slot + 16)


def by_parity(parity_ref, body):
    for parity in (0, 1):
        pl.when(parity_ref[0] == parity)(functools.partial(body, parity))


def near_rows(parity, rows_a):
    return (range(1, rows_a), 0) if parity == 0 else (range(rows_a - 1), rows_a - 1)


class Fields:
    def __init__(self, layout, own, parity, e=None, o=None, real=None, t=None, ed=None, od=None):
        self.layout, self.own, self.t = layout, own, t
        self.rows_a = own[POST].shape[1]
        sides = [(o, od, real), (e, ed, None)]
        self.sides = sides if parity == 0 else sides[::-1]

    def row(self, kind, q, a):
        if 0 <= a < self.rows_a:
            return self.own[FLAG][a] if kind == FLAG else self.own[kind][q, a]
        if kind == FACTOR:
            weight, *velocity = (self.row(MOTION, k, a) for k in range(4))
            return porosity_factor(q, weight, velocity)
        message, _, real = self.sides[a >= 0]
        slot = self.layout.slot[HI if a < 0 else LO][(kind, q)]
        return self.masked(kind, message[face_rows(slot), :], real)

    def masked(self, kind, value, real):
        if real is None or kind not in (ADJ, FLAG):
            return value
        return jnp.where(real == 1, value, 0.0)

    def row_label(self, a):
        row = 16 * self.layout.fields
        return self.sides[a >= 0][0][row : row + 1, :]

    def message(self, key, a):
        block, i = self.layout.place[key]
        if 0 <= a < self.rows_a:
            return self.t[block, i : i + 1, :]
        axial, corners, real = self.sides[a >= 0]
        if corners is None:
            row = 16 * self.layout.fields + 8 * block + i
            return self.masked(key[1], axial[row : row + 1, :], real)
        return self.masked(key[1], corners[max(block - 1, 0), i : i + 1, :], real)

    def edge(self, side, kind, q, a):
        row = self.rows_a - 1 if a < 0 else 0 if a >= self.rows_a else a
        return self.message((side, kind, q, row), a)

    def moved(self, kind, q, a, shift):
        sa, st, sr = shift
        value = self.row(kind, q, a + sa)
        rows_t, rows_r = value.shape
        if st:
            value = pltpu.roll(value, (-st) % rows_t, 0)
            beyond = self.edge(LO if st > 0 else HI, kind, q, a + sa)
            at_edge = lax.broadcasted_iota(jnp.int32, value.shape, 0) == (rows_t - 1 if st > 0 else 0)
            value = jnp.where(at_edge, beyond, value)
        if sr:
            value = pltpu.roll(value, (-sr) % rows_r, 1)
        return value


def cells(own, kind, q, a):
    return own[FLAG].at[a] if kind == FLAG else own[kind].at[q, a]


def stream_row(fields, a, around, result):
    post = fields.own[POST]
    result[0, a] = post[0, a]
    for q in range(1, 19):
        moved = fields.moved(POST, q, a, tuple(-c for c in VELOCITY[q]))
        result[q, a] = jnp.where(around[q - 1, a] > 0, moved, post[OPPOSITE[q], a])


def stream_adjoint_row(fields, a, centre, around, result):
    adj = fields.own[ADJ]
    result[0, a] = adj[0, a]
    for q in range(1, 19):
        opp = OPPOSITE[q]
        ahead = centre * fields.moved(ADJ, opp, a, tuple(-c for c in VELOCITY[q]))
        result[opp, a] = ahead + (1.0 - around[q - 1, a]) * adj[q, a]


def pack_azimuthal(layout, own, t_ref):
    rows_t = own[POST].shape[2]
    for key, (block, i) in layout.place.items():
        if len(key) == 4:
            side, kind, q, a = key
            t = 0 if side == LO else rows_t - 1
            t_ref[block, i : i + 1, :] = cells(own, kind, q, a)[t : t + 1, :]


def pack_axial(layout, own, parity, e_ref, o_ref):
    rows_a = own[POST].shape[1]
    low_ref, high_ref = (o_ref, e_ref) if parity == 0 else (e_ref, o_ref)
    for slot in range(layout.fields):
        low_ref[face_rows(slot), :] = cells(own, *layout.ax[LO][slot], 0)[...]
        high_ref[face_rows(slot), :] = cells(own, *layout.ax[HI][slot], rows_a - 1)[...]


def chunks(rows_a, shape, body):
    counts = (len(rows_a), shape[1] // 8, shape[2] // 128)

    def step(i, carry):
        a = rows_a[0] + i // (counts[1] * counts[2])
        t = pl.multiple_of((i // counts[2]) % counts[1] * 8, 8)
        r = pl.multiple_of(i % counts[2] * 128, 128)
        body((a, pl.ds(t, 8), pl.ds(r, 128)))
        return carry

    lax.fori_loop(0, counts[0] * counts[1] * counts[2], step, 0)


def load(ref, where):
    return [ref[(q,) + where] for q in range(19)]


def store(ref, where, values):
    for q in range(19):
        ref[(q,) + where] = values[q]


def label_of(regions, wide):
    label = jnp.max(jnp.max(regions[...], axis=0), axis=(0, 1), keepdims=True)
    return jnp.broadcast_to(label.astype(jnp.float32), (1, wide))


def porosity_factor(q, weight, velocity):
    ua, ut, ur = velocity
    pair = (q - 1) // 2
    cu = projections(velocity)[pair]
    scaled = (W_AXIS if pair < 3 else W_EDGE) * weight
    still = -1.5 * (ua * ua + ut * ut + ur * ur)
    return scaled * (still + 4.5 * cu * cu + (3.0 * cu if q % 2 else -3.0 * cu))


def factor_weight(lin):
    return -(lin["design"] * lin["rho"])


def porosity_factors(lin):
    ua, ut, ur = lin["u"]
    weight = factor_weight(lin)
    still = -1.5 * (ua * ua + ut * ut + ur * ur)
    result = [(1.0 / 3.0) * weight * still]
    for i, cu in enumerate(projections((ua, ut, ur))):
        scaled = (W_AXIS if i < 3 else W_EDGE) * weight
        even, odd = scaled * (still + 4.5 * cu * cu), 3.0 * scaled * cu
        result += [even + odd, even - odd]
    return result


def first_kernel(
    parity_ref, pops_hbm, seed_hbm, porous_hbm, types_hbm, regions_hbm,
    post, factors, e_out, o_out, t_out, ed_out, od_out, flags,
    pops, seed, porous, types, regions, motion, sems,
):
    rows_a, _, rows_r = porous.shape
    pairs = [(types_hbm, types), (regions_hbm, regions), (porous_hbm, porous)]
    pairs += [(pops_hbm.at[:, a], pops.at[:, a]) for a in range(rows_a)] + [(seed_hbm, seed)]
    loads = [pltpu.make_async_copy(*pair, sems.at[i]) for i, pair in enumerate(pairs)]
    for copy in loads:
        copy.start()
    for copy in loads[:3]:
        copy.wait()
    flags[...] = jnp.where(types[...] != 1, 1.0, 0.0)
    label = label_of(regions, rows_r)
    for side in (LO, HI):
        block, i = FIRST.place[(side, "label")]
        t_out[block, i : i + 1, :] = label
    for out in (e_out, o_out):
        out[16 * FIRST.fields : 16 * FIRST.fields + 8, :] = jnp.broadcast_to(label, (8, rows_r))

    def body(where):
        values = load(pops, where)
        lin = linearise(values, porous[where], types[where], regions[where])
        store(post, where, collide(values, lin))
        store(factors, where, porosity_factors(lin))
        for k, value in enumerate([factor_weight(lin), *lin["u"]]):
            motion[(k,) + where] = value

    for a in range(rows_a):
        loads[3 + a].wait()
        chunks([a], porous.shape, body)
    loads[-1].wait()
    own = {POST: post, ADJ: seed, FACTOR: factors, MOTION: motion, FLAG: flags}
    pack_azimuthal(FIRST, own, t_out)

    def run(parity):
        pack_axial(FIRST, own, parity, e_out, o_out)
        for out, block in ((ed_out, parity), (od_out, 1 - parity)):
            out[0] = t_out[block]
            out[1] = t_out[2]

    by_parity(parity_ref, run)


def second_rows(fields, rows, cell_refs, results, scratch):
    porous, types, regions = cell_refs
    post_next, adj, sens, around = results
    state, back = scratch
    for a in rows:
        for q in range(1, 19):
            around[q - 1, a] = fields.moved(FLAG, 0, a, tuple(-c for c in VELOCITY[q]))
        stream_row(fields, a, around, state)
        stream_adjoint_row(fields, a, fields.own[FLAG][a], around, back)

    def body(where):
        values = load(state, where)
        lin = linearise(values, porous[where], types[where], regions[where])
        store(post_next, where, collide(values, lin))
        result, partial_sens = pull_back(load(back, where), values, lin)
        store(adj, where, result)
        sens[where] = partial_sens

    chunks(rows, porous.shape, body)


def second_near_kernel(
    parity_ref, post, seed, flags, porous, types, regions, e, t, ed,
    post_next, adj, sens, around, state, back,
):
    def run(parity):
        own = {POST: post, ADJ: seed, FLAG: flags}
        fields = Fields(FIRST, own, parity, e=e, t=t, ed=ed)
        rows, _ = near_rows(parity, porous.shape[0])
        results = (post_next, adj, sens, around)
        second_rows(fields, rows, (porous, types, regions), results, (state, back))

    by_parity(parity_ref, run)


def second_far_kernel(
    parity_ref, real_ref, post_near, adj_near, sens_near, around_near,
    post, seed, factors, flags, porous, types, regions, e, o, t, ed, od,
    post_next, adj, sens, around, e_out, o_out, t_out, partial, state, back, parts,
):
    def run(parity):
        own = {POST: post, ADJ: seed, FACTOR: factors, FLAG: flags}
        fields = Fields(FIRST, own, parity, e, o, real_ref[0], t, ed, od)
        _, row = near_rows(parity, porous.shape[0])
        results = (post_next, adj, sens, around)
        second_rows(fields, [row], (porous, types, regions), results, (state, back))
        pack_axial(SECOND, {POST: post_next, ADJ: adj}, parity, e_out, o_out)
        pack_azimuthal(SECOND, {POST: post_next, ADJ: adj}, t_out)
        region_sums(fields, adj, sens, around, regions, parts, partial)

    by_parity(parity_ref, run)


def region_sums(fields, adj, sens, around, regions, parts, partial):
    factors = fields.own[FACTOR]
    rows_a, rows_t, rows_r = sens.shape
    sums = {(i, st): [] for i in (-1, 0, 1) for st in (-1, 0, 1)}
    for a in range(rows_a):
        sums[(0, 0)] += [sens[a], factors[0, a] * adj[0, a]]
        for q in range(1, 19):
            behind = tuple(-c for c in VELOCITY[q])
            open_, value = around[q - 1, a], adj[q, a]
            sums[(0, 0)].append(jnp.where(open_ > 0, 0.0, factors[OPPOSITE[q], a]) * value)
            term = jnp.where(open_ > 0, fields.moved(FACTOR, q, a, behind), 0.0) * value
            from_a = a + behind[0]
            beyond = -1 if from_a < 0 else 1 if from_a >= rows_a else 0
            sums[(beyond, behind[1])].append(term)
    at_t = lax.broadcasted_iota(jnp.int32, (rows_t, rows_r), 0)
    rows = []
    for beyond in (-1, 0, 1):
        low, centre, high = (functools.reduce(jnp.add, sums[(beyond, st)]) for st in (-1, 0, 1))
        inner = centre + jnp.where(at_t == 0, 0.0, low) + jnp.where(at_t == rows_t - 1, 0.0, high)
        a = {-1: -1, 0: 0, 1: rows_a}[beyond]
        label = fields.row_label(a) if beyond else label_of(regions, rows_r)
        rows.append((jnp.sum(inner, axis=0, keepdims=True), label))
        rows.append((high[rows_t - 1 : rows_t], fields.message((LO, "label"), a)))
        rows.append((low[0:1], fields.message((HI, "label"), a)))
    parts[...] = jnp.zeros_like(parts)
    for i, (value, label) in enumerate(rows):
        parts[0, i : i + 1, :] = value
        parts[1, i : i + 1, :] = label
    lanes = lax.broadcasted_iota(jnp.int32, parts.shape[1:], 1) + 1
    total = jnp.sum(parts[0], axis=1, keepdims=True)
    chosen = jnp.where(lanes == parts[1].astype(jnp.int32), total, 0.0)
    partial[...] = jnp.sum(chosen, axis=0, keepdims=True)


def corner_kernel(e, o, t, total, e_out, o_out):
    block, i = SECOND.place[(LO, "sum")]
    for out in (e_out, o_out):
        corners = out.at[16 * SECOND.fields : 16 * SECOND.fields + 16]
        for k in range(SECOND.corner_blocks):
            corners[8 * k : 8 * k + 8, :] = t[k]
        corners[8 * block + i : 8 * block + i + 1, :] = total[...]


def third_rows(fields, rows, cell_refs, own_refs, hbm, sens, scratch, sems):
    porous, types, regions = cell_refs
    around, flags, pops, sens_one = own_refs
    final, result, back = scratch
    stores = []

    def send(source, target, a):
        stores.append(pltpu.make_async_copy(source.at[:, a], target.at[:, a], sems.at[len(stores)]))
        stores[-1].start()

    def body(where):
        values = load(pops, where)
        lin = linearise(values, porous[where], types[where], regions[where])
        adjoint, partial_sens = pull_back(load(back, where), values, lin)
        store(result, where, adjoint)
        sens[where] = partial_sens + sens_one[where]

    for a in rows:
        stream_row(fields, a, around, final)
        send(final, hbm[0], a)
        stream_adjoint_row(fields, a, flags[a], around, back)
        chunks([a], porous.shape, body)
        send(result, hbm[1], a)
    for copy in stores:
        copy.wait()


def third_near_kernel(
    parity_ref, post, adj, flags, around, pops, porous, types, regions, sens_one, e, t,
    final_hbm, result_hbm, sens, final, result, back, sems,
):
    def run(parity):
        fields = Fields(SECOND, {POST: post, ADJ: adj}, parity, e=e, t=t)
        rows, _ = near_rows(parity, porous.shape[0])
        third_rows(
            fields, rows, (porous, types, regions), (around, flags, pops, sens_one),
            (final_hbm, result_hbm), sens, (final, result, back), sems,
        )

    by_parity(parity_ref, run)


def third_far_kernel(
    parity_ref, real_ref, final_near, result_near, sens_near,
    post, adj, flags, around, pops, porous, types, regions, sens_one, o, t,
    final_hbm, result_hbm, sens, final, result, back, sems,
):
    def run(parity):
        fields = Fields(SECOND, {POST: post, ADJ: adj}, parity, o=o, real=real_ref[0], t=t)
        rows, row = near_rows(parity, porous.shape[0])
        for a in rows:
            sens[a] = sens_near[a]
        third_rows(
            fields, [row], (porous, types, regions), (around, flags, pops, sens_one),
            (final_hbm, result_hbm), sens, (final, result, back), sems,
        )

    by_parity(parity_ref, run)


VMEM, HBM = pltpu.VMEM, pltpu.HBM


def call(body, in_spaces, outs, scratch, *arrays, aliases=None, cost=None):
    return pl.pallas_call(
        body,
        out_shape=[jax.ShapeDtypeStruct(shape, dtype) for shape, dtype, _ in outs],
        in_specs=[pl.BlockSpec(memory_space=space) for space in in_spaces],
        out_specs=[pl.BlockSpec(memory_space=space) for _, _, space in outs],
        scratch_shapes=scratch,
        input_output_aliases=aliases or {},
        cost_estimate=cost,
        compiler_params=pltpu.CompilerParams(vmem_limit_bytes=16 * 1024 * 1024),
    )(*arrays)


def axial_pairs(flip, shift_t=0):
    size_a, size_t = lax.axis_size("ax"), lax.axis_size("az")
    pairs = []
    for a in range(size_a):
        partner = ((a + flip) ^ 1) - flip
        for t in range(size_t):
            if 0 <= partner < size_a:
                pairs.append((a * size_t + t, partner * size_t + (t + shift_t) % size_t))
            elif shift_t:
                pairs.append((a * size_t + t, a * size_t + (t + shift_t) % size_t))
            elif size_t % 2 == 0:
                pairs.append((a * size_t + t, a * size_t + (t ^ 1)))
    return pairs


def from_both_sectors(message, high_rows, send):
    if lax.axis_size("az") == 2:
        return send(message, 1)
    return jnp.where(jnp.asarray(high_rows), send(message, 1), send(message, -1))


def high_rows(layout):
    rows = np.zeros((layout.blocks, 8, 1), bool)
    for key, (block, i) in layout.place.items():
        rows[block, i] = key[0] == HI
    return rows


def send_azimuthal(layout, message):
    size = lax.axis_size("az")

    def send(x, shift):
        return lax.ppermute(x, "az", [(i, (i + shift) % size) for i in range(size)])

    return from_both_sectors(message, high_rows(layout), send)


def send_axial(message, flip):
    return lax.ppermute(message, ("ax", "az"), axial_pairs(flip))


def send_diagonal(message, flip):
    def send(x, shift):
        return lax.ppermute(x, ("ax", "az"), axial_pairs(flip, shift))

    rows = high_rows(FIRST)
    return from_both_sectors(message, np.stack([rows[0], rows[2]]), send)


def from_partner(x, flip_a, flip_t):
    size_a, size_t = lax.axis_size("ax"), lax.axis_size("az")
    pairs = [
        (a * size_t + t, (a ^ flip_a) * size_t + (t ^ flip_t))
        for a in range(size_a)
        for t in range(size_t)
    ]
    return lax.ppermute(x, ("ax", "az"), pairs)


def shards(initial, adjoint_seed, porosity, cell_type, region):
    cells_ = porosity.shape
    pops = (19,) + cells_
    wide = cells_[2]
    f32, i32 = jnp.float32, jnp.int32
    size_a, size_t = lax.axis_size("ax"), lax.axis_size("az")
    index = lax.axis_index("ax")
    real = (index != 0) & (index != size_a - 1)
    place = ((index % 2).astype(i32).reshape(1), real.astype(i32).reshape(1))

    def axial(layout, more):
        return ((16 * layout.fields + more, wide), f32, VMEM)

    def azimuthal(layout):
        return [((layout.blocks, 8, wide), f32, VMEM)]

    inputs = (initial, adjoint_seed, porosity, cell_type, region)
    post, factors, e, o, t, ed, od, flags = call(
        first_kernel,
        [pltpu.SMEM] + [HBM] * 5,
        [(pops, f32, VMEM), (pops, f32, VMEM)] + [axial(FIRST, 8)] * 2 + azimuthal(FIRST)
        + [((2, 8, wide), f32, VMEM)] * 2 + [(cells_, f32, VMEM)],
        [VMEM(x.shape, x.dtype) for x in inputs]
        + [VMEM((4,) + cells_, f32), pltpu.SemaphoreType.DMA((4 + cells_[0],))],
        place[0],
        *(pltpu.with_memory_space_constraint(x, HBM) for x in inputs),
    )
    e, o = send_axial(e, 0), send_axial(o, 1)
    t_near = send_azimuthal(FIRST, t)
    ed, od = send_diagonal(ed, 0), send_diagonal(od, 1)
    layers = [(pops, f32, VMEM), (pops, f32, VMEM), (cells_, f32, VMEM), ((18,) + cells_, f32, VMEM)]
    inside = (flags, porosity, cell_type, region)
    near = call(
        second_near_kernel,
        [pltpu.SMEM] + [VMEM] * 9,
        layers,
        [VMEM(pops, f32), VMEM(pops, f32)],
        place[0], post, adjoint_seed, *inside, e, t_near, ed,
    )
    post, adj, sens_one, around, e, o, t, total = call(
        second_far_kernel,
        [pltpu.SMEM] * 2 + [VMEM] * 16,
        layers + [axial(SECOND, 16)] * 2 + azimuthal(SECOND) + [((1, wide), f32, VMEM)],
        [VMEM(pops, f32), VMEM(pops, f32), VMEM((2, 16, wide), f32)],
        *place, *near, post, adjoint_seed, factors, *inside, e, o, t_near, ed, od,
        aliases={2: 0, 3: 1, 4: 2, 5: 3},
    )
    t_near = send_azimuthal(SECOND, t)
    block, i = SECOND.place[(LO, "sum")]
    halving = size_a >= 4 and not (size_a & (size_a - 1) or size_t & (size_t - 1))
    flips = [((1 << k) | 1, 0) for k in range(2, size_a.bit_length() - 1)]
    if halving:
        total = total + from_partner(total, 3, 0)
        flips = [(1, 1 << k) for k in range(size_t.bit_length() - 1)] + flips
    e, o = call(
        corner_kernel,
        [VMEM] * 4,
        [axial(SECOND, 16)] * 2,
        [],
        e, o, t_near, total,
        aliases={0: 0, 1: 1},
    )
    e, o = send_axial(e, 0), send_axial(o, 1)
    stored = [(pops, f32, HBM), (pops, f32, HBM), (cells_, f32, VMEM)]
    third_scratch = [VMEM(pops, f32)] * 3 + [pltpu.SemaphoreType.DMA((2 * cells_[0],))]
    inside = (post, adj, flags, around, initial, porosity, cell_type, region, sens_one)
    near = call(
        third_near_kernel,
        [pltpu.SMEM] + [VMEM] * 11,
        stored,
        third_scratch,
        place[0], *inside, e, t_near,
    )
    if halving:
        row = 16 * SECOND.fields + 8 * block + i
        totals = total + e[row : row + 1]
        for flip in flips:
            if flip == flips[-1]:
                totals, _ = lax.optimization_barrier((totals, (o, near[2])))
            totals = totals + from_partner(totals, *flip)
    else:
        totals = lax.psum(total, ("ax", "az"))
    final, adjoint, sensitivity = call(
        third_far_kernel,
        [pltpu.SMEM] * 2 + [HBM] * 2 + [VMEM] * 12,
        stored,
        third_scratch,
        *place, *near, *inside, o, t_near,
        aliases={2: 0, 3: 1},
    )
    return final, adjoint, sensitivity, totals[0, : size_a * size_t // 4]


def solution(mesh):
    return jax.shard_map(
        shards,
        mesh=mesh,
        in_specs=(
            P(None, "ax", "az", None),
            P(None, "ax", "az", None),
            P("ax", "az", None),
            P("ax", "az", None),
            P("ax", "az", None),
        ),
        out_specs=(P(None, "ax", "az", None), P(None, "ax", "az", None), P("ax", "az", None), P()),
        check_vma=False,
    )
```

```python
import functools

import jax
import jax.numpy as jnp
import numpy as np
from jax import lax
from jax.experimental import pallas as pl
from jax.experimental.pallas import tpu as pltpu
from jax.sharding import PartitionSpec as P

VELOCITY = [
    (0, 0, 0),
    (1, 0, 0),
    (-1, 0, 0),
    (0, 1, 0),
    (0, -1, 0),
    (0, 0, 1),
    (0, 0, -1),
    (1, 1, 0),
    (-1, -1, 0),
    (1, -1, 0),
    (-1, 1, 0),
    (1, 0, 1),
    (-1, 0, -1),
    (1, 0, -1),
    (-1, 0, 1),
    (0, 1, 1),
    (0, -1, -1),
    (0, 1, -1),
    (0, -1, 1),
]
OPPOSITE = [0, 2, 1, 4, 3, 6, 5, 8, 7, 10, 9, 12, 11, 14, 13, 16, 15, 18, 17]
INLET_SPEED = (0.05, 0.05, 0.0)
W_AXIS = 1.0 / 18.0
W_EDGE = 1.0 / 36.0


def moving(axis, sign):
    return [q for q in range(19) if VELOCITY[q][axis] == sign]


LO, HI = 0, 1
POST, ADJ, FACTOR, FLAG, MOTION = 0, 1, 2, 3, 4


def face_fields(kinds, axis, side):
    sign = -1 if side == LO else 1
    fields = []
    for kind in kinds:
        if kind == FLAG:
            fields.append((FLAG, 0))
        elif kind == FACTOR and axis == 0:
            fields += [(MOTION, k) for k in range(4)]
        else:
            fields += [(kind, q) for q in moving(axis, -sign if kind == ADJ else sign)]
    return fields


class Layout:
    def __init__(self, kinds):
        self.ax = [face_fields(kinds, 0, side) for side in (LO, HI)]
        self.slot = [{key: i for i, key in enumerate(fields)} for fields in self.ax]
        self.fields = len(self.ax[LO])
        corner, rest = [], []
        for a, sign in ((1, 1), (0, -1)):
            for side in (LO, HI):
                for kind, q in face_fields(kinds, 1, side):
                    leaves = VELOCITY[q][0] == (-sign if kind == ADJ else sign)
                    key = (side, kind, q, a)
                    (corner if kind == FLAG or leaves else rest).append(key)
        self.corner_blocks = -(-len(corner) // 8)
        self.blocks = self.corner_blocks + -(-len(rest) // 8)
        self.place = {key: (i // 8, i % 8) for i, key in enumerate(corner)}
        self.place.update({key: (self.corner_blocks + i // 8, i % 8) for i, key in enumerate(rest)})


FIRST = Layout((POST, ADJ, FACTOR, FLAG))
SECOND = Layout((POST, ADJ))


def pairs_of(values):
    sums = [values[q] + values[q + 1] for q in range(1, 19, 2)]
    diffs = [values[q] - values[q + 1] for q in range(1, 19, 2)]
    return sums, diffs


def projections(vec):
    va, vt, vr = vec
    return [va, vt, vr, va + vt, va - vt, va + vr, va - vr, vt + vr, vt - vr]


def linearise(pops, porous, types, regions):
    sums, diffs = pairs_of(pops)
    s0, s1, s2, s3, s4, s5, s6, s7, s8 = sums
    d0, d1, d2, d3, d4, d5, d6, d7, d8 = diffs
    at, ar, tr = s3 + s4, s5 + s6, s7 + s8
    rho = pops[0] + ((s0 + s1) + (s2 + at)) + (ar + tr)
    ma = (d0 + (d3 + d4)) + (d5 + d6)
    mt = (d1 + (d3 - d4)) + (d7 + d8)
    mr = (d2 + (d5 - d6)) + (d7 - d8)
    inv = 1.0 / rho
    ua, ut, ur = ma * inv, mt * inv, mr * inv
    third = rho * (1.0 / 3.0)
    paa = (s0 + at + ar - third) - ma * ua
    ptt = (s1 + at + tr - third) - mt * ut
    prr = (s2 + ar + tr - third) - mr * ur
    pat = (s3 - s4) - ma * ut
    par = (s5 - s6) - ma * ur
    ptr = (s7 - s8) - mt * ur
    square = (paa * paa + ptt * ptt + prr * prr) + 2.0 * (pat * pat + par * par + ptr * ptr) + 0.0001
    inv_root = lax.rsqrt(square)
    shear = 1.5 * (square * inv_root) * inv
    shifted = shear + 0.01
    viscous = 0.02 * jnp.exp((0.7 - 1.0) * jnp.log(shifted))
    omega = 1.0 / (0.5 + 3.0 * viscous)
    relaxed = (types != 2) & (types != 3)
    kappa = jnp.where(regions > 0, porous, 0.0)
    return dict(
        rho=rho,
        inv=inv,
        u=(ua, ut, ur),
        p=(paa, ptt, prr, pat, par, ptr),
        inv_root=inv_root,
        shear=shear,
        shifted=shifted,
        viscous=viscous,
        omega=omega,
        relaxed=relaxed,
        kappa=kappa,
        keep=jnp.where(relaxed, 1.0 - omega, 0.0),
        design=jnp.where(relaxed & (regions > 0), 1.0, 0.0),
        inlet=types == 2,
        outlet=types == 3,
    )


def collide(pops, lin):
    rho, relaxed, inlet = lin["rho"], lin["relaxed"], lin["inlet"]
    ua, ut, ur = (jnp.where(inlet, speed, x) for x, speed in zip(lin["u"], INLET_SPEED))
    scale = jnp.where(relaxed, (lin["omega"] - lin["kappa"]) * rho, 1.0)
    rest = jnp.where(relaxed, lin["kappa"] * rho, 0.0)
    keep = lin["keep"]
    still = 1.0 - 1.5 * (ua * ua + ut * ut + ur * ur)
    post = [keep * pops[0] + (1.0 / 3.0) * (scale * still + rest)]
    for i, cu in enumerate(projections((ua, ut, ur))):
        weight = W_AXIS if i < 3 else W_EDGE
        even = weight * (scale * (still + 4.5 * cu * cu) + rest)
        odd = (3.0 * weight) * (scale * cu)
        post.append(keep * pops[1 + 2 * i] + (even + odd))
        post.append(keep * pops[2 + 2 * i] + (even - odd))
    return post


def pull_back(back, pops, lin):
    sums, diffs = pairs_of(back)
    s0, s1, s2, s3, s4, s5, s6, s7, s8 = sums
    d0, d1, d2, d3, d4, d5, d6, d7, d8 = diffs
    at, ar, tr = s3 + s4, s5 + s6, s7 + s8
    b0 = (1.0 / 3.0) * back[0] + W_AXIS * (s0 + s1 + s2) + W_EDGE * (at + ar + tr)
    ba = W_AXIS * d0 + W_EDGE * ((d3 + d4) + (d5 + d6))
    bt = W_AXIS * d1 + W_EDGE * ((d3 - d4) + (d7 + d8))
    br = W_AXIS * d2 + W_EDGE * ((d5 - d6) + (d7 - d8))
    baa = W_AXIS * s0 + W_EDGE * (at + ar)
    btt = W_AXIS * s1 + W_EDGE * (at + tr)
    brr = W_AXIS * s2 + W_EDGE * (ar + tr)
    bat, bar, btr = W_EDGE * (s3 - s4), W_EDGE * (s5 - s6), W_EDGE * (s7 - s8)
    along = back[0] * pops[0]
    for q in range(1, 19):
        along = along + back[q] * pops[q]
    rho, inv = lin["rho"], lin["inv"]
    ua, ut, ur = lin["u"]
    qa = baa * ua + bat * ut + bar * ur
    qt = bat * ua + btt * ut + btr * ur
    qr = bar * ua + btr * ut + brr * ur
    uu = ua * ua + ut * ut + ur * ur
    slope = 3.0 * (ua * ba + ut * bt + ur * br) + 4.5 * (ua * qa + ut * qt + ur * qr) - 1.5 * (uu * b0)
    full = b0 + slope
    sens = -(lin["design"] * (rho * slope))
    relaxed, omega = lin["relaxed"], lin["omega"]
    shear_bar = (rho * full - along) * (omega * omega) * (0.9 * lin["viscous"]) / lin["shifted"]
    shear_bar = jnp.where(relaxed, shear_bar, 0.0)
    z = shear_bar * (1.5 * inv) * lin["inv_root"]
    maa, mtt, mrr, mat, mar, mtr = (z * x for x in lin["p"])
    scale = jnp.where(relaxed, omega - lin["kappa"], jnp.where(lin["outlet"], inv, 0.0))
    la = maa * ua + mat * ut + mar * ur
    lt = mat * ua + mtt * ut + mtr * ur
    lr = mar * ua + mtr * ut + mrr * ur
    va = scale * (3.0 * (ba - b0 * ua) + 9.0 * qa) - 2.0 * la
    vt = scale * (3.0 * (bt - b0 * ut) + 9.0 * qt) - 2.0 * lt
    vr = scale * (3.0 * (br - b0 * ur) + 9.0 * qr) - 2.0 * lr
    total = jnp.where(relaxed, lin["kappa"] * b0 + scale * full, 0.0)
    total = total - shear_bar * lin["shear"] * inv - (1.0 / 3.0) * (maa + mtt + mrr)
    total = total - ((la + va) * ua + (lt + vt) * ut + (lr + vr) * ur)
    keep = lin["keep"]
    taa, ttt, trr = total + maa, total + mtt, total + mrr
    sat, sar, str_ = taa + mtt, taa + mrr, ttt + mrr
    mat2, mar2, mtr2 = 2.0 * mat, 2.0 * mar, 2.0 * mtr
    evens = [taa, ttt, trr, sat + mat2, sat - mat2, sar + mar2, sar - mar2, str_ + mtr2, str_ - mtr2]
    result = [keep * back[0] + total]
    for i, odd in enumerate(projections((va, vt, vr))):
        result.append(keep * back[1 + 2 * i] + (evens[i] + odd))
        result.append(keep * back[2 + 2 * i] + (evens[i] - odd))
    return result, sens


def face_rows(slot):
    return slice(16 * slot, 16 * slot + 16)


def by_parity(parity_ref, body):
    for parity in (0, 1):
        pl.when(parity_ref[0] == parity)(functools.partial(body, parity))


def near_rows(parity, rows_a):
    return (range(1, rows_a), 0) if parity == 0 else (range(rows_a - 1), rows_a - 1)


class Fields:
    def __init__(self, layout, own, parity, e=None, o=None, real=None, t=None, ed=None, od=None):
        self.layout, self.own, self.t = layout, own, t
        self.rows_a = own[POST].shape[1]
        sides = [(o, od, real), (e, ed, None)]
        self.sides = sides if parity == 0 else sides[::-1]

    def row(self, kind, q, a):
        if 0 <= a < self.rows_a:
            return self.own[FLAG][a] if kind == FLAG else self.own[kind][q, a]
        if kind == FACTOR:
            weight, *velocity = (self.row(MOTION, k, a) for k in range(4))
            return porosity_factor(q, weight, velocity)
        message, _, real = self.sides[a >= 0]
        slot = self.layout.slot[HI if a < 0 else LO][(kind, q)]
        return self.masked(kind, message[face_rows(slot), :], real)

    def masked(self, kind, value, real):
        if real is None or kind not in (ADJ, FLAG):
            return value
        return jnp.where(real == 1, value, 0.0)

    def row_label(self, a):
        row = 16 * self.layout.slot[HI if a < 0 else LO][(MOTION, 0)]
        return self.sides[a >= 0][0][row : row + 1, 0:1]

    def edge_label(self, side, a):
        sa = 1 if a < 0 else -1 if a >= self.rows_a else 0
        q = VELOCITY.index((sa, -1 if side == LO else 1, 0))
        return self.edge(side, FACTOR, q, a)[:, 0:1]

    def message(self, key, a):
        block, i = self.layout.place[key]
        if 0 <= a < self.rows_a:
            return self.t[block, i : i + 1, :]
        axial, corners, real = self.sides[a >= 0]
        if corners is None:
            row = 16 * self.layout.fields + 8 * block + i
            return self.masked(key[1], axial[row : row + 1, :], real)
        return self.masked(key[1], corners[i : i + 1, :], real)

    def edge(self, side, kind, q, a):
        row = self.rows_a - 1 if a < 0 else 0 if a >= self.rows_a else a
        return self.message((side, kind, q, row), a)

    def moved(self, kind, q, a, shift):
        sa, st, sr = shift
        value = self.row(kind, q, a + sa)
        rows_t, rows_r = value.shape
        if st:
            value = pltpu.roll(value, (-st) % rows_t, 0)
            beyond = self.edge(LO if st > 0 else HI, kind, q, a + sa)
            at_edge = lax.broadcasted_iota(jnp.int32, value.shape, 0) == (rows_t - 1 if st > 0 else 0)
            value = jnp.where(at_edge, beyond, value)
        if sr:
            value = pltpu.roll(value, (-sr) % rows_r, 1)
        return value


def cells(own, kind, q, a):
    return own[FLAG].at[a] if kind == FLAG else own[kind].at[q, a]


def stream_row(fields, a, around, result):
    post = fields.own[POST]
    result[0, a] = post[0, a]
    for q in range(1, 19):
        moved = fields.moved(POST, q, a, tuple(-c for c in VELOCITY[q]))
        result[q, a] = jnp.where(around[q - 1, a] > 0, moved, post[OPPOSITE[q], a])


def stream_adjoint_row(fields, a, centre, around, result):
    adj = fields.own[ADJ]
    result[0, a] = adj[0, a]
    for q in range(1, 19):
        opp = OPPOSITE[q]
        ahead = centre * fields.moved(ADJ, opp, a, tuple(-c for c in VELOCITY[q]))
        result[opp, a] = ahead + (1.0 - around[q - 1, a]) * adj[q, a]


def labelled(value, label):
    lanes = lax.broadcasted_iota(jnp.int32, value.shape, 1)
    return jnp.where(lanes == 0, label, value)


def pack_azimuthal(layout, own, rows, t_ref, label=None):
    rows_t = own[POST].shape[2]
    for (side, kind, q, a), (block, i) in layout.place.items():
        if a in rows:
            t = 0 if side == LO else rows_t - 1
            row = cells(own, kind, q, a)[t : t + 1, :]
            t_ref[block, i : i + 1, :] = labelled(row, label) if kind == FACTOR else row


def pack_face(layout, own, side, message, label=None):
    a = 0 if side == LO else own[POST].shape[1] - 1
    for slot, (kind, q) in enumerate(layout.ax[side]):
        value = cells(own, kind, q, a)[...]
        if (kind, q) == (MOTION, 0):
            value = labelled(value, label)
        message[face_rows(slot), :] = value


def near_side(parity):
    return (HI, LO) if parity == 0 else (LO, HI)


def chunks(rows_a, shape, body):
    counts = (len(rows_a), shape[1] // 8, shape[2] // 128)

    def step(i, carry):
        a = rows_a[0] + i // (counts[1] * counts[2])
        t = pl.multiple_of((i // counts[2]) % counts[1] * 8, 8)
        r = pl.multiple_of(i % counts[2] * 128, 128)
        body((a, pl.ds(t, 8), pl.ds(r, 128)))
        return carry

    lax.fori_loop(0, counts[0] * counts[1] * counts[2], step, 0, unroll=4)


def load(ref, where):
    return [ref[(q,) + where] for q in range(19)]


def store(ref, where, values):
    for q in range(19):
        ref[(q,) + where] = values[q]


def label_of(regions):
    label = jnp.max(jnp.max(regions[...], axis=0), axis=(0, 1), keepdims=True)
    return label.astype(jnp.float32)


def porosity_factor(q, weight, velocity):
    ua, ut, ur = velocity
    pair = (q - 1) // 2
    cu = projections(velocity)[pair]
    scaled = (W_AXIS if pair < 3 else W_EDGE) * weight
    still = -1.5 * (ua * ua + ut * ut + ur * ur)
    return scaled * (still + 4.5 * cu * cu + (3.0 * cu if q % 2 else -3.0 * cu))


def factor_weight(lin):
    return -(lin["design"] * lin["rho"])


def porosity_factors(lin):
    ua, ut, ur = lin["u"]
    weight = factor_weight(lin)
    still = -1.5 * (ua * ua + ut * ut + ur * ur)
    result = [(1.0 / 3.0) * weight * still]
    for i, cu in enumerate(projections((ua, ut, ur))):
        scaled = (W_AXIS if i < 3 else W_EDGE) * weight
        even, odd = scaled * (still + 4.5 * cu * cu), 3.0 * scaled * cu
        result += [even + odd, even - odd]
    return result


def first_kernel(
    parity_ref, pops_hbm, seed_hbm, porous_hbm, types_hbm, regions_hbm,
    post, factors, e_out, o_out, t_out, ed_out, od_out, flags,
    pops, seed, porous, types, regions, motion, sems,
):
    rows_a, _, rows_r = porous.shape
    pairs = [(types_hbm, types), (regions_hbm, regions), (porous_hbm, porous)]
    pairs += [(pops_hbm.at[:, a], pops.at[:, a]) for a in range(rows_a)] + [(seed_hbm, seed)]
    loads = [pltpu.make_async_copy(*pair, sems.at[i]) for i, pair in enumerate(pairs)]
    for copy in loads:
        copy.start()
    for copy in loads[:3]:
        copy.wait()
    flags[...] = jnp.where(types[...] != 1, 1.0, 0.0)
    label = label_of(regions)

    def body(where):
        values = load(pops, where)
        lin = linearise(values, porous[where], types[where], regions[where])
        store(post, where, collide(values, lin))
        store(factors, where, porosity_factors(lin))
        for k, value in enumerate([factor_weight(lin), *lin["u"]]):
            motion[(k,) + where] = value

    for a in range(rows_a):
        loads[3 + a].wait()
        chunks([a], porous.shape, body)
    loads[-1].wait()
    own = {POST: post, ADJ: seed, FACTOR: factors, MOTION: motion, FLAG: flags}
    pack_azimuthal(FIRST, own, range(rows_a), t_out, label)

    def run(parity):
        near, far = near_side(parity)
        pack_face(FIRST, own, near, e_out, label)
        pack_face(FIRST, own, far, o_out, label)
        ed_out[...] = t_out[parity]
        od_out[...] = t_out[1 - parity]

    by_parity(parity_ref, run)


def second_rows(fields, rows, cell_refs, results, scratch):
    porous, types, regions = cell_refs
    post_next, adj, sens, around = results
    state, back = scratch
    for a in rows:
        for q in range(1, 19):
            around[q - 1, a] = fields.moved(FLAG, 0, a, tuple(-c for c in VELOCITY[q]))
        stream_row(fields, a, around, state)
        stream_adjoint_row(fields, a, fields.own[FLAG][a], around, back)

    def body(where):
        values = load(state, where)
        lin = linearise(values, porous[where], types[where], regions[where])
        store(post_next, where, collide(values, lin))
        result, partial_sens = pull_back(load(back, where), values, lin)
        store(adj, where, result)
        sens[where] = partial_sens

    chunks(rows, porous.shape, body)


def second_near_kernel(
    parity_ref, post, seed, factors, flags, porous, types, regions, e, t, ed,
    post_next, adj, sens, around, e_out, t_out, partial, state, back, parts,
):
    def run(parity):
        own = {POST: post, ADJ: seed, FACTOR: factors, FLAG: flags}
        fields = Fields(FIRST, own, parity, e=e, t=t, ed=ed)
        rows, _ = near_rows(parity, porous.shape[0])
        results = (post_next, adj, sens, around)
        second_rows(fields, rows, (porous, types, regions), results, (state, back))
        own = {POST: post_next, ADJ: adj}
        pack_face(SECOND, own, near_side(parity)[0], e_out)
        pack_azimuthal(SECOND, own, rows, t_out)
        partial[...] = region_sums(fields, rows, adj, sens, around, regions, parts)

    by_parity(parity_ref, run)


def second_far_kernel(
    parity_ref, real_ref, post_near, adj_near, sens_near, around_near, t_near, partial_near,
    post, seed, factors, flags, porous, types, regions, o, t, od,
    post_next, adj, sens, around, t_out, o_out, partial, state, back, parts,
):
    def run(parity):
        own = {POST: post, ADJ: seed, FACTOR: factors, FLAG: flags}
        fields = Fields(FIRST, own, parity, o=o, real=real_ref[0], t=t, od=od)
        _, row = near_rows(parity, porous.shape[0])
        results = (post_next, adj, sens, around)
        second_rows(fields, [row], (porous, types, regions), results, (state, back))
        own = {POST: post_next, ADJ: adj}
        pack_face(SECOND, own, near_side(parity)[1], o_out)
        pack_azimuthal(SECOND, own, [row], t_out)
        sums = region_sums(fields, [row], adj, sens, around, regions, parts)
        partial[...] = partial_near[...] + sums

    by_parity(parity_ref, run)


def region_sums(fields, rows, adj, sens, around, regions, parts):
    factors = fields.own[FACTOR]
    rows_a, rows_t, rows_r = sens.shape
    sums = {}
    for a in rows:
        sums.setdefault((0, 0), []).extend([sens[a], factors[0, a] * adj[0, a]])
        for q in range(1, 19):
            behind = tuple(-c for c in VELOCITY[q])
            open_, value = around[q - 1, a], adj[q, a]
            sums[(0, 0)].append(jnp.where(open_ > 0, 0.0, factors[OPPOSITE[q], a]) * value)
            term = jnp.where(open_ > 0, fields.moved(FACTOR, q, a, behind), 0.0) * value
            from_a = a + behind[0]
            beyond = -1 if from_a < 0 else 1 if from_a >= rows_a else 0
            sums.setdefault((beyond, behind[1]), []).append(term)
    at_t = lax.broadcasted_iota(jnp.int32, (rows_t, rows_r), 0)
    lines = []
    for beyond in sorted({key[0] for key in sums}):
        low, centre, high = (functools.reduce(jnp.add, sums[(beyond, st)]) for st in (-1, 0, 1))
        inner = centre + jnp.where(at_t == 0, 0.0, low) + jnp.where(at_t == rows_t - 1, 0.0, high)
        a = {-1: -1, 0: 0, 1: rows_a}[beyond]
        label = fields.row_label(a) if beyond else label_of(regions)
        lines.append((jnp.sum(inner, axis=0, keepdims=True), label))
        a = a if beyond else rows[0]
        lines.append((high[rows_t - 1 : rows_t], fields.edge_label(LO, a)))
        lines.append((low[0:1], fields.edge_label(HI, a)))
    parts[...] = jnp.zeros_like(parts)
    for i, (value, label) in enumerate(lines):
        parts[0, i : i + 1, :] = value
        parts[1, i : i + 1, :] = jnp.broadcast_to(label, (1, rows_r))
    lanes = lax.broadcasted_iota(jnp.int32, parts.shape[1:], 1) + 1
    total = jnp.sum(parts[0], axis=1, keepdims=True)
    chosen = jnp.where(lanes == parts[1].astype(jnp.int32), total, 0.0)
    return jnp.sum(chosen, axis=0, keepdims=True)


def corner_kernel(e, o, t, total, e_out, o_out):
    row = 16 * SECOND.fields
    for out in (e_out, o_out):
        out[row : row + 8, :] = t[0]
    e_out[row + 8 : row + 16, :] = jnp.broadcast_to(total[...], (8, e_out.shape[1]))


def third_rows(fields, rows, cell_refs, own_refs, hbm, sens, scratch, sems):
    porous, types, regions = cell_refs
    around, flags, pops, sens_one = own_refs
    final, result, back = scratch
    stores = []

    def send(source, target, a):
        stores.append(pltpu.make_async_copy(source.at[:, a], target.at[:, a], sems.at[len(stores)]))
        stores[-1].start()

    def body(where):
        values = load(pops, where)
        lin = linearise(values, porous[where], types[where], regions[where])
        adjoint, partial_sens = pull_back(load(back, where), values, lin)
        store(result, where, adjoint)
        sens[where] = partial_sens + sens_one[where]

    for a in rows:
        stream_row(fields, a, around, final)
        send(final, hbm[0], a)
        stream_adjoint_row(fields, a, flags[a], around, back)
        chunks([a], porous.shape, body)
        send(result, hbm[1], a)
    for copy in stores:
        copy.wait()


def third_near_kernel(
    parity_ref, post, adj, flags, around, pops, porous, types, regions, sens_one, e, t,
    final_hbm, result_hbm, sens, final, result, back, sems,
):
    def run(parity):
        fields = Fields(SECOND, {POST: post, ADJ: adj}, parity, e=e, t=t)
        rows, _ = near_rows(parity, porous.shape[0])
        third_rows(
            fields, rows, (porous, types, regions), (around, flags, pops, sens_one),
            (final_hbm, result_hbm), sens, (final, result, back), sems,
        )

    by_parity(parity_ref, run)


def third_far_kernel(
    parity_ref, real_ref, final_near, result_near, sens_near,
    post, adj, flags, around, pops, porous, types, regions, sens_one, o, t,
    final_hbm, result_hbm, sens, final, result, back, sems,
):
    def run(parity):
        fields = Fields(SECOND, {POST: post, ADJ: adj}, parity, o=o, real=real_ref[0], t=t)
        rows, row = near_rows(parity, porous.shape[0])
        for a in rows:
            sens[a] = sens_near[a]
        third_rows(
            fields, [row], (porous, types, regions), (around, flags, pops, sens_one),
            (final_hbm, result_hbm), sens, (final, result, back), sems,
        )

    by_parity(parity_ref, run)


VMEM, HBM = pltpu.VMEM, pltpu.HBM


def call(body, in_spaces, outs, scratch, *arrays, aliases=None, cost=None):
    return pl.pallas_call(
        body,
        out_shape=[jax.ShapeDtypeStruct(shape, dtype) for shape, dtype, _ in outs],
        in_specs=[pl.BlockSpec(memory_space=space) for space in in_spaces],
        out_specs=[pl.BlockSpec(memory_space=space) for _, _, space in outs],
        scratch_shapes=scratch,
        input_output_aliases=aliases or {},
        cost_estimate=cost,
        compiler_params=pltpu.CompilerParams(vmem_limit_bytes=16 * 1024 * 1024),
    )(*arrays)


def axial_pairs(flip, shift_t=0):
    size_a, size_t = lax.axis_size("ax"), lax.axis_size("az")
    pairs = []
    for a in range(size_a):
        partner = ((a + flip) ^ 1) - flip
        for t in range(size_t):
            if 0 <= partner < size_a:
                pairs.append((a * size_t + t, partner * size_t + (t + shift_t) % size_t))
            elif shift_t:
                pairs.append((a * size_t + t, a * size_t + (t + shift_t) % size_t))
            elif size_t % 2 == 0:
                pairs.append((a * size_t + t, a * size_t + (t ^ 1)))
    return pairs


def from_both_sectors(message, high_rows, send):
    if lax.axis_size("az") == 2:
        return send(message, 1)
    return jnp.where(jnp.asarray(high_rows), send(message, 1), send(message, -1))


def high_rows(layout):
    rows = np.zeros((layout.blocks, 8, 1), bool)
    for key, (block, i) in layout.place.items():
        rows[block, i] = key[0] == HI
    return rows


def send_azimuthal(layout, message):
    size = lax.axis_size("az")

    def send(x, shift):
        return lax.ppermute(x, "az", [(i, (i + shift) % size) for i in range(size)])

    return from_both_sectors(message, high_rows(layout), send)


def send_axial(message, flip):
    return lax.ppermute(message, ("ax", "az"), axial_pairs(flip))


def send_diagonal(message, flip):
    def send(x, shift):
        return lax.ppermute(x, ("ax", "az"), axial_pairs(flip, shift))

    return from_both_sectors(message, high_rows(FIRST)[0], send)


def from_partner(x, flip_a, flip_t):
    size_a, size_t = lax.axis_size("ax"), lax.axis_size("az")
    pairs = [
        (a * size_t + t, (a ^ flip_a) * size_t + (t ^ flip_t))
        for a in range(size_a)
        for t in range(size_t)
    ]
    return lax.ppermute(x, ("ax", "az"), pairs)


def shards(initial, adjoint_seed, porosity, cell_type, region):
    cells_ = porosity.shape
    pops = (19,) + cells_
    wide = cells_[2]
    f32, i32 = jnp.float32, jnp.int32
    size_a, size_t = lax.axis_size("ax"), lax.axis_size("az")
    index = lax.axis_index("ax")
    real = (index != 0) & (index != size_a - 1)
    place = ((index % 2).astype(i32).reshape(1), real.astype(i32).reshape(1))

    def axial(layout, more):
        return ((16 * layout.fields + more, wide), f32, VMEM)

    def azimuthal(layout):
        return [((layout.blocks, 8, wide), f32, VMEM)]

    inputs = (initial, adjoint_seed, porosity, cell_type, region)
    post, factors, e, o, t, ed, od, flags = call(
        first_kernel,
        [pltpu.SMEM] + [HBM] * 5,
        [(pops, f32, VMEM), (pops, f32, VMEM)] + [axial(FIRST, 0)] * 2 + azimuthal(FIRST)
        + [((8, wide), f32, VMEM)] * 2 + [(cells_, f32, VMEM)],
        [VMEM(x.shape, x.dtype) for x in inputs]
        + [VMEM((4,) + cells_, f32), pltpu.SemaphoreType.DMA((4 + cells_[0],))],
        place[0],
        *(pltpu.with_memory_space_constraint(x, HBM) for x in inputs),
    )
    e, o = send_axial(e, 0), send_axial(o, 1)
    t_near = send_azimuthal(FIRST, t)
    ed, od = send_diagonal(ed, 0), send_diagonal(od, 1)
    layers = [(pops, f32, VMEM), (pops, f32, VMEM), (cells_, f32, VMEM), ((18,) + cells_, f32, VMEM)]
    inside = (post, adjoint_seed, factors, flags, porosity, cell_type, region)
    row = [((1, wide), f32, VMEM)]
    scratch = [VMEM(pops, f32), VMEM(pops, f32), VMEM((2, 8, wide), f32)]
    *near, e, t, total = call(
        second_near_kernel,
        [pltpu.SMEM] + [VMEM] * 10,
        layers + [axial(SECOND, 16)] + azimuthal(SECOND) + row,
        scratch,
        place[0], *inside, e, t_near, ed,
    )
    post, adj, sens_one, around, t, o, total = call(
        second_far_kernel,
        [pltpu.SMEM] * 2 + [VMEM] * 16,
        layers + azimuthal(SECOND) + [axial(SECOND, 8)] + row,
        scratch,
        *place, *near, t, total, *inside, o, t_near, od,
        aliases={2: 0, 3: 1, 4: 2, 5: 3, 6: 4},
    )
    t_near = send_azimuthal(SECOND, t)
    halving = size_a >= 4 and not (size_a & (size_a - 1) or size_t & (size_t - 1))
    flips = [((1 << k) | 1, 0) for k in range(size_a.bit_length() - 3, 0, -1)]
    if halving:
        total = total + from_partner(total, size_a // 2 | 1, 0)
        flips = [(1, 1 << k) for k in range(size_t.bit_length() - 1)] + flips
    e, o = call(
        corner_kernel,
        [VMEM] * 4,
        [axial(SECOND, 16), axial(SECOND, 8)],
        [],
        e, o, t_near, total,
        aliases={0: 0, 1: 1},
    )
    e, o = send_axial(e, 0), send_axial(o, 1)
    stored = [(pops, f32, HBM), (pops, f32, HBM), (cells_, f32, VMEM)]
    third_scratch = [VMEM(pops, f32)] * 3 + [pltpu.SemaphoreType.DMA((2 * cells_[0],))]
    inside = (post, adj, flags, around, initial, porosity, cell_type, region, sens_one)
    near = call(
        third_near_kernel,
        [pltpu.SMEM] + [VMEM] * 11,
        stored,
        third_scratch,
        place[0], *inside, e, t_near,
    )
    if halving:
        row = 16 * SECOND.fields + 8
        totals = total + e[row : row + 1]
        for flip in flips:
            if flip == flips[-1]:
                totals, _ = lax.optimization_barrier((totals, (o, near[2])))
            totals = totals + from_partner(totals, *flip)
    else:
        totals = lax.psum(total, ("ax", "az"))
    final, adjoint, sensitivity = call(
        third_far_kernel,
        [pltpu.SMEM] * 2 + [HBM] * 2 + [VMEM] * 12,
        stored,
        third_scratch,
        *place, *near, *inside, o, t_near,
        aliases={2: 0, 3: 1},
    )
    return final, adjoint, sensitivity, totals[0, : size_a * size_t // 4]


def solution(mesh):
    return jax.shard_map(
        shards,
        mesh=mesh,
        in_specs=(
            P(None, "ax", "az", None),
            P(None, "ax", "az", None),
            P("ax", "az", None),
            P("ax", "az", None),
            P("ax", "az", None),
        ),
        out_specs=(P(None, "ax", "az", None), P(None, "ax", "az", None), P("ax", "az", None), P()),
        check_vma=False,
    )
```

```python
import functools

import jax
import jax.numpy as jnp
import numpy as np
from jax import lax
from jax.experimental import pallas as pl
from jax.experimental.pallas import tpu as pltpu
from jax.sharding import PartitionSpec as P

VELOCITY = [
    (0, 0, 0),
    (1, 0, 0),
    (-1, 0, 0),
    (0, 1, 0),
    (0, -1, 0),
    (0, 0, 1),
    (0, 0, -1),
    (1, 1, 0),
    (-1, -1, 0),
    (1, -1, 0),
    (-1, 1, 0),
    (1, 0, 1),
    (-1, 0, -1),
    (1, 0, -1),
    (-1, 0, 1),
    (0, 1, 1),
    (0, -1, -1),
    (0, 1, -1),
    (0, -1, 1),
]
OPPOSITE = [0, 2, 1, 4, 3, 6, 5, 8, 7, 10, 9, 12, 11, 14, 13, 16, 15, 18, 17]
INLET_SPEED = (0.05, 0.05, 0.0)
W_AXIS = 1.0 / 18.0
W_EDGE = 1.0 / 36.0


def moving(axis, sign):
    return [q for q in range(19) if VELOCITY[q][axis] == sign]


LO, HI = 0, 1
POST, ADJ, FACTOR, FLAG, MOTION = 0, 1, 2, 3, 4


def face_fields(kinds, axis, side):
    sign = -1 if side == LO else 1
    fields = []
    for kind in kinds:
        if kind == FLAG:
            fields.append((FLAG, 0))
        elif kind == FACTOR and axis == 0:
            fields += [(MOTION, k) for k in range(4)]
        else:
            fields += [(kind, q) for q in moving(axis, -sign if kind == ADJ else sign)]
    return fields


class Layout:
    def __init__(self, kinds):
        self.ax = [face_fields(kinds, 0, side) for side in (LO, HI)]
        self.slot = [{key: i for i, key in enumerate(fields)} for fields in self.ax]
        self.fields = len(self.ax[LO])
        corner, rest = [], []
        for a, sign in ((1, 1), (0, -1)):
            for side in (LO, HI):
                for kind, q in face_fields(kinds, 1, side):
                    leaves = VELOCITY[q][0] == (-sign if kind == ADJ else sign)
                    key = (side, kind, q, a)
                    (corner if kind == FLAG or leaves else rest).append(key)
        self.corner_blocks = -(-len(corner) // 8)
        self.blocks = self.corner_blocks + -(-len(rest) // 8)
        self.place = {key: (i // 8, i % 8) for i, key in enumerate(corner)}
        self.place.update({key: (self.corner_blocks + i // 8, i % 8) for i, key in enumerate(rest)})


FIRST = Layout((POST, ADJ, FACTOR, FLAG))
SECOND = Layout((POST, ADJ))


def pairs_of(values):
    sums = [values[q] + values[q + 1] for q in range(1, 19, 2)]
    diffs = [values[q] - values[q + 1] for q in range(1, 19, 2)]
    return sums, diffs


def projections(vec):
    va, vt, vr = vec
    return [va, vt, vr, va + vt, va - vt, va + vr, va - vr, vt + vr, vt - vr]


def linearise(pops, porous, types, regions):
    sums, diffs = pairs_of(pops)
    s0, s1, s2, s3, s4, s5, s6, s7, s8 = sums
    d0, d1, d2, d3, d4, d5, d6, d7, d8 = diffs
    at, ar, tr = s3 + s4, s5 + s6, s7 + s8
    rho = pops[0] + ((s0 + s1) + (s2 + at)) + (ar + tr)
    ma = (d0 + (d3 + d4)) + (d5 + d6)
    mt = (d1 + (d3 - d4)) + (d7 + d8)
    mr = (d2 + (d5 - d6)) + (d7 - d8)
    inv = 1.0 / rho
    ua, ut, ur = ma * inv, mt * inv, mr * inv
    third = rho * (1.0 / 3.0)
    paa = (s0 + at + ar - third) - ma * ua
    ptt = (s1 + at + tr - third) - mt * ut
    prr = (s2 + ar + tr - third) - mr * ur
    pat = (s3 - s4) - ma * ut
    par = (s5 - s6) - ma * ur
    ptr = (s7 - s8) - mt * ur
    square = (paa * paa + ptt * ptt + prr * prr) + 2.0 * (pat * pat + par * par + ptr * ptr) + 0.0001
    inv_root = lax.rsqrt(square)
    shear = 1.5 * (square * inv_root) * inv
    shifted = shear + 0.01
    viscous = 0.02 * jnp.exp((0.7 - 1.0) * jnp.log(shifted))
    omega = 1.0 / (0.5 + 3.0 * viscous)
    relaxed = (types != 2) & (types != 3)
    kappa = jnp.where(regions > 0, porous, 0.0)
    return dict(
        rho=rho,
        inv=inv,
        u=(ua, ut, ur),
        p=(paa, ptt, prr, pat, par, ptr),
        inv_root=inv_root,
        shear=shear,
        shifted=shifted,
        viscous=viscous,
        omega=omega,
        relaxed=relaxed,
        kappa=kappa,
        keep=jnp.where(relaxed, 1.0 - omega, 0.0),
        design=jnp.where(relaxed & (regions > 0), 1.0, 0.0),
        inlet=types == 2,
        outlet=types == 3,
    )


def collide(pops, lin):
    rho, relaxed, inlet = lin["rho"], lin["relaxed"], lin["inlet"]
    ua, ut, ur = (jnp.where(inlet, speed, x) for x, speed in zip(lin["u"], INLET_SPEED))
    scale = jnp.where(relaxed, (lin["omega"] - lin["kappa"]) * rho, 1.0)
    rest = jnp.where(relaxed, lin["kappa"] * rho, 0.0)
    keep = lin["keep"]
    still = 1.0 - 1.5 * (ua * ua + ut * ut + ur * ur)
    post = [keep * pops[0] + (1.0 / 3.0) * (scale * still + rest)]
    for i, cu in enumerate(projections((ua, ut, ur))):
        weight = W_AXIS if i < 3 else W_EDGE
        even = weight * (scale * (still + 4.5 * cu * cu) + rest)
        odd = (3.0 * weight) * (scale * cu)
        post.append(keep * pops[1 + 2 * i] + (even + odd))
        post.append(keep * pops[2 + 2 * i] + (even - odd))
    return post


def pull_back(back, pops, lin):
    sums, diffs = pairs_of(back)
    s0, s1, s2, s3, s4, s5, s6, s7, s8 = sums
    d0, d1, d2, d3, d4, d5, d6, d7, d8 = diffs
    at, ar, tr = s3 + s4, s5 + s6, s7 + s8
    b0 = (1.0 / 3.0) * back[0] + W_AXIS * (s0 + s1 + s2) + W_EDGE * (at + ar + tr)
    ba = W_AXIS * d0 + W_EDGE * ((d3 + d4) + (d5 + d6))
    bt = W_AXIS * d1 + W_EDGE * ((d3 - d4) + (d7 + d8))
    br = W_AXIS * d2 + W_EDGE * ((d5 - d6) + (d7 - d8))
    baa = W_AXIS * s0 + W_EDGE * (at + ar)
    btt = W_AXIS * s1 + W_EDGE * (at + tr)
    brr = W_AXIS * s2 + W_EDGE * (ar + tr)
    bat, bar, btr = W_EDGE * (s3 - s4), W_EDGE * (s5 - s6), W_EDGE * (s7 - s8)
    along = back[0] * pops[0]
    for q in range(1, 19):
        along = along + back[q] * pops[q]
    rho, inv = lin["rho"], lin["inv"]
    ua, ut, ur = lin["u"]
    qa = baa * ua + bat * ut + bar * ur
    qt = bat * ua + btt * ut + btr * ur
    qr = bar * ua + btr * ut + brr * ur
    uu = ua * ua + ut * ut + ur * ur
    slope = 3.0 * (ua * ba + ut * bt + ur * br) + 4.5 * (ua * qa + ut * qt + ur * qr) - 1.5 * (uu * b0)
    full = b0 + slope
    sens = -(lin["design"] * (rho * slope))
    relaxed, omega = lin["relaxed"], lin["omega"]
    shear_bar = (rho * full - along) * (omega * omega) * (0.9 * lin["viscous"]) / lin["shifted"]
    shear_bar = jnp.where(relaxed, shear_bar, 0.0)
    z = shear_bar * (1.5 * inv) * lin["inv_root"]
    maa, mtt, mrr, mat, mar, mtr = (z * x for x in lin["p"])
    scale = jnp.where(relaxed, omega - lin["kappa"], jnp.where(lin["outlet"], inv, 0.0))
    la = maa * ua + mat * ut + mar * ur
    lt = mat * ua + mtt * ut + mtr * ur
    lr = mar * ua + mtr * ut + mrr * ur
    va = scale * (3.0 * (ba - b0 * ua) + 9.0 * qa) - 2.0 * la
    vt = scale * (3.0 * (bt - b0 * ut) + 9.0 * qt) - 2.0 * lt
    vr = scale * (3.0 * (br - b0 * ur) + 9.0 * qr) - 2.0 * lr
    total = jnp.where(relaxed, lin["kappa"] * b0 + scale * full, 0.0)
    total = total - shear_bar * lin["shear"] * inv - (1.0 / 3.0) * (maa + mtt + mrr)
    total = total - ((la + va) * ua + (lt + vt) * ut + (lr + vr) * ur)
    keep = lin["keep"]
    taa, ttt, trr = total + maa, total + mtt, total + mrr
    sat, sar, str_ = taa + mtt, taa + mrr, ttt + mrr
    mat2, mar2, mtr2 = 2.0 * mat, 2.0 * mar, 2.0 * mtr
    evens = [taa, ttt, trr, sat + mat2, sat - mat2, sar + mar2, sar - mar2, str_ + mtr2, str_ - mtr2]
    result = [keep * back[0] + total]
    for i, odd in enumerate(projections((va, vt, vr))):
        result.append(keep * back[1 + 2 * i] + (evens[i] + odd))
        result.append(keep * back[2 + 2 * i] + (evens[i] - odd))
    return result, sens


def face_rows(slot):
    return slice(16 * slot, 16 * slot + 16)


def by_parity(parity_ref, body):
    for parity in (0, 1):
        pl.when(parity_ref[0] == parity)(functools.partial(body, parity))


def near_rows(parity, rows_a):
    return (range(1, rows_a), 0) if parity == 0 else (range(rows_a - 1), rows_a - 1)


class Fields:
    def __init__(self, layout, own, parity, e=None, o=None, real=None, t=None, ed=None, od=None):
        self.layout, self.own, self.t = layout, own, t
        self.rows_a = own[POST].shape[1]
        sides = [(o, od, real), (e, ed, None)]
        self.sides = sides if parity == 0 else sides[::-1]

    def row(self, kind, q, a):
        if 0 <= a < self.rows_a:
            return self.own[FLAG][a] if kind == FLAG else self.own[kind][q, a]
        if kind == FACTOR:
            weight, *velocity = (self.row(MOTION, k, a) for k in range(4))
            return porosity_factor(q, weight, velocity)
        message, _, real = self.sides[a >= 0]
        slot = self.layout.slot[HI if a < 0 else LO][(kind, q)]
        return self.masked(kind, message[face_rows(slot), :], real)

    def masked(self, kind, value, real):
        if real is None or kind not in (ADJ, FLAG):
            return value
        return jnp.where(real == 1, value, 0.0)

    def row_label(self, a):
        row = 16 * self.layout.slot[HI if a < 0 else LO][(MOTION, 0)]
        return self.sides[a >= 0][0][row : row + 1, 0:1]

    def edge_label(self, side, a):
        sa = 1 if a < 0 else -1 if a >= self.rows_a else 0
        q = VELOCITY.index((sa, -1 if side == LO else 1, 0))
        return self.edge(side, FACTOR, q, a)[:, 0:1]

    def message(self, key, a):
        block, i = self.layout.place[key]
        if 0 <= a < self.rows_a:
            return self.t[block, i : i + 1, :]
        axial, corners, real = self.sides[a >= 0]
        if corners is None:
            row = 16 * self.layout.fields + 8 * block + i
            return self.masked(key[1], axial[row : row + 1, :], real)
        return self.masked(key[1], corners[i : i + 1, :], real)

    def edge(self, side, kind, q, a):
        row = self.rows_a - 1 if a < 0 else 0 if a >= self.rows_a else a
        return self.message((side, kind, q, row), a)

    def moved(self, kind, q, a, shift):
        sa, st, sr = shift
        value = self.row(kind, q, a + sa)
        rows_t, rows_r = value.shape
        if st:
            value = pltpu.roll(value, (-st) % rows_t, 0)
            beyond = self.edge(LO if st > 0 else HI, kind, q, a + sa)
            at_edge = lax.broadcasted_iota(jnp.int32, value.shape, 0) == (rows_t - 1 if st > 0 else 0)
            value = jnp.where(at_edge, beyond, value)
        if sr:
            value = pltpu.roll(value, (-sr) % rows_r, 1)
        return value


def cells(own, kind, q, a):
    return own[FLAG].at[a] if kind == FLAG else own[kind].at[q, a]


def stream_row(fields, a, around, result):
    post = fields.own[POST]
    result[0, a] = post[0, a]
    for q in range(1, 19):
        moved = fields.moved(POST, q, a, tuple(-c for c in VELOCITY[q]))
        result[q, a] = jnp.where(around[q - 1, a] > 0, moved, post[OPPOSITE[q], a])


def stream_adjoint_row(fields, a, centre, around, result):
    adj = fields.own[ADJ]
    result[0, a] = adj[0, a]
    for q in range(1, 19):
        opp = OPPOSITE[q]
        ahead = centre * fields.moved(ADJ, opp, a, tuple(-c for c in VELOCITY[q]))
        result[opp, a] = ahead + (1.0 - around[q - 1, a]) * adj[q, a]


def labelled(value, label):
    lanes = lax.broadcasted_iota(jnp.int32, value.shape, 1)
    return jnp.where(lanes == 0, label, value)


def pack_azimuthal(layout, own, rows, t_ref, label=None):
    rows_t = own[POST].shape[2]
    for (side, kind, q, a), (block, i) in layout.place.items():
        if a in rows:
            t = 0 if side == LO else rows_t - 1
            row = cells(own, kind, q, a)[t : t + 1, :]
            t_ref[block, i : i + 1, :] = labelled(row, label) if kind == FACTOR else row


def pack_face(layout, own, side, message, label=None):
    a = 0 if side == LO else own[POST].shape[1] - 1
    for slot, (kind, q) in enumerate(layout.ax[side]):
        value = cells(own, kind, q, a)[...]
        if (kind, q) == (MOTION, 0):
            value = labelled(value, label)
        message[face_rows(slot), :] = value


def near_side(parity):
    return (HI, LO) if parity == 0 else (LO, HI)


def chunks(rows_a, shape, body):
    counts = (len(rows_a), shape[1] // 8, shape[2] // 128)

    def step(i, carry):
        a = rows_a[0] + i // (counts[1] * counts[2])
        t = pl.multiple_of((i // counts[2]) % counts[1] * 8, 8)
        r = pl.multiple_of(i % counts[2] * 128, 128)
        body((a, pl.ds(t, 8), pl.ds(r, 128)))
        return carry

    lax.fori_loop(0, counts[0] * counts[1] * counts[2], step, 0, unroll=4)


def load(ref, where):
    return [ref[(q,) + where] for q in range(19)]


def store(ref, where, values):
    for q in range(19):
        ref[(q,) + where] = values[q]


def label_of(regions):
    label = jnp.max(jnp.max(regions[...], axis=0), axis=(0, 1), keepdims=True)
    return label.astype(jnp.float32)


def porosity_factor(q, weight, velocity):
    ua, ut, ur = velocity
    pair = (q - 1) // 2
    cu = projections(velocity)[pair]
    scaled = (W_AXIS if pair < 3 else W_EDGE) * weight
    still = -1.5 * (ua * ua + ut * ut + ur * ur)
    return scaled * (still + 4.5 * cu * cu + (3.0 * cu if q % 2 else -3.0 * cu))


def factor_weight(lin):
    return -(lin["design"] * lin["rho"])


def porosity_factors(lin):
    ua, ut, ur = lin["u"]
    weight = factor_weight(lin)
    still = -1.5 * (ua * ua + ut * ut + ur * ur)
    result = [(1.0 / 3.0) * weight * still]
    for i, cu in enumerate(projections((ua, ut, ur))):
        scaled = (W_AXIS if i < 3 else W_EDGE) * weight
        even, odd = scaled * (still + 4.5 * cu * cu), 3.0 * scaled * cu
        result += [even + odd, even - odd]
    return result


def first_kernel(
    parity_ref, pops_hbm, seed_hbm, porous_hbm, types_hbm, regions_hbm,
    post, factors, e_out, o_out, t_out, ed_out, od_out, flags,
    pops, seed, porous, types, regions, motion, sems,
):
    rows_a, _, rows_r = porous.shape
    pairs = [(types_hbm, types), (regions_hbm, regions), (porous_hbm, porous)]
    pairs += [(pops_hbm.at[:, a], pops.at[:, a]) for a in range(rows_a)] + [(seed_hbm, seed)]
    loads = [pltpu.make_async_copy(*pair, sems.at[i]) for i, pair in enumerate(pairs)]
    for copy in loads:
        copy.start()
    for copy in loads[:3]:
        copy.wait()
    flags[...] = jnp.where(types[...] != 1, 1.0, 0.0)
    label = label_of(regions)

    def body(where):
        values = load(pops, where)
        lin = linearise(values, porous[where], types[where], regions[where])
        store(post, where, collide(values, lin))
        store(factors, where, porosity_factors(lin))
        for k, value in enumerate([factor_weight(lin), *lin["u"]]):
            motion[(k,) + where] = value

    for a in range(rows_a):
        loads[3 + a].wait()
        chunks([a], porous.shape, body)
    loads[-1].wait()
    own = {POST: post, ADJ: seed, FACTOR: factors, MOTION: motion, FLAG: flags}
    pack_azimuthal(FIRST, own, range(rows_a), t_out, label)

    def run(parity):
        near, far = near_side(parity)
        pack_face(FIRST, own, near, e_out, label)
        pack_face(FIRST, own, far, o_out, label)
        ed_out[...] = t_out[parity]
        od_out[...] = t_out[1 - parity]

    by_parity(parity_ref, run)


def second_rows(fields, rows, cell_refs, results, scratch):
    porous, types, regions = cell_refs
    post_next, adj, sens, around = results
    state, back = scratch
    for a in rows:
        for q in range(1, 19):
            around[q - 1, a] = fields.moved(FLAG, 0, a, tuple(-c for c in VELOCITY[q]))
        stream_row(fields, a, around, state)
        stream_adjoint_row(fields, a, fields.own[FLAG][a], around, back)

    def body(where):
        values = load(state, where)
        lin = linearise(values, porous[where], types[where], regions[where])
        store(post_next, where, collide(values, lin))
        result, partial_sens = pull_back(load(back, where), values, lin)
        store(adj, where, result)
        sens[where] = partial_sens

    chunks(rows, porous.shape, body)


def second_near_kernel(
    parity_ref, post, seed, factors, flags, porous, types, regions, e, t, ed,
    post_next, adj, sens, around, e_out, t_out, partial, state, back, parts,
):
    def run(parity):
        own = {POST: post, ADJ: seed, FACTOR: factors, FLAG: flags}
        fields = Fields(FIRST, own, parity, e=e, t=t, ed=ed)
        rows, _ = near_rows(parity, porous.shape[0])
        results = (post_next, adj, sens, around)
        second_rows(fields, rows, (porous, types, regions), results, (state, back))
        own = {POST: post_next, ADJ: adj}
        pack_face(SECOND, own, near_side(parity)[0], e_out)
        pack_azimuthal(SECOND, own, rows, t_out)
        partial[...] = region_sums(fields, rows, adj, sens, around, regions, parts)

    by_parity(parity_ref, run)


def second_far_kernel(
    parity_ref, real_ref, post_near, adj_near, sens_near, around_near, t_near, partial_near,
    post, seed, factors, flags, porous, types, regions, o, t, od,
    post_next, adj, sens, around, t_out, o_out, partial, state, back, parts,
):
    def run(parity):
        own = {POST: post, ADJ: seed, FACTOR: factors, FLAG: flags}
        fields = Fields(FIRST, own, parity, o=o, real=real_ref[0], t=t, od=od)
        _, row = near_rows(parity, porous.shape[0])
        results = (post_next, adj, sens, around)
        second_rows(fields, [row], (porous, types, regions), results, (state, back))
        own = {POST: post_next, ADJ: adj}
        pack_face(SECOND, own, near_side(parity)[1], o_out)
        pack_azimuthal(SECOND, own, [row], t_out)
        sums = region_sums(fields, [row], adj, sens, around, regions, parts)
        partial[...] = partial_near[...] + sums

    by_parity(parity_ref, run)


def region_sums(fields, rows, adj, sens, around, regions, parts):
    factors = fields.own[FACTOR]
    rows_a, rows_t, rows_r = sens.shape
    sums = {}
    for a in rows:
        sums.setdefault((0, 0), []).extend([sens[a], factors[0, a] * adj[0, a]])
        for q in range(1, 19):
            behind = tuple(-c for c in VELOCITY[q])
            open_, value = around[q - 1, a], adj[q, a]
            sums[(0, 0)].append(jnp.where(open_ > 0, 0.0, factors[OPPOSITE[q], a]) * value)
            term = jnp.where(open_ > 0, fields.moved(FACTOR, q, a, behind), 0.0) * value
            from_a = a + behind[0]
            beyond = -1 if from_a < 0 else 1 if from_a >= rows_a else 0
            sums.setdefault((beyond, behind[1]), []).append(term)
    at_t = lax.broadcasted_iota(jnp.int32, (rows_t, rows_r), 0)
    lines = []
    for beyond in sorted({key[0] for key in sums}):
        low, centre, high = (functools.reduce(jnp.add, sums[(beyond, st)]) for st in (-1, 0, 1))
        inner = centre + jnp.where(at_t == 0, 0.0, low) + jnp.where(at_t == rows_t - 1, 0.0, high)
        a = {-1: -1, 0: 0, 1: rows_a}[beyond]
        label = fields.row_label(a) if beyond else label_of(regions)
        lines.append((jnp.sum(inner, axis=0, keepdims=True), label))
        a = a if beyond else rows[0]
        lines.append((high[rows_t - 1 : rows_t], fields.edge_label(LO, a)))
        lines.append((low[0:1], fields.edge_label(HI, a)))
    parts[...] = jnp.zeros_like(parts)
    for i, (value, label) in enumerate(lines):
        parts[0, i : i + 1, :] = value
        parts[1, i : i + 1, :] = jnp.broadcast_to(label, (1, rows_r))
    lanes = lax.broadcasted_iota(jnp.int32, parts.shape[1:], 1) + 1
    total = jnp.sum(parts[0], axis=1, keepdims=True)
    chosen = jnp.where(lanes == parts[1].astype(jnp.int32), total, 0.0)
    return jnp.sum(chosen, axis=0, keepdims=True)


def corner_kernel(e, o, t, total, e_out, o_out):
    row = 16 * SECOND.fields
    for out in (e_out, o_out):
        out[row : row + 8, :] = t[0]
    e_out[row + 8 : row + 16, :] = jnp.broadcast_to(total[...], (8, e_out.shape[1]))


def third_rows(fields, rows, cell_refs, own_refs, hbm, sens, scratch, sems):
    porous, types, regions = cell_refs
    around, flags, pops, sens_one = own_refs
    final, result, back = scratch
    stores = []

    def send(source, target, a):
        stores.append(pltpu.make_async_copy(source.at[:, a], target.at[:, a], sems.at[len(stores)]))
        stores[-1].start()

    def body(where):
        values = load(pops, where)
        lin = linearise(values, porous[where], types[where], regions[where])
        adjoint, partial_sens = pull_back(load(back, where), values, lin)
        store(result, where, adjoint)
        sens[where] = partial_sens + sens_one[where]

    for a in rows:
        stream_row(fields, a, around, final)
        send(final, hbm[0], a)
        stream_adjoint_row(fields, a, flags[a], around, back)
        chunks([a], porous.shape, body)
        send(result, hbm[1], a)
    for copy in stores:
        copy.wait()


def third_near_kernel(
    parity_ref, post, adj, flags, around, pops, porous, types, regions, sens_one, e, t,
    final_hbm, result_hbm, sens, final, result, back, sems,
):
    def run(parity):
        fields = Fields(SECOND, {POST: post, ADJ: adj}, parity, e=e, t=t)
        rows, _ = near_rows(parity, porous.shape[0])
        third_rows(
            fields, rows, (porous, types, regions), (around, flags, pops, sens_one),
            (final_hbm, result_hbm), sens, (final, result, back), sems,
        )

    by_parity(parity_ref, run)


def third_far_kernel(
    parity_ref, real_ref, final_near, result_near, sens_near,
    post, adj, flags, around, pops, porous, types, regions, sens_one, o, t,
    final_hbm, result_hbm, sens, final, result, back, sems,
):
    def run(parity):
        fields = Fields(SECOND, {POST: post, ADJ: adj}, parity, o=o, real=real_ref[0], t=t)
        rows, row = near_rows(parity, porous.shape[0])
        for a in rows:
            sens[a] = sens_near[a]
        third_rows(
            fields, [row], (porous, types, regions), (around, flags, pops, sens_one),
            (final_hbm, result_hbm), sens, (final, result, back), sems,
        )

    by_parity(parity_ref, run)


VMEM, HBM = pltpu.VMEM, pltpu.HBM


def call(body, in_spaces, outs, scratch, *arrays, aliases=None, cost=None):
    return pl.pallas_call(
        body,
        out_shape=[jax.ShapeDtypeStruct(shape, dtype) for shape, dtype, _ in outs],
        in_specs=[pl.BlockSpec(memory_space=space) for space in in_spaces],
        out_specs=[pl.BlockSpec(memory_space=space) for _, _, space in outs],
        scratch_shapes=scratch,
        input_output_aliases=aliases or {},
        cost_estimate=cost,
        compiler_params=pltpu.CompilerParams(vmem_limit_bytes=16 * 1024 * 1024),
    )(*arrays)


def axial_pairs(flip, shift_t=0):
    size_a, size_t = lax.axis_size("ax"), lax.axis_size("az")
    pairs = []
    for a in range(size_a):
        partner = ((a + flip) ^ 1) - flip
        for t in range(size_t):
            if 0 <= partner < size_a:
                pairs.append((a * size_t + t, partner * size_t + (t + shift_t) % size_t))
            elif shift_t:
                pairs.append((a * size_t + t, a * size_t + (t + shift_t) % size_t))
            elif size_t % 2 == 0:
                pairs.append((a * size_t + t, a * size_t + (t ^ 1)))
    return pairs


def from_both_sectors(message, high_rows, send):
    if lax.axis_size("az") == 2:
        return send(message, 1)
    return jnp.where(jnp.asarray(high_rows), send(message, 1), send(message, -1))


def high_rows(layout):
    rows = np.zeros((layout.blocks, 8, 1), bool)
    for key, (block, i) in layout.place.items():
        rows[block, i] = key[0] == HI
    return rows


def send_azimuthal(layout, message):
    size = lax.axis_size("az")

    def send(x, shift):
        return lax.ppermute(x, "az", [(i, (i + shift) % size) for i in range(size)])

    return from_both_sectors(message, high_rows(layout), send)


def send_axial(message, flip):
    return lax.ppermute(message, ("ax", "az"), axial_pairs(flip))


def send_diagonal(message, flip):
    def send(x, shift):
        return lax.ppermute(x, ("ax", "az"), axial_pairs(flip, shift))

    return from_both_sectors(message, high_rows(FIRST)[0], send)


def from_partner(x, flip_a, flip_t):
    size_a, size_t = lax.axis_size("ax"), lax.axis_size("az")
    pairs = [
        (a * size_t + t, (a ^ flip_a) * size_t + (t ^ flip_t))
        for a in range(size_a)
        for t in range(size_t)
    ]
    return lax.ppermute(x, ("ax", "az"), pairs)


def shards(initial, adjoint_seed, porosity, cell_type, region):
    cells_ = porosity.shape
    pops = (19,) + cells_
    wide = cells_[2]
    f32, i32 = jnp.float32, jnp.int32
    size_a, size_t = lax.axis_size("ax"), lax.axis_size("az")
    index = lax.axis_index("ax")
    real = (index != 0) & (index != size_a - 1)
    place = ((index % 2).astype(i32).reshape(1), real.astype(i32).reshape(1))

    def axial(layout, more):
        return ((16 * layout.fields + more, wide), f32, VMEM)

    def azimuthal(layout):
        return [((layout.blocks, 8, wide), f32, VMEM)]

    inputs = (initial, adjoint_seed, porosity, cell_type, region)
    post, factors, e, o, t, ed, od, flags = call(
        first_kernel,
        [pltpu.SMEM] + [HBM] * 5,
        [(pops, f32, VMEM), (pops, f32, VMEM)] + [axial(FIRST, 0)] * 2 + azimuthal(FIRST)
        + [((8, wide), f32, VMEM)] * 2 + [(cells_, f32, VMEM)],
        [VMEM(x.shape, x.dtype) for x in inputs]
        + [VMEM((4,) + cells_, f32), pltpu.SemaphoreType.DMA((4 + cells_[0],))],
        place[0],
        *(pltpu.with_memory_space_constraint(x, HBM) for x in inputs),
    )
    e, o = send_axial(e, 0), send_axial(o, 1)
    t_near = send_azimuthal(FIRST, t)
    ed, od = send_diagonal(ed, 0), send_diagonal(od, 1)
    layers = [(pops, f32, VMEM), (pops, f32, VMEM), (cells_, f32, VMEM), ((18,) + cells_, f32, VMEM)]
    inside = (post, adjoint_seed, factors, flags, porosity, cell_type, region)
    row = [((1, wide), f32, VMEM)]
    scratch = [VMEM(pops, f32), VMEM(pops, f32), VMEM((2, 8, wide), f32)]
    *near, e, t, total = call(
        second_near_kernel,
        [pltpu.SMEM] + [VMEM] * 10,
        layers + [axial(SECOND, 16)] + azimuthal(SECOND) + row,
        scratch,
        place[0], *inside, e, t_near, ed,
    )
    post, adj, sens_one, around, t, o, total = call(
        second_far_kernel,
        [pltpu.SMEM] * 2 + [VMEM] * 16,
        layers + azimuthal(SECOND) + [axial(SECOND, 8)] + row,
        scratch,
        *place, *near, t, total, *inside, o, t_near, od,
        aliases={2: 0, 3: 1, 4: 2, 5: 3, 6: 4},
    )
    t_near = send_azimuthal(SECOND, t)
    halving = size_a >= 4 and not (size_a & (size_a - 1) or size_t & (size_t - 1))
    flips, last = [(1, 1 << k) for k in range(size_t.bit_length() - 1)], []
    if halving:
        total = total + from_partner(total, size_a // 2 | 1, 0)
        left = [(1 << k) | 1 for k in range(size_a.bit_length() - 3, 0, -1)]
        last = left[-2:] if len(left) > 1 else []
        flips += [(flip, 0) for flip in left[: len(left) - len(last)]]
    e, o = call(
        corner_kernel,
        [VMEM] * 4,
        [axial(SECOND, 16), axial(SECOND, 8)],
        [],
        e, o, t_near, total,
        aliases={0: 0, 1: 1},
    )
    e, o = send_axial(e, 0), send_axial(o, 1)
    stored = [(pops, f32, HBM), (pops, f32, HBM), (cells_, f32, VMEM)]
    third_scratch = [VMEM(pops, f32)] * 3 + [pltpu.SemaphoreType.DMA((2 * cells_[0],))]
    inside = (post, adj, flags, around, initial, porosity, cell_type, region, sens_one)
    near = call(
        third_near_kernel,
        [pltpu.SMEM] + [VMEM] * 11,
        stored,
        third_scratch,
        place[0], *inside, e, t_near,
    )
    if halving:
        row = 16 * SECOND.fields + 8
        totals = total + e[row : row + 1]
        for flip in flips:
            totals = totals + from_partner(totals, *flip)
        if last:
            totals, _ = lax.optimization_barrier((totals, near[2]))
            one, two = last
            pair = totals + from_partner(totals, one, 0)
            totals = pair + (from_partner(totals, two, 0) + from_partner(totals, one ^ two, 0))
    else:
        totals = lax.psum(total, ("ax", "az"))
    final, adjoint, sensitivity = call(
        third_far_kernel,
        [pltpu.SMEM] * 2 + [HBM] * 2 + [VMEM] * 12,
        stored,
        third_scratch,
        *place, *near, *inside, o, t_near,
        aliases={2: 0, 3: 1},
    )
    return final, adjoint, sensitivity, totals[0, : size_a * size_t // 4]


def solution(mesh):
    return jax.shard_map(
        shards,
        mesh=mesh,
        in_specs=(
            P(None, "ax", "az", None),
            P(None, "ax", "az", None),
            P("ax", "az", None),
            P("ax", "az", None),
            P("ax", "az", None),
        ),
        out_specs=(P(None, "ax", "az", None), P(None, "ax", "az", None), P("ax", "az", None), P()),
        check_vma=False,
    )
```

```python
import functools

import jax
import jax.numpy as jnp
import numpy as np
from jax import lax
from jax.experimental import pallas as pl
from jax.experimental.pallas import tpu as pltpu
from jax.sharding import PartitionSpec as P

VELOCITY = [
    (0, 0, 0),
    (1, 0, 0),
    (-1, 0, 0),
    (0, 1, 0),
    (0, -1, 0),
    (0, 0, 1),
    (0, 0, -1),
    (1, 1, 0),
    (-1, -1, 0),
    (1, -1, 0),
    (-1, 1, 0),
    (1, 0, 1),
    (-1, 0, -1),
    (1, 0, -1),
    (-1, 0, 1),
    (0, 1, 1),
    (0, -1, -1),
    (0, 1, -1),
    (0, -1, 1),
]
OPPOSITE = [0, 2, 1, 4, 3, 6, 5, 8, 7, 10, 9, 12, 11, 14, 13, 16, 15, 18, 17]
INLET_SPEED = (0.05, 0.05, 0.0)
W_AXIS = 1.0 / 18.0
W_EDGE = 1.0 / 36.0


def moving(axis, sign):
    return [q for q in range(19) if VELOCITY[q][axis] == sign]


LO, HI = 0, 1
POST, ADJ, FACTOR, FLAG, MOTION = 0, 1, 2, 3, 4


def face_fields(kinds, axis, side):
    sign = -1 if side == LO else 1
    fields = []
    for kind in kinds:
        if kind == FLAG:
            fields.append((FLAG, 0))
        elif kind == FACTOR and axis == 0:
            fields += [(MOTION, k) for k in range(4)]
        else:
            fields += [(kind, q) for q in moving(axis, -sign if kind == ADJ else sign)]
    return fields


class Layout:
    def __init__(self, kinds):
        self.ax = [face_fields(kinds, 0, side) for side in (LO, HI)]
        self.slot = [{key: i for i, key in enumerate(fields)} for fields in self.ax]
        self.fields = len(self.ax[LO])
        corner, rest = [], []
        for a, sign in ((1, 1), (0, -1)):
            for side in (LO, HI):
                for kind, q in face_fields(kinds, 1, side):
                    leaves = VELOCITY[q][0] == (-sign if kind == ADJ else sign)
                    key = (side, kind, q, a)
                    (corner if kind == FLAG or leaves else rest).append(key)
        self.corner_blocks = -(-len(corner) // 8)
        self.blocks = self.corner_blocks + -(-len(rest) // 8)
        self.place = {key: (i // 8, i % 8) for i, key in enumerate(corner)}
        self.place.update({key: (self.corner_blocks + i // 8, i % 8) for i, key in enumerate(rest)})


FIRST = Layout((POST, ADJ, FACTOR, FLAG))
SECOND = Layout((POST, ADJ))


def pairs_of(values):
    sums = [values[q] + values[q + 1] for q in range(1, 19, 2)]
    diffs = [values[q] - values[q + 1] for q in range(1, 19, 2)]
    return sums, diffs


def projections(vec):
    va, vt, vr = vec
    return [va, vt, vr, va + vt, va - vt, va + vr, va - vr, vt + vr, vt - vr]


def linearise(pops, porous, types, regions):
    sums, diffs = pairs_of(pops)
    s0, s1, s2, s3, s4, s5, s6, s7, s8 = sums
    d0, d1, d2, d3, d4, d5, d6, d7, d8 = diffs
    at, ar, tr = s3 + s4, s5 + s6, s7 + s8
    rho = pops[0] + ((s0 + s1) + (s2 + at)) + (ar + tr)
    ma = (d0 + (d3 + d4)) + (d5 + d6)
    mt = (d1 + (d3 - d4)) + (d7 + d8)
    mr = (d2 + (d5 - d6)) + (d7 - d8)
    inv = 1.0 / rho
    ua, ut, ur = ma * inv, mt * inv, mr * inv
    third = rho * (1.0 / 3.0)
    paa = (s0 + at + ar - third) - ma * ua
    ptt = (s1 + at + tr - third) - mt * ut
    prr = (s2 + ar + tr - third) - mr * ur
    pat = (s3 - s4) - ma * ut
    par = (s5 - s6) - ma * ur
    ptr = (s7 - s8) - mt * ur
    square = (paa * paa + ptt * ptt + prr * prr) + 2.0 * (pat * pat + par * par + ptr * ptr) + 0.0001
    inv_root = lax.rsqrt(square)
    shear = 1.5 * (square * inv_root) * inv
    shifted = shear + 0.01
    viscous = 0.02 * jnp.exp((0.7 - 1.0) * jnp.log(shifted))
    omega = 1.0 / (0.5 + 3.0 * viscous)
    relaxed = (types != 2) & (types != 3)
    kappa = jnp.where(regions > 0, porous, 0.0)
    return dict(
        rho=rho,
        inv=inv,
        u=(ua, ut, ur),
        p=(paa, ptt, prr, pat, par, ptr),
        inv_root=inv_root,
        shear=shear,
        shifted=shifted,
        viscous=viscous,
        omega=omega,
        relaxed=relaxed,
        kappa=kappa,
        keep=jnp.where(relaxed, 1.0 - omega, 0.0),
        design=jnp.where(relaxed & (regions > 0), 1.0, 0.0),
        inlet=types == 2,
        outlet=types == 3,
    )


def collide(pops, lin):
    rho, relaxed, inlet = lin["rho"], lin["relaxed"], lin["inlet"]
    ua, ut, ur = (jnp.where(inlet, speed, x) for x, speed in zip(lin["u"], INLET_SPEED))
    scale = jnp.where(relaxed, (lin["omega"] - lin["kappa"]) * rho, 1.0)
    rest = jnp.where(relaxed, lin["kappa"] * rho, 0.0)
    keep = lin["keep"]
    still = 1.0 - 1.5 * (ua * ua + ut * ut + ur * ur)
    post = [keep * pops[0] + (1.0 / 3.0) * (scale * still + rest)]
    for i, cu in enumerate(projections((ua, ut, ur))):
        weight = W_AXIS if i < 3 else W_EDGE
        even = weight * (scale * (still + 4.5 * cu * cu) + rest)
        odd = (3.0 * weight) * (scale * cu)
        post.append(keep * pops[1 + 2 * i] + (even + odd))
        post.append(keep * pops[2 + 2 * i] + (even - odd))
    return post


def pull_back(back, pops, lin):
    sums, diffs = pairs_of(back)
    s0, s1, s2, s3, s4, s5, s6, s7, s8 = sums
    d0, d1, d2, d3, d4, d5, d6, d7, d8 = diffs
    at, ar, tr = s3 + s4, s5 + s6, s7 + s8
    b0 = (1.0 / 3.0) * back[0] + W_AXIS * (s0 + s1 + s2) + W_EDGE * (at + ar + tr)
    ba = W_AXIS * d0 + W_EDGE * ((d3 + d4) + (d5 + d6))
    bt = W_AXIS * d1 + W_EDGE * ((d3 - d4) + (d7 + d8))
    br = W_AXIS * d2 + W_EDGE * ((d5 - d6) + (d7 - d8))
    baa = W_AXIS * s0 + W_EDGE * (at + ar)
    btt = W_AXIS * s1 + W_EDGE * (at + tr)
    brr = W_AXIS * s2 + W_EDGE * (ar + tr)
    bat, bar, btr = W_EDGE * (s3 - s4), W_EDGE * (s5 - s6), W_EDGE * (s7 - s8)
    along = back[0] * pops[0]
    for q in range(1, 19):
        along = along + back[q] * pops[q]
    rho, inv = lin["rho"], lin["inv"]
    ua, ut, ur = lin["u"]
    qa = baa * ua + bat * ut + bar * ur
    qt = bat * ua + btt * ut + btr * ur
    qr = bar * ua + btr * ut + brr * ur
    uu = ua * ua + ut * ut + ur * ur
    slope = 3.0 * (ua * ba + ut * bt + ur * br) + 4.5 * (ua * qa + ut * qt + ur * qr) - 1.5 * (uu * b0)
    full = b0 + slope
    sens = -(lin["design"] * (rho * slope))
    relaxed, omega = lin["relaxed"], lin["omega"]
    shear_bar = (rho * full - along) * (omega * omega) * (0.9 * lin["viscous"]) / lin["shifted"]
    shear_bar = jnp.where(relaxed, shear_bar, 0.0)
    z = shear_bar * (1.5 * inv) * lin["inv_root"]
    maa, mtt, mrr, mat, mar, mtr = (z * x for x in lin["p"])
    scale = jnp.where(relaxed, omega - lin["kappa"], jnp.where(lin["outlet"], inv, 0.0))
    la = maa * ua + mat * ut + mar * ur
    lt = mat * ua + mtt * ut + mtr * ur
    lr = mar * ua + mtr * ut + mrr * ur
    va = scale * (3.0 * (ba - b0 * ua) + 9.0 * qa) - 2.0 * la
    vt = scale * (3.0 * (bt - b0 * ut) + 9.0 * qt) - 2.0 * lt
    vr = scale * (3.0 * (br - b0 * ur) + 9.0 * qr) - 2.0 * lr
    total = jnp.where(relaxed, lin["kappa"] * b0 + scale * full, 0.0)
    total = total - shear_bar * lin["shear"] * inv - (1.0 / 3.0) * (maa + mtt + mrr)
    total = total - ((la + va) * ua + (lt + vt) * ut + (lr + vr) * ur)
    keep = lin["keep"]
    taa, ttt, trr = total + maa, total + mtt, total + mrr
    sat, sar, str_ = taa + mtt, taa + mrr, ttt + mrr
    mat2, mar2, mtr2 = 2.0 * mat, 2.0 * mar, 2.0 * mtr
    evens = [taa, ttt, trr, sat + mat2, sat - mat2, sar + mar2, sar - mar2, str_ + mtr2, str_ - mtr2]
    result = [keep * back[0] + total]
    for i, odd in enumerate(projections((va, vt, vr))):
        result.append(keep * back[1 + 2 * i] + (evens[i] + odd))
        result.append(keep * back[2 + 2 * i] + (evens[i] - odd))
    return result, sens


def face_rows(slot):
    return slice(16 * slot, 16 * slot + 16)


def by_parity(parity_ref, body):
    for parity in (0, 1):
        pl.when(parity_ref[0] == parity)(functools.partial(body, parity))


def near_rows(parity, rows_a):
    return (range(1, rows_a), 0) if parity == 0 else (range(rows_a - 1), rows_a - 1)


class Fields:
    def __init__(self, layout, own, parity, e=None, o=None, real=None, t=None, ed=None, od=None):
        self.layout, self.own, self.t = layout, own, t
        self.rows_a = own[POST].shape[1]
        sides = [(o, od, real), (e, ed, None)]
        self.sides = sides if parity == 0 else sides[::-1]

    def row(self, kind, q, a):
        if 0 <= a < self.rows_a:
            return self.own[FLAG][a] if kind == FLAG else self.own[kind][q, a]
        if kind == FACTOR:
            weight, *velocity = (self.row(MOTION, k, a) for k in range(4))
            return porosity_factor(q, weight, velocity)
        message, _, real = self.sides[a >= 0]
        slot = self.layout.slot[HI if a < 0 else LO][(kind, q)]
        return self.masked(kind, message[face_rows(slot), :], real)

    def masked(self, kind, value, real):
        if real is None or kind not in (ADJ, FLAG):
            return value
        return jnp.where(real == 1, value, 0.0)

    def row_label(self, a):
        row = 16 * self.layout.slot[HI if a < 0 else LO][(MOTION, 0)]
        return self.sides[a >= 0][0][row : row + 1, 0:1]

    def edge_label(self, side, a):
        sa = 1 if a < 0 else -1 if a >= self.rows_a else 0
        q = VELOCITY.index((sa, -1 if side == LO else 1, 0))
        return self.edge(side, FACTOR, q, a)[:, 0:1]

    def message(self, key, a):
        block, i = self.layout.place[key]
        if 0 <= a < self.rows_a:
            return self.t[block, i : i + 1, :]
        axial, corners, real = self.sides[a >= 0]
        if corners is None:
            row = 16 * self.layout.fields + 8 * block + i
            return self.masked(key[1], axial[row : row + 1, :], real)
        return self.masked(key[1], corners[i : i + 1, :], real)

    def edge(self, side, kind, q, a):
        row = self.rows_a - 1 if a < 0 else 0 if a >= self.rows_a else a
        return self.message((side, kind, q, row), a)

    def moved(self, kind, q, a, shift):
        sa, st, sr = shift
        value = self.row(kind, q, a + sa)
        rows_t, rows_r = value.shape
        if st:
            value = pltpu.roll(value, (-st) % rows_t, 0)
            beyond = self.edge(LO if st > 0 else HI, kind, q, a + sa)
            at_edge = lax.broadcasted_iota(jnp.int32, value.shape, 0) == (rows_t - 1 if st > 0 else 0)
            value = jnp.where(at_edge, beyond, value)
        if sr:
            value = pltpu.roll(value, (-sr) % rows_r, 1)
        return value


def cells(own, kind, q, a):
    return own[FLAG].at[a] if kind == FLAG else own[kind].at[q, a]


def stream_row(fields, a, around, result):
    post = fields.own[POST]
    result[0, a] = post[0, a]
    for q in range(1, 19):
        moved = fields.moved(POST, q, a, tuple(-c for c in VELOCITY[q]))
        result[q, a] = jnp.where(around[q - 1, a] > 0, moved, post[OPPOSITE[q], a])


def stream_adjoint_row(fields, a, centre, around, result):
    adj = fields.own[ADJ]
    result[0, a] = adj[0, a]
    for q in range(1, 19):
        opp = OPPOSITE[q]
        ahead = centre * fields.moved(ADJ, opp, a, tuple(-c for c in VELOCITY[q]))
        result[opp, a] = ahead + (1.0 - around[q - 1, a]) * adj[q, a]


def labelled(value, label):
    lanes = lax.broadcasted_iota(jnp.int32, value.shape, 1)
    return jnp.where(lanes == 0, label, value)


def pack_azimuthal(layout, own, rows, t_ref, label=None):
    rows_t = own[POST].shape[2]
    for (side, kind, q, a), (block, i) in layout.place.items():
        if a in rows:
            t = 0 if side == LO else rows_t - 1
            row = cells(own, kind, q, a)[t : t + 1, :]
            t_ref[block, i : i + 1, :] = labelled(row, label) if kind == FACTOR else row


def pack_face(layout, own, side, message, label=None):
    a = 0 if side == LO else own[POST].shape[1] - 1
    for slot, (kind, q) in enumerate(layout.ax[side]):
        value = cells(own, kind, q, a)[...]
        if (kind, q) == (MOTION, 0):
            value = labelled(value, label)
        message[face_rows(slot), :] = value


def near_side(parity):
    return (HI, LO) if parity == 0 else (LO, HI)


def chunks(rows_a, shape, body):
    counts = (len(rows_a), shape[1] // 8, shape[2] // 128)

    def step(i, carry):
        a = rows_a[0] + i // (counts[1] * counts[2])
        t = pl.multiple_of((i // counts[2]) % counts[1] * 8, 8)
        r = pl.multiple_of(i % counts[2] * 128, 128)
        body((a, pl.ds(t, 8), pl.ds(r, 128)))
        return carry

    lax.fori_loop(0, counts[0] * counts[1] * counts[2], step, 0, unroll=4)


def load(ref, where):
    return [ref[(q,) + where] for q in range(19)]


def store(ref, where, values):
    for q in range(19):
        ref[(q,) + where] = values[q]


def label_of(regions):
    label = jnp.max(jnp.max(regions[...], axis=0), axis=(0, 1), keepdims=True)
    return label.astype(jnp.float32)


def porosity_factor(q, weight, velocity):
    ua, ut, ur = velocity
    pair = (q - 1) // 2
    cu = projections(velocity)[pair]
    scaled = (W_AXIS if pair < 3 else W_EDGE) * weight
    still = -1.5 * (ua * ua + ut * ut + ur * ur)
    return scaled * (still + 4.5 * cu * cu + (3.0 * cu if q % 2 else -3.0 * cu))


def factor_weight(lin):
    return -(lin["design"] * lin["rho"])


def porosity_factors(lin):
    ua, ut, ur = lin["u"]
    weight = factor_weight(lin)
    still = -1.5 * (ua * ua + ut * ut + ur * ur)
    result = [(1.0 / 3.0) * weight * still]
    for i, cu in enumerate(projections((ua, ut, ur))):
        scaled = (W_AXIS if i < 3 else W_EDGE) * weight
        even, odd = scaled * (still + 4.5 * cu * cu), 3.0 * scaled * cu
        result += [even + odd, even - odd]
    return result


def first_kernel(
    parity_ref, pops_hbm, seed_hbm, porous_hbm, types_hbm, regions_hbm,
    post, factors, e_out, o_out, t_out, ed_out, od_out, flags,
    pops, seed, porous, types, regions, motion, sems,
):
    rows_a, _, rows_r = porous.shape
    pairs = [(types_hbm, types), (regions_hbm, regions), (porous_hbm, porous)]
    pairs += [(pops_hbm.at[:, a], pops.at[:, a]) for a in range(rows_a)] + [(seed_hbm, seed)]
    loads = [pltpu.make_async_copy(*pair, sems.at[i]) for i, pair in enumerate(pairs)]
    for copy in loads:
        copy.start()
    for copy in loads[:3]:
        copy.wait()
    flags[...] = jnp.where(types[...] != 1, 1.0, 0.0)
    label = label_of(regions)

    def body(where):
        values = load(pops, where)
        lin = linearise(values, porous[where], types[where], regions[where])
        store(post, where, collide(values, lin))
        store(factors, where, porosity_factors(lin))
        for k, value in enumerate([factor_weight(lin), *lin["u"]]):
            motion[(k,) + where] = value

    for a in range(rows_a):
        loads[3 + a].wait()
        chunks([a], porous.shape, body)
    loads[-1].wait()
    own = {POST: post, ADJ: seed, FACTOR: factors, MOTION: motion, FLAG: flags}
    pack_azimuthal(FIRST, own, range(rows_a), t_out, label)

    def run(parity):
        near, far = near_side(parity)
        pack_face(FIRST, own, near, e_out, label)
        pack_face(FIRST, own, far, o_out, label)
        ed_out[...] = t_out[parity]
        od_out[...] = t_out[1 - parity]

    by_parity(parity_ref, run)


def second_rows(fields, rows, cell_refs, results, scratch):
    porous, types, regions = cell_refs
    post_next, adj, sens, around = results
    state, back = scratch
    for a in rows:
        for q in range(1, 19):
            around[q - 1, a] = fields.moved(FLAG, 0, a, tuple(-c for c in VELOCITY[q]))
        stream_row(fields, a, around, state)
        stream_adjoint_row(fields, a, fields.own[FLAG][a], around, back)

    def body(where):
        values = load(state, where)
        lin = linearise(values, porous[where], types[where], regions[where])
        store(post_next, where, collide(values, lin))
        result, partial_sens = pull_back(load(back, where), values, lin)
        store(adj, where, result)
        sens[where] = partial_sens

    chunks(rows, porous.shape, body)


def second_near_kernel(
    parity_ref, post, seed, factors, flags, porous, types, regions, e, t, ed,
    post_next, adj, sens, around, e_out, t_out, partial, state, back, parts,
):
    def run(parity):
        own = {POST: post, ADJ: seed, FACTOR: factors, FLAG: flags}
        fields = Fields(FIRST, own, parity, e=e, t=t, ed=ed)
        rows, _ = near_rows(parity, porous.shape[0])
        results = (post_next, adj, sens, around)
        second_rows(fields, rows, (porous, types, regions), results, (state, back))
        own = {POST: post_next, ADJ: adj}
        pack_face(SECOND, own, near_side(parity)[0], e_out)
        pack_azimuthal(SECOND, own, rows, t_out)
        partial[...] = region_sums(fields, rows, adj, sens, around, regions, parts)

    by_parity(parity_ref, run)


def second_far_kernel(
    parity_ref, real_ref, post_near, adj_near, sens_near, around_near, t_near, partial_near,
    post, seed, factors, flags, porous, types, regions, o, t, od,
    post_next, adj, sens, around, t_out, o_out, partial, state, back, parts,
):
    def run(parity):
        own = {POST: post, ADJ: seed, FACTOR: factors, FLAG: flags}
        fields = Fields(FIRST, own, parity, o=o, real=real_ref[0], t=t, od=od)
        _, row = near_rows(parity, porous.shape[0])
        results = (post_next, adj, sens, around)
        second_rows(fields, [row], (porous, types, regions), results, (state, back))
        own = {POST: post_next, ADJ: adj}
        pack_face(SECOND, own, near_side(parity)[1], o_out)
        pack_azimuthal(SECOND, own, [row], t_out)
        sums = region_sums(fields, [row], adj, sens, around, regions, parts)
        partial[...] = partial_near[...] + sums

    by_parity(parity_ref, run)


def region_sums(fields, rows, adj, sens, around, regions, parts):
    factors = fields.own[FACTOR]
    rows_a, rows_t, rows_r = sens.shape
    sums = {}
    for a in rows:
        sums.setdefault((0, 0), []).extend([sens[a], factors[0, a] * adj[0, a]])
        for q in range(1, 19):
            behind = tuple(-c for c in VELOCITY[q])
            open_, value = around[q - 1, a], adj[q, a]
            sums[(0, 0)].append(jnp.where(open_ > 0, 0.0, factors[OPPOSITE[q], a]) * value)
            term = jnp.where(open_ > 0, fields.moved(FACTOR, q, a, behind), 0.0) * value
            from_a = a + behind[0]
            beyond = -1 if from_a < 0 else 1 if from_a >= rows_a else 0
            sums.setdefault((beyond, behind[1]), []).append(term)
    at_t = lax.broadcasted_iota(jnp.int32, (rows_t, rows_r), 0)
    lines = []
    for beyond in sorted({key[0] for key in sums}):
        low, centre, high = (functools.reduce(jnp.add, sums[(beyond, st)]) for st in (-1, 0, 1))
        inner = centre + jnp.where(at_t == 0, 0.0, low) + jnp.where(at_t == rows_t - 1, 0.0, high)
        a = {-1: -1, 0: 0, 1: rows_a}[beyond]
        label = fields.row_label(a) if beyond else label_of(regions)
        lines.append((jnp.sum(inner, axis=0, keepdims=True), label))
        a = a if beyond else rows[0]
        lines.append((high[rows_t - 1 : rows_t], fields.edge_label(LO, a)))
        lines.append((low[0:1], fields.edge_label(HI, a)))
    parts[...] = jnp.zeros_like(parts)
    for i, (value, label) in enumerate(lines):
        parts[0, i : i + 1, :] = value
        parts[1, i : i + 1, :] = jnp.broadcast_to(label, (1, rows_r))
    lanes = lax.broadcasted_iota(jnp.int32, parts.shape[1:], 1) + 1
    total = jnp.sum(parts[0], axis=1, keepdims=True)
    chosen = jnp.where(lanes == parts[1].astype(jnp.int32), total, 0.0)
    return jnp.sum(chosen, axis=0, keepdims=True)


def corner_kernel(e, o, t, total, e_out, o_out):
    row = 16 * SECOND.fields
    for out in (e_out, o_out):
        out[row : row + 8, :] = t[0]
    e_out[row + 8 : row + 16, :] = jnp.broadcast_to(total[...], (8, e_out.shape[1]))


def third_rows(fields, rows, cell_refs, own_refs, hbm, sens, scratch, sems):
    porous, types, regions = cell_refs
    around, flags, pops, sens_one = own_refs
    final, result, back = scratch
    stores = []

    def send(source, target, a):
        stores.append(pltpu.make_async_copy(source.at[:, a], target.at[:, a], sems.at[len(stores)]))
        stores[-1].start()

    def body(where):
        values = load(pops, where)
        lin = linearise(values, porous[where], types[where], regions[where])
        adjoint, partial_sens = pull_back(load(back, where), values, lin)
        store(result, where, adjoint)
        sens[where] = partial_sens + sens_one[where]

    for a in rows:
        stream_row(fields, a, around, final)
        send(final, hbm[0], a)
        stream_adjoint_row(fields, a, flags[a], around, back)
        chunks([a], porous.shape, body)
        send(result, hbm[1], a)
    return stores


def third_near_kernel(
    parity_ref, post, adj, flags, around, pops, porous, types, regions, sens_one, e, t,
    final_hbm, result_hbm, sens, final, result, back, sems,
):
    def run(parity):
        fields = Fields(SECOND, {POST: post, ADJ: adj}, parity, e=e, t=t)
        rows, _ = near_rows(parity, porous.shape[0])
        stores = third_rows(
            fields, rows, (porous, types, regions), (around, flags, pops, sens_one),
            (final_hbm, result_hbm), sens, (final, result, back), sems,
        )
        for copy in stores:
            copy.wait()

    by_parity(parity_ref, run)


def third_far_kernel(
    parity_ref, real_ref, final_near, result_near, sens_near,
    post, adj, flags, around, pops, porous, types, regions, sens_one, o, t,
    final_hbm, result_hbm, sens_hbm, final, result, back, sems, sens,
):
    def run(parity):
        fields = Fields(SECOND, {POST: post, ADJ: adj}, parity, o=o, real=real_ref[0], t=t)
        rows, row = near_rows(parity, porous.shape[0])
        for a in rows:
            sens[a] = sens_near[a]
        stores = third_rows(
            fields, [row], (porous, types, regions), (around, flags, pops, sens_one),
            (final_hbm, result_hbm), sens, (final, result, back), sems,
        )
        stores.append(pltpu.make_async_copy(sens, sens_hbm, sems.at[len(stores)]))
        stores[-1].start()
        for copy in stores:
            copy.wait()

    by_parity(parity_ref, run)


VMEM, HBM = pltpu.VMEM, pltpu.HBM


def call(body, in_spaces, outs, scratch, *arrays, aliases=None, cost=None):
    return pl.pallas_call(
        body,
        out_shape=[jax.ShapeDtypeStruct(shape, dtype) for shape, dtype, _ in outs],
        in_specs=[pl.BlockSpec(memory_space=space) for space in in_spaces],
        out_specs=[pl.BlockSpec(memory_space=space) for _, _, space in outs],
        scratch_shapes=scratch,
        input_output_aliases=aliases or {},
        cost_estimate=cost,
        compiler_params=pltpu.CompilerParams(vmem_limit_bytes=16 * 1024 * 1024),
    )(*arrays)


def axial_pairs(flip, shift_t=0):
    size_a, size_t = lax.axis_size("ax"), lax.axis_size("az")
    pairs = []
    for a in range(size_a):
        partner = ((a + flip) ^ 1) - flip
        for t in range(size_t):
            if 0 <= partner < size_a:
                pairs.append((a * size_t + t, partner * size_t + (t + shift_t) % size_t))
            elif shift_t:
                pairs.append((a * size_t + t, a * size_t + (t + shift_t) % size_t))
            elif size_t % 2 == 0:
                pairs.append((a * size_t + t, a * size_t + (t ^ 1)))
    return pairs


def from_both_sectors(message, high_rows, send):
    if lax.axis_size("az") == 2:
        return send(message, 1)
    return jnp.where(jnp.asarray(high_rows), send(message, 1), send(message, -1))


def high_rows(layout):
    rows = np.zeros((layout.blocks, 8, 1), bool)
    for key, (block, i) in layout.place.items():
        rows[block, i] = key[0] == HI
    return rows


def send_azimuthal(layout, message):
    size = lax.axis_size("az")

    def send(x, shift):
        return lax.ppermute(x, "az", [(i, (i + shift) % size) for i in range(size)])

    return from_both_sectors(message, high_rows(layout), send)


def send_axial(message, flip):
    return lax.ppermute(message, ("ax", "az"), axial_pairs(flip))


def send_diagonal(message, flip):
    def send(x, shift):
        return lax.ppermute(x, ("ax", "az"), axial_pairs(flip, shift))

    return from_both_sectors(message, high_rows(FIRST)[0], send)


def from_partner(x, flip_a, flip_t):
    size_a, size_t = lax.axis_size("ax"), lax.axis_size("az")
    pairs = [
        (a * size_t + t, (a ^ flip_a) * size_t + (t ^ flip_t))
        for a in range(size_a)
        for t in range(size_t)
    ]
    return lax.ppermute(x, ("ax", "az"), pairs)


def shards(initial, adjoint_seed, porosity, cell_type, region):
    cells_ = porosity.shape
    pops = (19,) + cells_
    wide = cells_[2]
    f32, i32 = jnp.float32, jnp.int32
    size_a, size_t = lax.axis_size("ax"), lax.axis_size("az")
    index = lax.axis_index("ax")
    real = (index != 0) & (index != size_a - 1)
    place = ((index % 2).astype(i32).reshape(1), real.astype(i32).reshape(1))

    def axial(layout, more):
        return ((16 * layout.fields + more, wide), f32, VMEM)

    def azimuthal(layout):
        return [((layout.blocks, 8, wide), f32, VMEM)]

    inputs = (initial, adjoint_seed, porosity, cell_type, region)
    post, factors, e, o, t, ed, od, flags = call(
        first_kernel,
        [pltpu.SMEM] + [HBM] * 5,
        [(pops, f32, VMEM), (pops, f32, VMEM)] + [axial(FIRST, 0), axial(FIRST, 8)] + azimuthal(FIRST)
        + [((8, wide), f32, VMEM)] * 2 + [(cells_, f32, VMEM)],
        [VMEM(x.shape, x.dtype) for x in inputs]
        + [VMEM((4,) + cells_, f32), pltpu.SemaphoreType.DMA((4 + cells_[0],))],
        place[0],
        *(pltpu.with_memory_space_constraint(x, HBM) for x in inputs),
    )
    e, o = send_axial(e, 0), send_axial(o, 1)
    t_near = send_azimuthal(FIRST, t)
    ed, od = send_diagonal(ed, 0), send_diagonal(od, 1)
    layers = [(pops, f32, VMEM), (pops, f32, VMEM), (cells_, f32, VMEM), ((18,) + cells_, f32, VMEM)]
    inside = (post, adjoint_seed, factors, flags, porosity, cell_type, region)
    row = [((1, wide), f32, VMEM)]
    scratch = [VMEM(pops, f32), VMEM(pops, f32), VMEM((2, 8, wide), f32)]
    *near, e, t, total = call(
        second_near_kernel,
        [pltpu.SMEM] + [VMEM] * 10,
        layers + [axial(SECOND, 16)] + azimuthal(SECOND) + row,
        scratch,
        place[0], *inside, e, t_near, ed,
    )
    post, adj, sens_one, around, t, o, total = call(
        second_far_kernel,
        [pltpu.SMEM] * 2 + [VMEM] * 16,
        layers + azimuthal(SECOND) + [axial(SECOND, 8)] + row,
        scratch,
        *place, *near, t, total, *inside, o, t_near, od,
        aliases={2: 0, 3: 1, 4: 2, 5: 3, 6: 4},
    )
    t_near = send_azimuthal(SECOND, t)
    halving = size_a >= 4 and not (size_a & (size_a - 1) or size_t & (size_t - 1))
    flips, last = [(1, 1 << k) for k in range(size_t.bit_length() - 1)], []
    if halving:
        total = total + from_partner(total, size_a // 2 | 1, 0)
        left = [(1 << k) | 1 for k in range(size_a.bit_length() - 3, 0, -1)]
        last = left[-2:] if len(left) > 1 else []
        flips += [(flip, 0) for flip in left[: len(left) - len(last)]]
    e, o = call(
        corner_kernel,
        [VMEM] * 4,
        [axial(SECOND, 16), axial(SECOND, 8)],
        [],
        e, o, t_near, total,
        aliases={0: 0, 1: 1},
    )
    e, o = send_axial(e, 0), send_axial(o, 1)
    stored = [(pops, f32, HBM), (pops, f32, HBM), (cells_, f32, VMEM)]
    third_scratch = [VMEM(pops, f32)] * 3 + [pltpu.SemaphoreType.DMA((2 * cells_[0],))]
    inside = (post, adj, flags, around, initial, porosity, cell_type, region, sens_one)
    near = call(
        third_near_kernel,
        [pltpu.SMEM] + [VMEM] * 11,
        stored,
        third_scratch,
        place[0], *inside, e, t_near,
    )
    if halving:
        row = 16 * SECOND.fields + 8
        totals = total + e[row : row + 1]
        for flip in flips:
            totals = totals + from_partner(totals, *flip)
        if last:
            totals, _ = lax.optimization_barrier((totals, near[2]))
            two, one = last
            pair = totals + from_partner(totals, one, 0)
            totals = pair + (from_partner(totals, two, 0) + from_partner(totals, one ^ two, 0))
    else:
        totals = lax.psum(total, ("ax", "az"))
    final, adjoint, sensitivity = call(
        third_far_kernel,
        [pltpu.SMEM] * 2 + [HBM] * 2 + [VMEM] * 12,
        stored[:2] + [(cells_, f32, HBM)],
        third_scratch + [VMEM(cells_, f32)],
        *place, *near, *inside, o, t_near,
        aliases={2: 0, 3: 1},
    )
    return final, adjoint, sensitivity, totals[0, : size_a * size_t // 4]


def solution(mesh):
    return jax.shard_map(
        shards,
        mesh=mesh,
        in_specs=(
            P(None, "ax", "az", None),
            P(None, "ax", "az", None),
            P("ax", "az", None),
            P("ax", "az", None),
            P("ax", "az", None),
        ),
        out_specs=(P(None, "ax", "az", None), P(None, "ax", "az", None), P("ax", "az", None), P()),
        check_vma=False,
    )
```

```python
import functools

import jax
import jax.numpy as jnp
import numpy as np
from jax import lax
from jax.experimental import pallas as pl
from jax.experimental.pallas import tpu as pltpu
from jax.sharding import PartitionSpec as P

VELOCITY = [
    (0, 0, 0),
    (1, 0, 0),
    (-1, 0, 0),
    (0, 1, 0),
    (0, -1, 0),
    (0, 0, 1),
    (0, 0, -1),
    (1, 1, 0),
    (-1, -1, 0),
    (1, -1, 0),
    (-1, 1, 0),
    (1, 0, 1),
    (-1, 0, -1),
    (1, 0, -1),
    (-1, 0, 1),
    (0, 1, 1),
    (0, -1, -1),
    (0, 1, -1),
    (0, -1, 1),
]
OPPOSITE = [0, 2, 1, 4, 3, 6, 5, 8, 7, 10, 9, 12, 11, 14, 13, 16, 15, 18, 17]
INLET_SPEED = (0.05, 0.05, 0.0)
W_AXIS = 1.0 / 18.0
W_EDGE = 1.0 / 36.0


def moving(axis, sign):
    return [q for q in range(19) if VELOCITY[q][axis] == sign]


LO, HI = 0, 1
POST, ADJ, FACTOR, FLAG, MOTION = 0, 1, 2, 3, 4


def face_fields(kinds, axis, side):
    sign = -1 if side == LO else 1
    fields = []
    for kind in kinds:
        if kind == FLAG:
            fields.append((FLAG, 0))
        elif kind == FACTOR and axis == 0:
            fields += [(MOTION, k) for k in range(4)]
        else:
            fields += [(kind, q) for q in moving(axis, -sign if kind == ADJ else sign)]
    return fields


class Layout:
    def __init__(self, kinds):
        self.ax = [face_fields(kinds, 0, side) for side in (LO, HI)]
        self.slot = [{key: i for i, key in enumerate(fields)} for fields in self.ax]
        self.fields = len(self.ax[LO])
        corner, rest = [], []
        for a, sign in ((1, 1), (0, -1)):
            for side in (LO, HI):
                for kind, q in face_fields(kinds, 1, side):
                    leaves = VELOCITY[q][0] == (-sign if kind == ADJ else sign)
                    key = (side, kind, q, a)
                    (corner if kind == FLAG or leaves else rest).append(key)
        self.corner_blocks = -(-len(corner) // 8)
        self.blocks = self.corner_blocks + -(-len(rest) // 8)
        self.place = {key: (i // 8, i % 8) for i, key in enumerate(corner)}
        self.place.update({key: (self.corner_blocks + i // 8, i % 8) for i, key in enumerate(rest)})


FIRST = Layout((POST, ADJ, FACTOR, FLAG))
SECOND = Layout((POST, ADJ))


def pairs_of(values):
    sums = [values[q] + values[q + 1] for q in range(1, 19, 2)]
    diffs = [values[q] - values[q + 1] for q in range(1, 19, 2)]
    return sums, diffs


def projections(vec):
    va, vt, vr = vec
    return [va, vt, vr, va + vt, va - vt, va + vr, va - vr, vt + vr, vt - vr]


def linearise(pops, porous, types, regions):
    sums, diffs = pairs_of(pops)
    s0, s1, s2, s3, s4, s5, s6, s7, s8 = sums
    d0, d1, d2, d3, d4, d5, d6, d7, d8 = diffs
    at, ar, tr = s3 + s4, s5 + s6, s7 + s8
    rho = pops[0] + ((s0 + s1) + (s2 + at)) + (ar + tr)
    ma = (d0 + (d3 + d4)) + (d5 + d6)
    mt = (d1 + (d3 - d4)) + (d7 + d8)
    mr = (d2 + (d5 - d6)) + (d7 - d8)
    inv = 1.0 / rho
    ua, ut, ur = ma * inv, mt * inv, mr * inv
    third = rho * (1.0 / 3.0)
    paa = (s0 + at + ar - third) - ma * ua
    ptt = (s1 + at + tr - third) - mt * ut
    prr = (s2 + ar + tr - third) - mr * ur
    pat = (s3 - s4) - ma * ut
    par = (s5 - s6) - ma * ur
    ptr = (s7 - s8) - mt * ur
    square = (paa * paa + ptt * ptt + prr * prr) + 2.0 * (pat * pat + par * par + ptr * ptr) + 0.0001
    inv_root = lax.rsqrt(square)
    shear = 1.5 * (square * inv_root) * inv
    shifted = shear + 0.01
    viscous = 0.02 * jnp.exp((0.7 - 1.0) * jnp.log(shifted))
    omega = 1.0 / (0.5 + 3.0 * viscous)
    relaxed = (types != 2) & (types != 3)
    kappa = jnp.where(regions > 0, porous, 0.0)
    return dict(
        rho=rho,
        inv=inv,
        u=(ua, ut, ur),
        p=(paa, ptt, prr, pat, par, ptr),
        inv_root=inv_root,
        shear=shear,
        shifted=shifted,
        viscous=viscous,
        omega=omega,
        relaxed=relaxed,
        kappa=kappa,
        keep=jnp.where(relaxed, 1.0 - omega, 0.0),
        design=jnp.where(relaxed & (regions > 0), 1.0, 0.0),
        inlet=types == 2,
        outlet=types == 3,
    )


def collide(pops, lin):
    rho, relaxed, inlet = lin["rho"], lin["relaxed"], lin["inlet"]
    ua, ut, ur = (jnp.where(inlet, speed, x) for x, speed in zip(lin["u"], INLET_SPEED))
    scale = jnp.where(relaxed, (lin["omega"] - lin["kappa"]) * rho, 1.0)
    rest = jnp.where(relaxed, lin["kappa"] * rho, 0.0)
    keep = lin["keep"]
    still = 1.0 - 1.5 * (ua * ua + ut * ut + ur * ur)
    post = [keep * pops[0] + (1.0 / 3.0) * (scale * still + rest)]
    for i, cu in enumerate(projections((ua, ut, ur))):
        weight = W_AXIS if i < 3 else W_EDGE
        even = weight * (scale * (still + 4.5 * cu * cu) + rest)
        odd = (3.0 * weight) * (scale * cu)
        post.append(keep * pops[1 + 2 * i] + (even + odd))
        post.append(keep * pops[2 + 2 * i] + (even - odd))
    return post


def pull_back(back, pops, lin):
    sums, diffs = pairs_of(back)
    s0, s1, s2, s3, s4, s5, s6, s7, s8 = sums
    d0, d1, d2, d3, d4, d5, d6, d7, d8 = diffs
    at, ar, tr = s3 + s4, s5 + s6, s7 + s8
    b0 = (1.0 / 3.0) * back[0] + W_AXIS * (s0 + s1 + s2) + W_EDGE * (at + ar + tr)
    ba = W_AXIS * d0 + W_EDGE * ((d3 + d4) + (d5 + d6))
    bt = W_AXIS * d1 + W_EDGE * ((d3 - d4) + (d7 + d8))
    br = W_AXIS * d2 + W_EDGE * ((d5 - d6) + (d7 - d8))
    baa = W_AXIS * s0 + W_EDGE * (at + ar)
    btt = W_AXIS * s1 + W_EDGE * (at + tr)
    brr = W_AXIS * s2 + W_EDGE * (ar + tr)
    bat, bar, btr = W_EDGE * (s3 - s4), W_EDGE * (s5 - s6), W_EDGE * (s7 - s8)
    along = back[0] * pops[0]
    for q in range(1, 19):
        along = along + back[q] * pops[q]
    rho, inv = lin["rho"], lin["inv"]
    ua, ut, ur = lin["u"]
    qa = baa * ua + bat * ut + bar * ur
    qt = bat * ua + btt * ut + btr * ur
    qr = bar * ua + btr * ut + brr * ur
    uu = ua * ua + ut * ut + ur * ur
    slope = 3.0 * (ua * ba + ut * bt + ur * br) + 4.5 * (ua * qa + ut * qt + ur * qr) - 1.5 * (uu * b0)
    full = b0 + slope
    sens = -(lin["design"] * (rho * slope))
    relaxed, omega = lin["relaxed"], lin["omega"]
    shear_bar = (rho * full - along) * (omega * omega) * (0.9 * lin["viscous"]) / lin["shifted"]
    shear_bar = jnp.where(relaxed, shear_bar, 0.0)
    z = shear_bar * (1.5 * inv) * lin["inv_root"]
    maa, mtt, mrr, mat, mar, mtr = (z * x for x in lin["p"])
    scale = jnp.where(relaxed, omega - lin["kappa"], jnp.where(lin["outlet"], inv, 0.0))
    la = maa * ua + mat * ut + mar * ur
    lt = mat * ua + mtt * ut + mtr * ur
    lr = mar * ua + mtr * ut + mrr * ur
    va = scale * (3.0 * (ba - b0 * ua) + 9.0 * qa) - 2.0 * la
    vt = scale * (3.0 * (bt - b0 * ut) + 9.0 * qt) - 2.0 * lt
    vr = scale * (3.0 * (br - b0 * ur) + 9.0 * qr) - 2.0 * lr
    total = jnp.where(relaxed, lin["kappa"] * b0 + scale * full, 0.0)
    total = total - shear_bar * lin["shear"] * inv - (1.0 / 3.0) * (maa + mtt + mrr)
    total = total - ((la + va) * ua + (lt + vt) * ut + (lr + vr) * ur)
    keep = lin["keep"]
    taa, ttt, trr = total + maa, total + mtt, total + mrr
    sat, sar, str_ = taa + mtt, taa + mrr, ttt + mrr
    mat2, mar2, mtr2 = 2.0 * mat, 2.0 * mar, 2.0 * mtr
    evens = [taa, ttt, trr, sat + mat2, sat - mat2, sar + mar2, sar - mar2, str_ + mtr2, str_ - mtr2]
    result = [keep * back[0] + total]
    for i, odd in enumerate(projections((va, vt, vr))):
        result.append(keep * back[1 + 2 * i] + (evens[i] + odd))
        result.append(keep * back[2 + 2 * i] + (evens[i] - odd))
    return result, sens


def face_rows(slot):
    return slice(16 * slot, 16 * slot + 16)


def by_parity(parity_ref, body):
    for parity in (0, 1):
        pl.when(parity_ref[0] == parity)(functools.partial(body, parity))


def near_rows(parity, rows_a):
    return (range(1, rows_a), 0) if parity == 0 else (range(rows_a - 1), rows_a - 1)


class Fields:
    def __init__(self, layout, own, parity, e=None, o=None, real=None, t=None, ed=None, od=None):
        self.layout, self.own, self.t = layout, own, t
        self.rows_a = own[POST].shape[1]
        sides = [(o, od, real), (e, ed, None)]
        self.sides = sides if parity == 0 else sides[::-1]

    def row(self, kind, q, a):
        if 0 <= a < self.rows_a:
            return self.own[FLAG][a] if kind == FLAG else self.own[kind][q, a]
        if kind == FACTOR:
            weight, *velocity = (self.row(MOTION, k, a) for k in range(4))
            return porosity_factor(q, weight, velocity)
        message, _, real = self.sides[a >= 0]
        slot = self.layout.slot[HI if a < 0 else LO][(kind, q)]
        return self.masked(kind, message[face_rows(slot), :], real)

    def masked(self, kind, value, real):
        if real is None or kind not in (ADJ, FLAG):
            return value
        return jnp.where(real == 1, value, 0.0)

    def row_label(self, a):
        row = 16 * self.layout.slot[HI if a < 0 else LO][(MOTION, 0)]
        return self.sides[a >= 0][0][row : row + 1, 0:1]

    def edge_label(self, side, a):
        sa = 1 if a < 0 else -1 if a >= self.rows_a else 0
        q = VELOCITY.index((sa, -1 if side == LO else 1, 0))
        return self.edge(side, FACTOR, q, a)[:, 0:1]

    def message(self, key, a):
        block, i = self.layout.place[key]
        if 0 <= a < self.rows_a:
            return self.t[block, i : i + 1, :]
        axial, corners, real = self.sides[a >= 0]
        if corners is None:
            row = 16 * self.layout.fields + 8 * block + i
            return self.masked(key[1], axial[row : row + 1, :], real)
        return self.masked(key[1], corners[i : i + 1, :], real)

    def edge(self, side, kind, q, a):
        row = self.rows_a - 1 if a < 0 else 0 if a >= self.rows_a else a
        return self.message((side, kind, q, row), a)

    def moved(self, kind, q, a, shift):
        sa, st, sr = shift
        value = self.row(kind, q, a + sa)
        rows_t, rows_r = value.shape
        if st:
            value = pltpu.roll(value, (-st) % rows_t, 0)
            beyond = self.edge(LO if st > 0 else HI, kind, q, a + sa)
            at_edge = lax.broadcasted_iota(jnp.int32, value.shape, 0) == (rows_t - 1 if st > 0 else 0)
            value = jnp.where(at_edge, beyond, value)
        if sr:
            value = pltpu.roll(value, (-sr) % rows_r, 1)
        return value


def cells(own, kind, q, a):
    return own[FLAG].at[a] if kind == FLAG else own[kind].at[q, a]


def stream_row(fields, a, around, result):
    post = fields.own[POST]
    result[0, a] = post[0, a]
    for q in range(1, 19):
        moved = fields.moved(POST, q, a, tuple(-c for c in VELOCITY[q]))
        result[q, a] = jnp.where(around[q - 1, a] > 0, moved, post[OPPOSITE[q], a])


def stream_adjoint_row(fields, a, centre, around, result):
    adj = fields.own[ADJ]
    result[0, a] = adj[0, a]
    for q in range(1, 19):
        opp = OPPOSITE[q]
        ahead = centre * fields.moved(ADJ, opp, a, tuple(-c for c in VELOCITY[q]))
        result[opp, a] = ahead + (1.0 - around[q - 1, a]) * adj[q, a]


def labelled(value, label):
    lanes = lax.broadcasted_iota(jnp.int32, value.shape, 1)
    return jnp.where(lanes == 0, label, value)


def pack_azimuthal(layout, own, rows, t_ref, label=None):
    rows_t = own[POST].shape[2]
    for (side, kind, q, a), (block, i) in layout.place.items():
        if a in rows:
            t = 0 if side == LO else rows_t - 1
            row = cells(own, kind, q, a)[t : t + 1, :]
            t_ref[block, i : i + 1, :] = labelled(row, label) if kind == FACTOR else row


def pack_face(layout, own, side, message, label=None):
    a = 0 if side == LO else own[POST].shape[1] - 1
    for slot, (kind, q) in enumerate(layout.ax[side]):
        value = cells(own, kind, q, a)[...]
        if (kind, q) == (MOTION, 0):
            value = labelled(value, label)
        message[face_rows(slot), :] = value


def near_side(parity):
    return (HI, LO) if parity == 0 else (LO, HI)


def chunks(rows_a, shape, body):
    counts = (len(rows_a), shape[1] // 8, shape[2] // 128)

    def step(i, carry):
        a = rows_a[0] + i // (counts[1] * counts[2])
        t = pl.multiple_of((i // counts[2]) % counts[1] * 8, 8)
        r = pl.multiple_of(i % counts[2] * 128, 128)
        body((a, pl.ds(t, 8), pl.ds(r, 128)))
        return carry

    lax.fori_loop(0, counts[0] * counts[1] * counts[2], step, 0, unroll=4)


def load(ref, where):
    return [ref[(q,) + where] for q in range(19)]


def store(ref, where, values):
    for q in range(19):
        ref[(q,) + where] = values[q]


def label_of(regions):
    label = jnp.max(jnp.max(regions[...], axis=0), axis=(0, 1), keepdims=True)
    return label.astype(jnp.float32)


def porosity_factor(q, weight, velocity):
    ua, ut, ur = velocity
    pair = (q - 1) // 2
    cu = projections(velocity)[pair]
    scaled = (W_AXIS if pair < 3 else W_EDGE) * weight
    still = -1.5 * (ua * ua + ut * ut + ur * ur)
    return scaled * (still + 4.5 * cu * cu + (3.0 * cu if q % 2 else -3.0 * cu))


def factor_weight(lin):
    return -(lin["design"] * lin["rho"])


def porosity_factors(lin):
    ua, ut, ur = lin["u"]
    weight = factor_weight(lin)
    still = -1.5 * (ua * ua + ut * ut + ur * ur)
    result = [(1.0 / 3.0) * weight * still]
    for i, cu in enumerate(projections((ua, ut, ur))):
        scaled = (W_AXIS if i < 3 else W_EDGE) * weight
        even, odd = scaled * (still + 4.5 * cu * cu), 3.0 * scaled * cu
        result += [even + odd, even - odd]
    return result


def first_kernel(
    parity_ref, pops_hbm, seed_hbm, porous_hbm, types_hbm, regions_hbm,
    post, factors, e_out, o_out, t_out, ed_out, od_out, flags,
    pops, seed, porous, types, regions, motion, sems,
):
    rows_a, _, rows_r = porous.shape
    pairs = [(types_hbm, types), (regions_hbm, regions), (porous_hbm, porous)]
    pairs += [(pops_hbm.at[:, a], pops.at[:, a]) for a in range(rows_a)] + [(seed_hbm, seed)]
    loads = [pltpu.make_async_copy(*pair, sems.at[i]) for i, pair in enumerate(pairs)]
    for copy in loads:
        copy.start()
    for copy in loads[:3]:
        copy.wait()
    def body(where):
        values = load(pops, where)
        lin = linearise(values, porous[where], types[where], regions[where])
        store(post, where, collide(values, lin))
        store(factors, where, porosity_factors(lin))
        for k, value in enumerate([factor_weight(lin), *lin["u"]]):
            motion[(k,) + where] = value

    for a in range(rows_a):
        loads[3 + a].wait()
        chunks([a], porous.shape, body)
    flags[...] = jnp.where(types[...] != 1, 1.0, 0.0)
    label = label_of(regions)
    loads[-1].wait()
    own = {POST: post, ADJ: seed, FACTOR: factors, MOTION: motion, FLAG: flags}
    pack_azimuthal(FIRST, own, range(rows_a), t_out, label)

    def run(parity):
        near, far = near_side(parity)
        pack_face(FIRST, own, near, e_out, label)
        pack_face(FIRST, own, far, o_out, label)
        ed_out[...] = t_out[parity]
        od_out[...] = t_out[1 - parity]

    by_parity(parity_ref, run)


def second_rows(fields, rows, cell_refs, results, scratch):
    porous, types, regions = cell_refs
    post_next, adj, sens, around = results
    state, back = scratch
    for a in rows:
        for q in range(1, 19):
            around[q - 1, a] = fields.moved(FLAG, 0, a, tuple(-c for c in VELOCITY[q]))
        stream_row(fields, a, around, state)
        stream_adjoint_row(fields, a, fields.own[FLAG][a], around, back)

    def body(where):
        values = load(state, where)
        lin = linearise(values, porous[where], types[where], regions[where])
        store(post_next, where, collide(values, lin))
        result, partial_sens = pull_back(load(back, where), values, lin)
        store(adj, where, result)
        sens[where] = partial_sens

    chunks(rows, porous.shape, body)


def second_near_kernel(
    parity_ref, post, seed, factors, flags, porous, types, regions, e, t, ed,
    post_next, adj, sens, around, e_out, t_out, partial, state, back, parts,
):
    def run(parity):
        own = {POST: post, ADJ: seed, FACTOR: factors, FLAG: flags}
        fields = Fields(FIRST, own, parity, e=e, t=t, ed=ed)
        rows, _ = near_rows(parity, porous.shape[0])
        results = (post_next, adj, sens, around)
        second_rows(fields, rows, (porous, types, regions), results, (state, back))
        own = {POST: post_next, ADJ: adj}
        pack_face(SECOND, own, near_side(parity)[0], e_out)
        pack_azimuthal(SECOND, own, rows, t_out)
        partial[...] = region_sums(fields, rows, adj, sens, around, regions, parts)

    by_parity(parity_ref, run)


def second_far_kernel(
    parity_ref, real_ref, post_near, adj_near, sens_near, around_near, t_near, partial_near,
    post, seed, factors, flags, porous, types, regions, o, t, od,
    post_next, adj, sens, around, t_out, o_out, partial, state, back, parts,
):
    def run(parity):
        own = {POST: post, ADJ: seed, FACTOR: factors, FLAG: flags}
        fields = Fields(FIRST, own, parity, o=o, real=real_ref[0], t=t, od=od)
        _, row = near_rows(parity, porous.shape[0])
        results = (post_next, adj, sens, around)
        second_rows(fields, [row], (porous, types, regions), results, (state, back))
        own = {POST: post_next, ADJ: adj}
        pack_face(SECOND, own, near_side(parity)[1], o_out)
        pack_azimuthal(SECOND, own, [row], t_out)
        sums = region_sums(fields, [row], adj, sens, around, regions, parts)
        partial[...] = partial_near[...] + sums

    by_parity(parity_ref, run)


def region_sums(fields, rows, adj, sens, around, regions, parts):
    factors = fields.own[FACTOR]
    rows_a, rows_t, rows_r = sens.shape
    sums = {}
    for a in rows:
        sums.setdefault((0, 0), []).extend([sens[a], factors[0, a] * adj[0, a]])
        for q in range(1, 19):
            behind = tuple(-c for c in VELOCITY[q])
            open_, value = around[q - 1, a], adj[q, a]
            sums[(0, 0)].append(jnp.where(open_ > 0, 0.0, factors[OPPOSITE[q], a]) * value)
            term = jnp.where(open_ > 0, fields.moved(FACTOR, q, a, behind), 0.0) * value
            from_a = a + behind[0]
            beyond = -1 if from_a < 0 else 1 if from_a >= rows_a else 0
            sums.setdefault((beyond, behind[1]), []).append(term)
    at_t = lax.broadcasted_iota(jnp.int32, (rows_t, rows_r), 0)
    lines = []
    for beyond in sorted({key[0] for key in sums}):
        low, centre, high = (functools.reduce(jnp.add, sums[(beyond, st)]) for st in (-1, 0, 1))
        inner = centre + jnp.where(at_t == 0, 0.0, low) + jnp.where(at_t == rows_t - 1, 0.0, high)
        a = {-1: -1, 0: 0, 1: rows_a}[beyond]
        label = fields.row_label(a) if beyond else label_of(regions)
        lines.append((jnp.sum(inner, axis=0, keepdims=True), label))
        a = a if beyond else rows[0]
        lines.append((high[rows_t - 1 : rows_t], fields.edge_label(LO, a)))
        lines.append((low[0:1], fields.edge_label(HI, a)))
    parts[...] = jnp.zeros_like(parts)
    for i, (value, label) in enumerate(lines):
        parts[0, i : i + 1, :] = value
        parts[1, i : i + 1, :] = jnp.broadcast_to(label, (1, rows_r))
    lanes = lax.broadcasted_iota(jnp.int32, parts.shape[1:], 1) + 1
    total = jnp.sum(parts[0], axis=1, keepdims=True)
    chosen = jnp.where(lanes == parts[1].astype(jnp.int32), total, 0.0)
    return jnp.sum(chosen, axis=0, keepdims=True)


def corner_kernel(e, o, t, total, e_out, o_out):
    row = 16 * SECOND.fields
    for out in (e_out, o_out):
        out[row : row + 8, :] = t[0]
    e_out[row + 8 : row + 16, :] = jnp.broadcast_to(total[...], (8, e_out.shape[1]))


def third_rows(fields, rows, cell_refs, own_refs, hbm, sens, scratch, sems):
    porous, types, regions = cell_refs
    around, flags, pops, sens_one = own_refs
    final, result, back = scratch
    stores = []

    def send(source, target, a):
        stores.append(pltpu.make_async_copy(source.at[:, a], target.at[:, a], sems.at[len(stores)]))
        stores[-1].start()

    def body(where):
        values = load(pops, where)
        lin = linearise(values, porous[where], types[where], regions[where])
        adjoint, partial_sens = pull_back(load(back, where), values, lin)
        store(result, where, adjoint)
        sens[where] = partial_sens + sens_one[where]

    for a in rows:
        stream_row(fields, a, around, final)
        send(final, hbm[0], a)
        stream_adjoint_row(fields, a, flags[a], around, back)
        chunks([a], porous.shape, body)
        send(result, hbm[1], a)
    return stores


def third_near_kernel(
    parity_ref, post, adj, flags, around, pops, porous, types, regions, sens_one, e, t,
    final_hbm, result_hbm, sens, final, result, back, sems,
):
    def run(parity):
        fields = Fields(SECOND, {POST: post, ADJ: adj}, parity, e=e, t=t)
        rows, _ = near_rows(parity, porous.shape[0])
        stores = third_rows(
            fields, rows, (porous, types, regions), (around, flags, pops, sens_one),
            (final_hbm, result_hbm), sens, (final, result, back), sems,
        )
        for copy in stores:
            copy.wait()

    by_parity(parity_ref, run)


def third_far_kernel(
    parity_ref, real_ref, final_near, result_near, sens_near,
    post, adj, flags, around, pops, porous, types, regions, sens_one, o, t,
    final_hbm, result_hbm, sens_hbm, final, result, back, sems, sens,
):
    def run(parity):
        fields = Fields(SECOND, {POST: post, ADJ: adj}, parity, o=o, real=real_ref[0], t=t)
        rows, row = near_rows(parity, porous.shape[0])
        for a in rows:
            sens[a] = sens_near[a]
        stores = third_rows(
            fields, [row], (porous, types, regions), (around, flags, pops, sens_one),
            (final_hbm, result_hbm), sens, (final, result, back), sems,
        )
        stores.append(pltpu.make_async_copy(sens, sens_hbm, sems.at[len(stores)]))
        stores[-1].start()
        for copy in stores:
            copy.wait()

    by_parity(parity_ref, run)


VMEM, HBM = pltpu.VMEM, pltpu.HBM


def call(body, in_spaces, outs, scratch, *arrays, aliases=None, cost=None):
    return pl.pallas_call(
        body,
        out_shape=[jax.ShapeDtypeStruct(shape, dtype) for shape, dtype, _ in outs],
        in_specs=[pl.BlockSpec(memory_space=space) for space in in_spaces],
        out_specs=[pl.BlockSpec(memory_space=space) for _, _, space in outs],
        scratch_shapes=scratch,
        input_output_aliases=aliases or {},
        cost_estimate=cost,
        compiler_params=pltpu.CompilerParams(vmem_limit_bytes=16 * 1024 * 1024),
    )(*arrays)


def axial_pairs(flip, shift_t=0):
    size_a, size_t = lax.axis_size("ax"), lax.axis_size("az")
    pairs = []
    for a in range(size_a):
        partner = ((a + flip) ^ 1) - flip
        for t in range(size_t):
            if 0 <= partner < size_a:
                pairs.append((a * size_t + t, partner * size_t + (t + shift_t) % size_t))
            elif shift_t:
                pairs.append((a * size_t + t, a * size_t + (t + shift_t) % size_t))
            elif size_t % 2 == 0:
                pairs.append((a * size_t + t, a * size_t + (t ^ 1)))
    return pairs


def from_both_sectors(message, high_rows, send):
    if lax.axis_size("az") == 2:
        return send(message, 1)
    return jnp.where(jnp.asarray(high_rows), send(message, 1), send(message, -1))


def high_rows(layout):
    rows = np.zeros((layout.blocks, 8, 1), bool)
    for key, (block, i) in layout.place.items():
        rows[block, i] = key[0] == HI
    return rows


def send_azimuthal(layout, message):
    size = lax.axis_size("az")

    def send(x, shift):
        return lax.ppermute(x, "az", [(i, (i + shift) % size) for i in range(size)])

    return from_both_sectors(message, high_rows(layout), send)


def send_axial(message, flip):
    return lax.ppermute(message, ("ax", "az"), axial_pairs(flip))


def send_diagonal(message, flip):
    def send(x, shift):
        return lax.ppermute(x, ("ax", "az"), axial_pairs(flip, shift))

    return from_both_sectors(message, high_rows(FIRST)[0], send)


def from_partner(x, flip_a, flip_t):
    size_a, size_t = lax.axis_size("ax"), lax.axis_size("az")
    pairs = [
        (a * size_t + t, (a ^ flip_a) * size_t + (t ^ flip_t))
        for a in range(size_a)
        for t in range(size_t)
    ]
    return lax.ppermute(x, ("ax", "az"), pairs)


def shards(initial, adjoint_seed, porosity, cell_type, region):
    cells_ = porosity.shape
    pops = (19,) + cells_
    wide = cells_[2]
    f32, i32 = jnp.float32, jnp.int32
    size_a, size_t = lax.axis_size("ax"), lax.axis_size("az")
    index = lax.axis_index("ax")
    real = (index != 0) & (index != size_a - 1)
    place = ((index % 2).astype(i32).reshape(1), real.astype(i32).reshape(1))

    def axial(layout, more):
        return ((16 * layout.fields + more, wide), f32, VMEM)

    def azimuthal(layout):
        return [((layout.blocks, 8, wide), f32, VMEM)]

    inputs = (initial, adjoint_seed, porosity, cell_type, region)
    post, factors, e, o, t, ed, od, flags = call(
        first_kernel,
        [pltpu.SMEM] + [HBM] * 5,
        [(pops, f32, VMEM), (pops, f32, VMEM)] + [axial(FIRST, 0), axial(FIRST, 8)] + azimuthal(FIRST)
        + [((8, wide), f32, VMEM)] * 2 + [(cells_, f32, VMEM)],
        [VMEM(x.shape, x.dtype) for x in inputs]
        + [VMEM((4,) + cells_, f32), pltpu.SemaphoreType.DMA((4 + cells_[0],))],
        place[0],
        *(pltpu.with_memory_space_constraint(x, HBM) for x in inputs),
    )
    e, o = send_axial(e, 0), send_axial(o, 1)
    t_near = send_azimuthal(FIRST, t)
    ed, od = send_diagonal(ed, 0), send_diagonal(od, 1)
    layers = [(pops, f32, VMEM), (pops, f32, VMEM), (cells_, f32, VMEM), ((18,) + cells_, f32, VMEM)]
    inside = (post, adjoint_seed, factors, flags, porosity, cell_type, region)
    row = [((1, wide), f32, VMEM)]
    scratch = [VMEM(pops, f32), VMEM(pops, f32), VMEM((2, 8, wide), f32)]
    *near, e, t, total = call(
        second_near_kernel,
        [pltpu.SMEM] + [VMEM] * 10,
        layers + [axial(SECOND, 16)] + azimuthal(SECOND) + row,
        scratch,
        place[0], *inside, e, t_near, ed,
    )
    post, adj, sens_one, around, t, o, total = call(
        second_far_kernel,
        [pltpu.SMEM] * 2 + [VMEM] * 16,
        layers + azimuthal(SECOND) + [axial(SECOND, 8)] + row,
        scratch,
        *place, *near, t, total, *inside, o, t_near, od,
        aliases={2: 0, 3: 1, 4: 2, 5: 3, 6: 4},
    )
    t_near = send_azimuthal(SECOND, t)
    halving = size_a >= 4 and not (size_a & (size_a - 1) or size_t & (size_t - 1))
    flips, last = [(1, 1 << k) for k in range(size_t.bit_length() - 1)], []
    if halving:
        total = total + from_partner(total, size_a // 2 | 1, 0)
        left = [(1 << k) | 1 for k in range(size_a.bit_length() - 3, 0, -1)]
        last = left[-2:] if len(left) > 1 else []
        flips += [(flip, 0) for flip in left[: len(left) - len(last)]]
    e, o = call(
        corner_kernel,
        [VMEM] * 4,
        [axial(SECOND, 16), axial(SECOND, 8)],
        [],
        e, o, t_near, total,
        aliases={0: 0, 1: 1},
    )
    e, o = send_axial(e, 0), send_axial(o, 1)
    stored = [(pops, f32, HBM), (pops, f32, HBM), (cells_, f32, VMEM)]
    third_scratch = [VMEM(pops, f32)] * 3 + [pltpu.SemaphoreType.DMA((2 * cells_[0],))]
    inside = (post, adj, flags, around, initial, porosity, cell_type, region, sens_one)
    near = call(
        third_near_kernel,
        [pltpu.SMEM] + [VMEM] * 11,
        stored,
        third_scratch,
        place[0], *inside, e, t_near,
    )
    if halving:
        row = 16 * SECOND.fields + 8
        totals = total + e[row : row + 1]
        for flip in flips:
            totals = totals + from_partner(totals, *flip)
        if last:
            totals, _ = lax.optimization_barrier((totals, near[2]))
            two, one = last
            pair = totals + from_partner(totals, one, 0)
            totals = pair + (from_partner(totals, two, 0) + from_partner(totals, one ^ two, 0))
    else:
        totals = lax.psum(total, ("ax", "az"))
    final, adjoint, sensitivity = call(
        third_far_kernel,
        [pltpu.SMEM] * 2 + [HBM] * 2 + [VMEM] * 12,
        stored[:2] + [(cells_, f32, HBM)],
        third_scratch + [VMEM(cells_, f32)],
        *place, *near, *inside, o, t_near,
        aliases={2: 0, 3: 1},
    )
    return final, adjoint, sensitivity, totals[0, : size_a * size_t // 4]


def solution(mesh):
    return jax.shard_map(
        shards,
        mesh=mesh,
        in_specs=(
            P(None, "ax", "az", None),
            P(None, "ax", "az", None),
            P("ax", "az", None),
            P("ax", "az", None),
            P("ax", "az", None),
        ),
        out_specs=(P(None, "ax", "az", None), P(None, "ax", "az", None), P("ax", "az", None), P()),
        check_vma=False,
    )
```
